32 devices in a mesh: lon: 8 (over z, y), lat: 4 (over x, core).
Axes of the slice: x: 2, y: 2, z: 4, core: 2. Of those that a mesh axis runs over, the one named last changes fastest.
Arguments:
- spectrum: float32 [1296, 64, 512], P(None, 'lon', 'lat'), may hold values from -6 to 6
- sea_mask: int32 [64, 512], P('lon', 'lat'), may hold values 0 or 1
- transfer: bfloat16 [1296, 1296], replicated, may hold values from -0.15625 to 0.15625
- bulk_weight: float32 [5, 1296], replicated, may hold values from -0.15625 to 0.15625
- remap_cell: int32 [192, 1536, 4], P('lon', 'lat'), may hold values from 0 to 8703, as said below
- remap_weight: float32 [192, 1536, 4], P('lon', 'lat'), may hold values from 0.1 to 0.5
- ocean_u: float32 [8, 192, 1536], P(None, 'lon', 'lat'), may hold values from -6 to 6
- ocean_v: float32 [8, 192, 1536], P(None, 'lon', 'lat'), may hold values from -6 to 6
- ocean_mask: int32 [192, 1536], P('lon', 'lat'), may hold values 0 or 1
- coriolis: float32 [1536], P('lat'), may hold values from -1 to 1
Outputs:
- spectrum_out: float32 [1296, 64, 512], P(None, 'lon', 'lat')
- ocean_u_out: float32 [8, 192, 1536], P(None, 'lon', 'lat')
- ocean_v_out: float32 [8, 192, 1536], P(None, 'lon', 'lat')
The draws below stay inside these ranges and needn't reach their ends.
Inputs may be any that keep to these rules, and one draw needn't show every extreme that they name: `remap_cell`: for ocean cell (i, j) each entry c has c // 512 between 0 and 16, and its wave latitude c % 512 lies in the same block of 128 latitude cells as j // 3.
All inputs are finite; a program needn't handle non-finite values. No bound on the sum of `sea_mask` or of `ocean_mask` on one device may be relied on, other than what follows from the above.
Results may differ from the reference program's by a relative error of at most 0.0016.
Values sent between devices are 32-bit elements; how exact they have to be, the bound alone decides.
No kernel may reach another device: no remote copies, remote signals or barrier semaphores. Data moves between devices by JAX's collectives and lax.ppermute only.
A program may use at most 128 MiB of HBM per device.

```python
import jax
import jax.numpy as jnp
from jax import lax

NDIR = 36
NFREQ = 36
K = 1296
WX = 8
WY = 128
LEV = 8
TAPS = 4
NXW = 64
NYW = 512
OXT = 192
OYT = 1536


def draw_remap_cell(key, part):
    key_lon = jax.random.fold_in(key, 11)
    key_lat = jax.random.fold_in(key, 23)
    ocean_lat = jnp.arange(OYT, dtype=jnp.int32)[None, :, None]
    shift_lon = jax.random.randint(key_lon, (OXT, OYT, TAPS), 0, 2 * WX + 1, dtype=jnp.int32)
    shift_lat = jax.random.randint(key_lat, (OXT, OYT, TAPS), -2, 3, dtype=jnp.int32)
    block = ocean_lat // 3 // WY
    wave_lat = jnp.clip(ocean_lat // 3 + shift_lat, block * WY, block * WY + WY - 1)
    return (shift_lon * NYW + wave_lat).astype(jnp.int32)


def plant(values, key, smallest, largest):
    longest = values.shape.index(max(values.shape))
    spots = []
    for shift in (0, 1):
        where = [jax.random.randint(jax.random.fold_in(key, axis), (), 0, length) for axis, length in enumerate(values.shape)]
        where[longest] = (where[longest] + shift) % values.shape[longest]
        spots.append(tuple(where))
    return values.at[spots[0]].set(smallest).at[spots[1]].set(largest)


def steps_of(stream_key, shape, shards, low, high):
    level = 1.0
    for position, blocks in shards:
        steps = jax.random.uniform(jax.random.fold_in(jax.random.fold_in(stream_key, 6), position), (blocks,), jnp.float32, low / len(shards), high / len(shards))
        level = level * jnp.repeat(jnp.exp(steps), shape[position] // blocks).reshape((-1,) + (1,) * (len(shape) - 1 - position))
    return level


def noise(rng, extent, spread, limit, split=(), kind=jnp.bfloat16):
    drawn = spread * jax.random.normal(rng, extent, jnp.float32)
    if split:
        drawn = drawn * steps_of(rng, extent, split, -0.22, 0.18)
    return jnp.clip(drawn, -limit, limit).astype(kind)


def setup_inputs(seed: int = 0) -> dict:
    streams_of = jax.random.split(jax.random.key(seed), 11)
    spectrum = noise(streams_of[0], (K, NXW, NYW), 1.0, 6.0, ((1, 8), (2, 4)), jnp.float32)
    sea_mask = plant((jax.random.randint(streams_of[1], (NXW, NYW), 0, 4) < 3).astype(jnp.int32), jax.random.fold_in(streams_of[1], 1), 0, 1)
    transfer = noise(streams_of[2], (K, K), K ** -0.5, 0.15625)
    bulk_weight = noise(streams_of[3], (5, K), K ** -0.5, 0.15625, (), jnp.float32)
    remap_cell = draw_remap_cell(jax.random.fold_in(streams_of[10], 71), 0)
    remap_weight = jnp.clip(0.1 + 0.4 * jax.random.uniform(streams_of[5], (OXT, OYT, TAPS), jnp.float32) ** steps_of(streams_of[5], (OXT, OYT, TAPS), ((0, 8), (1, 4)), -0.2, 0.2), 0.1, 0.5)
    ocean_u = noise(streams_of[6], (LEV, OXT, OYT), 1.0, 6.0, ((1, 8), (2, 4)), jnp.float32)
    ocean_v = noise(streams_of[7], (LEV, OXT, OYT), 1.0, 6.0, ((1, 8), (2, 4)), jnp.float32)
    ocean_mask = plant((jax.random.randint(streams_of[8], (OXT, OYT), 0, 8) < 7).astype(jnp.int32), jax.random.fold_in(streams_of[8], 1), 0, 1)
    coriolis = jnp.clip(jax.random.uniform(streams_of[9], (OYT,), jnp.float32, -1.0, 1.0) * steps_of(streams_of[9], (OYT,), ((0, 4),), -0.4, 0.0), -1.0, 1.0)
    return dict(spectrum=spectrum, sea_mask=sea_mask, transfer=transfer, bulk_weight=bulk_weight, remap_cell=remap_cell, remap_weight=remap_weight, ocean_u=ocean_u, ocean_v=ocean_v, ocean_mask=ocean_mask, coriolis=coriolis)


def courant():
    index = jnp.arange(NDIR * NFREQ, dtype=jnp.int32)
    direction = (index // NFREQ).astype(jnp.float32)
    level = (index % NFREQ).astype(jnp.float32)
    theta = 2.0 * jnp.pi * (direction + 0.5) / NDIR
    speed = jnp.power(jnp.float32(1.1), -level)
    return (0.45 * speed * jnp.cos(theta))[:, None, None], (0.45 * speed * jnp.sin(theta))[:, None, None]


def advect(extended, east, north):
    centre = extended[:, 1:-1, 1:-1]
    result = (1.0 - jnp.abs(east) - jnp.abs(north)) * centre
    result = result + jnp.maximum(east, 0.0) * extended[:, :-2, 1:-1] + jnp.maximum(-east, 0.0) * extended[:, 2:, 1:-1]
    result = result + jnp.maximum(north, 0.0) * extended[:, 1:-1, :-2] + jnp.maximum(-north, 0.0) * extended[:, 1:-1, 2:]
    return result


def source(advected, transfer, maskf):
    flat = advected.reshape(advected.shape[0], -1).astype(jnp.bfloat16)
    added = jnp.dot(transfer, flat, preferred_element_type=jnp.float32).reshape(advected.shape)
    return maskf * (advected + 0.5 * added)


def ocean_update(padded, ocean_u, ocean_v, drift_u, drift_v, maskf, coriolis):
    levels = ocean_u.shape[0]

    def dxx(q):
        return 0.5 * (q[2:, 1:-1] - q[:-2, 1:-1])

    def dyy(q):
        return 0.5 * (q[1:-1, 2:] - q[1:-1, :-2])

    sxx = padded[2 * levels]
    sxy = padded[2 * levels + 1]
    syy = padded[2 * levels + 2]
    force_x = -(dxx(sxx) + dyy(sxy))
    force_y = -(dxx(sxy) + dyy(syy))

    def laplace(q):
        return q[:, 2:, 1:-1] + q[:, :-2, 1:-1] + q[:, 1:-1, 2:] + q[:, 1:-1, :-2] - 4.0 * q[:, 1:-1, 1:-1]

    decay = jnp.exp(-jnp.arange(levels, dtype=jnp.float32) / 3.0)[:, None, None]
    lap_u = laplace(padded[:levels])
    lap_v = laplace(padded[levels:2 * levels])
    fcor = coriolis[None, None, :]
    new_u = maskf * (ocean_u + 0.5 * fcor * (ocean_v + decay * drift_v) + 0.5 * decay * force_x + 0.1 * lap_u)
    new_v = maskf * (ocean_v - 0.5 * fcor * (ocean_u + decay * drift_u) + 0.5 * decay * force_y + 0.1 * lap_v)
    return new_u, new_v


def pad_grid(field, lon_dim, lat_dim):
    first = lax.slice_in_dim(field, field.shape[lon_dim] - 1, field.shape[lon_dim], axis=lon_dim)
    last = lax.slice_in_dim(field, 0, 1, axis=lon_dim)
    wrapped = jnp.concatenate([first, field, last], axis=lon_dim)
    widths = [(0, 0)] * field.ndim
    widths[lat_dim] = (1, 1)
    return jnp.pad(wrapped, widths)


def reference(spectrum, sea_mask, transfer, bulk_weight, remap_cell, remap_weight, ocean_u, ocean_v, ocean_mask, coriolis):
    east, north = courant()
    maskf = sea_mask.astype(jnp.float32)[None]
    state = spectrum * maskf
    for step in range(2):
        state = source(advect(pad_grid(state, 1, 2), east, north), transfer, maskf)
    flat = state.reshape(state.shape[0], -1)
    bulk = jnp.dot(bulk_weight, flat, precision=lax.Precision.HIGHEST, preferred_element_type=jnp.float32)
    ocean_lon = jnp.arange(OXT, dtype=jnp.int32)[:, None, None]
    wave_lon = (ocean_lon // 3 + remap_cell // NYW - WX + NXW) % NXW
    wave_lat = remap_cell % NYW
    cell = (wave_lon * NYW + wave_lat).astype(jnp.int32)
    taken = jnp.take(bulk, cell.reshape(-1), axis=1).reshape((5,) + remap_cell.shape)
    forcing = jnp.sum(taken * remap_weight[None], axis=-1)
    stacked = jnp.concatenate([ocean_u, ocean_v, forcing[:3]], axis=0)
    padded = pad_grid(stacked, 1, 2)
    new_u, new_v = ocean_update(padded, ocean_u, ocean_v, forcing[3], forcing[4], ocean_mask.astype(jnp.float32)[None], coriolis)
    return state, new_u, new_v
```

```python
import functools

import jax
import jax.numpy as jnp
import numpy as np
from jax import lax
from jax.experimental import pallas as pl
from jax.experimental.pallas import tpu as pltpu
from jax.sharding import PartitionSpec as P

NFREQ = 36
STEP = 16
LANES = 128
BULK = 5
F32 = jnp.float32
VMEM = pl.BlockSpec(memory_space=pltpu.VMEM)
ANY = pl.BlockSpec(memory_space=pl.ANY)
PARAMS = pltpu.CompilerParams(vmem_limit_bytes=40 << 20)


class Plan:
    def __init__(self, comps):
        dirs = comps // NFREQ
        k = np.arange(comps)
        theta = 2.0 * np.pi * ((k // NFREQ) + 0.5) / dirs
        speed = 1.1 ** (-(k % NFREQ).astype(np.float64))
        cx = 0.45 * speed * np.cos(theta)
        cy = 0.45 * speed * np.sin(theta)
        self.comps = comps
        self.coef = np.stack([1.0 - np.abs(cx) - np.abs(cy), np.abs(cx), np.abs(cy)], 1).astype(np.float32)
        self.flag = {"x": cx > 0, "y": cy > 0}
        self.seg = {}
        for axis, step in (("x", 8), ("y", STEP)):
            for sign in (True, False):
                self.seg[axis, sign] = self.runs(self.flag[axis] == sign, step)

    def runs(self, flag, step):
        out = []
        for n in np.flatnonzero(flag.reshape(-1, step).any(1)):
            if out and out[-1][1] == n * step:
                out[-1][1] = int(n + 1) * step
            else:
                out.append([int(n) * step, int(n + 1) * step])
        return [(a, b) for a, b in out]

    def rows(self, axis, sign):
        return sum(b - a for a, b in self.seg[axis, sign])

    def shift(self, axis, sign, first):
        used = np.flatnonzero(self.flag[axis][first : first + STEP] == sign) + first
        if not len(used):
            return None
        base = 0
        for a, b in self.seg[axis, sign]:
            if a <= used[0] < b:
                at = base + first - a
                assert used[-1] < b and 0 <= at <= self.rows(axis, sign) - STEP
                return base - a
            base += b - a
        raise ValueError("no segment")

    def regions(self):
        out = []
        for r in range(0, self.comps, STEP):
            sign = {}
            for axis in "xy":
                part = self.flag[axis][r : r + STEP]
                sign[axis] = 1 if part.all() else (0 if part.any() else -1)
            shifts = {(axis, s): self.shift(axis, s, r) for axis in "xy" for s in (True, False)}
            if out and sign["x"] and sign["y"] and out[-1][2:] == [sign["x"], sign["y"], shifts]:
                out[-1][1] = r + STEP
            else:
                out.append([r, r + STEP, sign["x"], sign["y"], shifts])
        return out


def for_range(count, body, unroll=1):
    if count == 1:
        body(0)
        return

    def step(n, carry):
        body(n)
        return carry

    lax.fori_loop(0, count, step, 0, unroll=unroll)


def chunk_rows(first, n):
    return pl.ds(pl.multiple_of(first + n * STEP, STEP), STEP)


def shifted_rows(first, n, shift):
    return pl.ds(pl.multiple_of(first + shift + n * STEP, 8), STEP)


def lanes_of(rows=STEP):
    return lax.broadcasted_iota(jnp.int32, (rows, LANES), 1)


def picked(flag, first):
    row = lax.broadcasted_iota(jnp.int32, (STEP, LANES), 0)
    part = flag[first : first + STEP]
    out, n = (None, 0)
    while n < STEP:
        if not part[n]:
            n += 1
            continue
        m = n
        while m < STEP and part[m]:
            m += 1
        here = (row >= n) & (row < m)
        out = here if out is None else out | here
        n = m
    return out


def upwind(plan, axis, sign, first, from_plus, from_minus):
    if sign > 0:
        return from_plus()
    if sign < 0:
        return from_minus()
    plus, minus = (from_plus(), from_minus())
    where = picked(plan.flag[axis], first)
    zero = jnp.zeros((STEP, LANES), F32)
    if plus is None and minus is None:
        return None
    return jnp.where(where, zero if plus is None else plus, zero if minus is None else minus)


def pack_lon_kernel(plan, spec, mask, u, v, east, west, sem):
    last_col, last_row, levels = (spec.shape[1] - 1, u.shape[1] - 1, u.shape[0])
    copies = []
    for out, sign, col in ((east, True, last_col), (west, False, 0)):
        at = 0
        for a, b in plan.seg["x", sign]:
            c = pltpu.make_async_copy(
                spec.at[pl.ds(a, b - a), col, 0, :], out.at[pl.ds(at, b - a), :], sem.at[len(copies)]
            )
            c.start()
            copies.append(c)
            at += b - a
    for out, row, sign in ((east, last_row, True), (west, 0, False)):
        at = plan.rows("x", sign)
        for field in (u, v):
            for m in range(u.shape[2] // LANES):
                out[at : at + levels, :] = field[:, row, m * LANES : (m + 1) * LANES]
                at += levels
    for c in copies:
        c.wait()
    for out, sign, col in ((east, True, last_col), (west, False, 0)):
        rows = plan.rows("x", sign)
        out[:rows, :] = out[:rows, :] * mask[col : col + 1, :].astype(F32)


def pack_lon(plan, spec4, mask, u, v):
    extra = 2 * u.shape[0] * u.shape[2] // LANES
    segments = sum(len(plan.seg["x", s]) for s in (True, False))
    return pl.pallas_call(
        functools.partial(pack_lon_kernel, plan),
        out_shape=[jax.ShapeDtypeStruct((plan.rows("x", s) + extra, LANES), F32) for s in (True, False)],
        in_specs=[pl.BlockSpec(memory_space=pltpu.HBM), VMEM, VMEM, VMEM],
        out_specs=[VMEM, VMEM],
        scratch_shapes=[pltpu.SemaphoreType.DMA((segments,))],
        compiler_params=PARAMS,
        name="pack_lon",
    )(spec4, mask, u, v)


def to_lane(acc, column, source, lane, lanes):
    return jnp.where(lanes == lane, pltpu.roll(column, (lane - source) % LANES, 1), acc)


def pack_lat_kernel(plan, spec, mask, u, v, north, south, cols, sem):
    width_x = spec.shape[1]
    copies = [pltpu.make_async_copy(spec.at[:, i, 0, :], cols.at[i], sem.at[i]) for i in range(width_x)]
    for c in copies:
        c.start()
    levels, ocean_x = u.shape[:2]
    last = u.shape[2] - LANES
    for out, source, sign, m in ((north, LANES - 1, True, last), (south, 0, False, 0)):
        at = plan.rows("y", sign)
        acc = jnp.zeros((ocean_x, LANES), F32)
        for f in range(2 * levels):
            field = (u, v)[f // levels]
            acc = to_lane(acc, field[f % levels, :, m : m + LANES], source, f, lanes_of(ocean_x))
        out[at : at + ocean_x, :] = acc
    for c in copies:
        c.wait()
    maskf = mask[...].astype(F32)
    for out, source, sign in ((north, LANES - 1, True), (south, 0, False)):
        (a, b), = plan.seg["y", sign]

        def body(n, a=a, out=out, source=source):
            rows = chunk_rows(a, n)
            acc = jnp.zeros((STEP, LANES), F32)
            for i in range(width_x):
                acc = to_lane(acc, cols[i, rows, :] * maskf[i : i + 1, :], source, i, lanes_of())
            out[chunk_rows(0, n), :] = acc

        for_range((b - a) // STEP, body)


def pack_lat(plan, spec4, mask, u, v):
    extra = u.shape[1]
    return pl.pallas_call(
        functools.partial(pack_lat_kernel, plan),
        out_shape=[jax.ShapeDtypeStruct((plan.rows("y", s) + extra, LANES), F32) for s in (True, False)],
        in_specs=[ANY, VMEM, VMEM, VMEM],
        out_specs=[VMEM, VMEM],
        scratch_shapes=[
            pltpu.VMEM((spec4.shape[1], plan.comps, LANES), F32),
            pltpu.SemaphoreType.DMA((spec4.shape[1],)),
        ],
        compiler_params=PARAMS,
        name="pack_lat",
    )(spec4, mask, u, v)


def advect_columns(plan, column, coefs, south, north, put):
    def run(first, last, xs, ys, shifts):
        def body(n):
            rows = chunk_rows(first, n)
            x = [column(i, rows) for i in range(put.width)]
            c = coefs[rows, :]
            keep, east, up = (jnp.broadcast_to(c[:, q : q + 1], (STEP, LANES)) for q in range(3))
            lanes = lanes_of()
            from_south = from_north = None
            if shifts["y", True] is not None:
                from_south = south[shifted_rows(first, n, shifts["y", True]), :]
            if shifts["y", False] is not None:
                from_north = north[shifted_rows(first, n, shifts["y", False]), :]
            for i in range(put.width):
                lat = upwind(
                    plan, "y", ys, first,
                    lambda: to_lane(pltpu.roll(x[i], 1, 1), from_south, i, 0, lanes),
                    lambda: to_lane(pltpu.roll(x[i], LANES - 1, 1), from_north, i, LANES - 1, lanes),
                )
                lon = upwind(
                    plan, "x", xs, first,
                    lambda: x[i - 1] if i else None,
                    lambda: x[i + 1] if i + 1 < put.width else None,
                )
                a = keep * x[i] + up * lat
                if lon is not None:
                    a = a + east * lon
                put(i, rows, a)

        for_range((last - first) // STEP, body)

    for region in plan.regions():
        run(*region)


def block_rows(comps):
    return max(b for b in range(STEP, 449, STEP) if comps % b == 0)


def source_blocks(transfer, moved, comps, body):
    block = block_rows(comps)

    def step(n):
        rows = pl.ds(pl.multiple_of(n * block, STEP), block)
        body(n, rows, jnp.dot(transfer[rows, :], moved[...], preferred_element_type=F32))

    for_range(comps // block, step)


def add_bulk(coefs, rows, first, state, total, slot):
    count = state.shape[0]
    for q in range(BULK):
        w = coefs[rows, 3 + q : 4 + q]
        part = (w * state).reshape(count // 8, 8, LANES).sum(0)
        total[q, slot] = total[q, slot] + part


def interior_kernel(plan, step, *refs):
    refs = list(refs)
    if step == 0:
        spec, south, north, transfer, coefs, mask = refs[:6]
        inner, edge, up, down = refs[6:10]
        cols, full, moved, sem = refs[10:]
        width = spec.shape[1]
        copies = [pltpu.make_async_copy(spec.at[:, i, 0, :], cols.at[i], sem.at[i]) for i in range(width)]
        for c in copies:
            c.start()
        for c in copies:
            c.wait()
    else:
        sides, middle, south, north, transfer, coefs, mask = refs[:7]
        out, edge, bulk = refs[7:10]
        inner, full, moved, total, sem = refs[10:]
        width = middle.shape[0] + 2
    maskf = mask[...].astype(F32)

    def column(i, rows):
        if step == 0:
            return cols[i, rows, :] * maskf[i : i + 1, :]
        if i in (0, width - 1):
            return sides[min(i, 1), rows, :]
        return middle[i - 1, rows, :]

    def put(i, rows, a):
        if i in (0, width - 1):
            edge[min(i, 1), rows, :] = a
        else:
            full[i - 1, rows, :] = a
            moved[rows, (i - 1) * LANES : i * LANES] = a.astype(jnp.bfloat16)

    put_ = Put(width, put)
    advect_columns(plan, column, coefs, south, north, put_)
    if step:
        total[...] = jnp.zeros_like(total)

    def done(n, rows, added):
        for i in range(1, width - 1):
            s = maskf[i : i + 1, :] * (full[i - 1, rows, :] + 0.5 * added[:, (i - 1) * LANES : i * LANES])
            inner[i - 1, rows, :] = s
            if step:
                add_bulk(coefs, rows, n, s, total, i - 1)

    source_blocks(transfer, moved, plan.comps, done)
    if step:
        copies = [pltpu.make_async_copy(inner.at[i - 1], out.at[:, i, 0, :], sem.at[i]) for i in range(1, width - 1)]
        for c in copies:
            c.start()
        for q in range(BULK):
            for i in range(1, width - 1):
                bulk[q, i : i + 1, :] = total[q, i - 1].sum(0, keepdims=True)
            bulk[q, 0:1, :] = jnp.zeros((1, LANES), F32)
            bulk[q, width - 1 : width, :] = jnp.zeros((1, LANES), F32)
        for c in copies:
            c.wait()
    else:
        for out_ref, source, sign in ((up, LANES - 1, True), (down, 0, False)):
            (a, b), = plan.seg["y", sign]

            def body(n, a=a, out_ref=out_ref, source=source):
                rows = chunk_rows(a, n)
                acc = jnp.zeros((STEP, LANES), F32)
                for i in range(1, width - 1):
                    acc = to_lane(acc, inner[i - 1, rows, :], source, i, lanes_of())
                out_ref[chunk_rows(0, n), :] = acc

            for_range((b - a) // STEP, body)


class Put:
    def __init__(self, width, put):
        self.width, self.put = (width, put)

    def __call__(self, *args):
        self.put(*args)


def interior(plan, step, state, south, north, transfer, coefs, mask):
    comps, width = (plan.comps, mask.shape[0])
    middle = (width - 2, comps, LANES)
    edge = jax.ShapeDtypeStruct((2, comps, LANES), F32)
    full = [pltpu.VMEM(middle, F32), pltpu.VMEM((comps, (width - 2) * LANES), jnp.bfloat16)]
    sems = pltpu.SemaphoreType.DMA((width,))
    if step == 0:
        outs = [jax.ShapeDtypeStruct(middle, F32), edge]
        outs += [jax.ShapeDtypeStruct((plan.rows("y", s), LANES), F32) for s in (True, False)]
        in_specs = [ANY] + [VMEM] * 5
        out_specs = [VMEM] * 4
        scratch = [pltpu.VMEM((width, comps, LANES), F32)] + full + [sems]
    else:
        outs = [
            jax.ShapeDtypeStruct((comps, width, 1, LANES), F32),
            edge,
            jax.ShapeDtypeStruct((BULK, width, LANES), F32),
        ]
        in_specs = [VMEM] * 7
        out_specs = [ANY, VMEM, VMEM]
        scratch = [pltpu.VMEM(middle, F32)] + full + [pltpu.VMEM((BULK, width - 2, 8, LANES), F32), sems]
    return pl.pallas_call(
        functools.partial(interior_kernel, plan, step),
        out_shape=outs,
        in_specs=in_specs,
        out_specs=out_specs,
        scratch_shapes=scratch,
        compiler_params=PARAMS,
        cost_estimate=pl.CostEstimate(
            flops=2 * comps * comps * (width - 2) * LANES, bytes_accessed=20 << 20, transcendentals=0
        ),
        name="interior",
    )(*state, south, north, transfer, coefs, mask)


def edges_kernel(plan, step, *refs):
    refs = list(refs)
    part, from_west, from_east, transfer, coefs, mask = refs[:6]
    if step == 0:
        up_in, down_in = refs[6:8]
        state, east, west, up, down = refs[8:13]
        full, moved = refs[13:]
    else:
        bulk_in = refs[6]
        state, bulk = refs[7:9]
        full, moved, total = refs[9:]
    width = mask.shape[0]
    maskf = jnp.concatenate([mask[0:1, :], mask[width - 1 : width, :]], axis=0).astype(F32)

    def run(first, last, xs, ys, shifts):
        def body(n):
            rows = chunk_rows(first, n)
            speed = jnp.broadcast_to(coefs[rows, 1:2], (STEP, LANES))
            for side, sign, buffer in ((0, True, from_west), (1, False, from_east)):
                a = part[side, rows, :]
                shift = shifts["x", sign]
                if shift is not None:
                    halo = buffer[shifted_rows(first, n, shift), :]
                    if xs == 0:
                        halo = jnp.where(picked(plan.flag["x"] == sign, first), halo, 0.0)
                    a = a + speed * halo
                full[side, rows, :] = a
                moved[rows, side * LANES : (side + 1) * LANES] = a.astype(jnp.bfloat16)

        for_range((last - first) // STEP, body)

    for region in plan.regions():
        run(*region)
    if step:
        total[...] = jnp.zeros_like(total)

    def done(n, rows, added):
        for side in range(2):
            s = maskf[side : side + 1, :] * (full[side, rows, :] + 0.5 * added[:, side * LANES : (side + 1) * LANES])
            state[side, rows, :] = s
            if step:
                add_bulk(coefs, rows, n, s, total, side)

    source_blocks(transfer, moved, plan.comps, done)
    if step:
        for q in range(BULK):
            bulk[q] = bulk_in[q]
            bulk[q, 0:1, :] = total[q, 0].sum(0, keepdims=True)
            bulk[q, width - 1 : width, :] = total[q, 1].sum(0, keepdims=True)
        return
    for out, side, sign in ((east, 1, True), (west, 0, False)):
        at = 0
        for a, b in plan.seg["x", sign]:
            out[at : at + b - a, :] = state[side, a:b, :]
            at += b - a
    for out, given, source, sign in ((up, up_in, LANES - 1, True), (down, down_in, 0, False)):
        (a, b), = plan.seg["y", sign]

        def body(n, a=a, out=out, given=given, source=source):
            rows = chunk_rows(a, n)
            acc = given[chunk_rows(0, n), :]
            for side, lane in ((0, 0), (1, width - 1)):
                acc = to_lane(acc, state[side, rows, :], source, lane, lanes_of())
            out[chunk_rows(0, n), :] = acc

        for_range((b - a) // STEP, body)


def edges(plan, step, part, from_west, from_east, transfer, coefs, mask, *more):
    comps, width = (plan.comps, mask.shape[0])
    outs = [jax.ShapeDtypeStruct((2, comps, LANES), F32)]
    scratch = [pltpu.VMEM((2, comps, LANES), F32), pltpu.VMEM((comps, 2 * LANES), jnp.bfloat16)]
    if step == 0:
        for axis in "xy":
            outs += [jax.ShapeDtypeStruct((plan.rows(axis, s), LANES), F32) for s in (True, False)]
    else:
        outs += [jax.ShapeDtypeStruct((BULK, width, LANES), F32)]
        scratch += [pltpu.VMEM((BULK, 2, 8, LANES), F32)]
    return pl.pallas_call(
        functools.partial(edges_kernel, plan, step),
        out_shape=outs,
        in_specs=[VMEM] * (6 + len(more)),
        out_specs=[VMEM] * len(outs),
        scratch_shapes=scratch,
        compiler_params=PARAMS,
        cost_estimate=pl.CostEstimate(
            flops=2 * comps * comps * 2 * LANES, bytes_accessed=8 << 20, transcendentals=0
        ),
        name="edges",
    )(part, from_west, from_east, transfer, coefs, mask, *more)


def finish_kernel(state, given, out, sem):
    width = out.shape[1]
    copies = [
        pltpu.make_async_copy(state.at[side], out.at[:, col, 0, :], sem.at[side])
        for side, col in ((0, 0), (1, width - 1))
    ]
    for c in copies:
        c.start()
    for c in copies:
        c.wait()


def finish(state, out4):
    return pl.pallas_call(
        finish_kernel,
        out_shape=jax.ShapeDtypeStruct(out4.shape, F32),
        in_specs=[ANY, ANY],
        out_specs=ANY,
        scratch_shapes=[pltpu.SemaphoreType.DMA((2,))],
        input_output_aliases={1: 0},
        compiler_params=PARAMS,
        name="finish",
    )(state, out4)


def ocean_shifts(q, west, east, south, north):
    rows, lanes = q.shape
    row = lax.broadcasted_iota(jnp.int32, q.shape, 0)
    lane = lax.broadcasted_iota(jnp.int32, q.shape, 1)
    before = jnp.where(row == 0, west, pltpu.roll(q, 1, 0))
    after = jnp.where(row == rows - 1, east, pltpu.roll(q, rows - 1, 0))
    below = jnp.where(lane == 0, south, pltpu.roll(q, 1, 1))
    above = jnp.where(lane == lanes - 1, north, pltpu.roll(q, lanes - 1, 1))
    return before, after, below, above


def ocean_base_kernel(plan, u, v, from_west, from_east, from_south, from_north, mask, coriolis, base_u, base_v):
    levels, ocean_x, ocean_y = u.shape
    tiles = ocean_y // LANES
    maskf = mask[...].astype(F32)
    half = 0.5 * coriolis[...]
    west_at, east_at = (plan.rows("x", s) for s in (True, False))
    south_at, north_at = (plan.rows("y", s) for s in (True, False))
    for f, (field, other, out, sign) in enumerate(((u, v, base_u, 1.0), (v, u, base_v, -1.0))):
        for level in range(levels):
            q = field[level]

            def line(buffer, at):
                parts = [buffer[at + (f * tiles + m) * levels + level, :][None, :] for m in range(tiles)]
                return jnp.concatenate(parts, axis=1)

            lane = f * levels + level
            before, after, below, above = ocean_shifts(
                q,
                line(from_west, west_at),
                line(from_east, east_at),
                from_south[south_at : south_at + ocean_x, lane : lane + 1],
                from_north[north_at : north_at + ocean_x, lane : lane + 1],
            )
            lap = before + after + below + above - 4.0 * q
            out[level] = maskf * (q + sign * half * other[level] + 0.1 * lap)


def ocean_base(plan, u, v, from_west, from_east, from_south, from_north, mask, coriolis):
    return pl.pallas_call(
        functools.partial(ocean_base_kernel, plan),
        out_shape=[jax.ShapeDtypeStruct(u.shape, F32)] * 2,
        in_specs=[VMEM] * 8,
        out_specs=[VMEM] * 2,
        compiler_params=PARAMS,
        name="ocean_base",
    )(u, v, from_west, from_east, from_south, from_north, mask, coriolis)


def remap_kernel(own, left, right, cell, offset, weight, stress, drift, east, west, north, south, table):
    ocean_x, ocean_y = cell.shape[1:]
    width = own.shape[1]
    ratio = ocean_x // width
    taps = cell.shape[0]
    for q in range(BULK):
        for b, ref in enumerate((left, own, right)):
            for r in range(ratio):
                table[q, pl.ds(b * width * ratio + r, width, stride=ratio), :] = ref[q]
    for t in range(ocean_x // 8):
        for m in range(ocean_y // LANES):
            rows, lanes = (pl.ds(8 * t, 8), pl.ds(m * LANES, LANES))
            at = [cell[p, rows, lanes] for p in range(taps)]
            off = [offset[p, rows, lanes] for p in range(taps)]
            w = [weight[p, rows, lanes] for p in range(taps)]
            acc = [jnp.zeros((8, LANES), F32) for _ in range(BULK)]
            for o in range(2 * width + 1):
                slabs = [table[q, pl.ds(8 * t + ratio * o, 8), :] for q in range(BULK)]
                for p in range(taps):
                    wp = jnp.where(off[p] == o, w[p], 0.0)
                    for q in range(BULK):
                        got = jnp.take_along_axis(slabs[q], at[p], axis=1, mode="promise_in_bounds")
                        acc[q] = acc[q] + wp * got
            for q in range(3):
                stress[q, rows, lanes] = acc[q]
            for q in range(2):
                drift[q, rows, lanes] = acc[3 + q]
    last = ocean_x - 1
    for out, row in ((east, last), (west, 0)):
        out[...] = jnp.zeros_like(out)
        for q in range(2):
            for m in range(ocean_y // LANES):
                n = q * (ocean_y // LANES) + m
                out[n : n + 1, :] = stress[q, row : row + 1, m * LANES : (m + 1) * LANES]
    for out, m, source in ((north, ocean_y - LANES, LANES - 1), (south, 0, 0)):
        acc = jnp.zeros((ocean_x, LANES), F32)
        for q in range(2):
            acc = to_lane(acc, stress[1 + q, :, m : m + LANES], source, q, lanes_of(ocean_x))
        out[...] = acc


def remap(own, left, right, cell, offset, weight):
    taps, ocean_x, ocean_y = cell.shape
    width = own.shape[1]
    side = jax.ShapeDtypeStruct((8 * pl.cdiv(2 * ocean_y // LANES, 8), LANES), F32)
    end = jax.ShapeDtypeStruct((ocean_x, LANES), F32)
    return pl.pallas_call(
        remap_kernel,
        out_shape=[
            jax.ShapeDtypeStruct((3, ocean_x, ocean_y), F32),
            jax.ShapeDtypeStruct((2, ocean_x, ocean_y), F32),
            side,
            side,
            end,
            end,
        ],
        in_specs=[VMEM] * 6,
        out_specs=[VMEM] * 6,
        scratch_shapes=[pltpu.VMEM((BULK, 3 * ocean_x, LANES), F32)],
        compiler_params=PARAMS,
        name="remap",
    )(own, left, right, cell, offset, weight)


def ocean_final_kernel(stress, drift, from_west, from_east, from_south, from_north, base_u, base_v, mask, coriolis, new_u, new_v):
    levels, ocean_x, ocean_y = base_u.shape
    tiles = ocean_y // LANES

    def line(buffer, q):
        return jnp.concatenate([buffer[q * tiles + m : q * tiles + m + 1, :] for m in range(tiles)], axis=1)

    zero_line = jnp.zeros((1, ocean_y), F32)
    zero_end = jnp.zeros((ocean_x, 1), F32)
    grad = []
    for q in range(3):
        lon = q < 2
        lat = q > 0
        before, after, below, above = ocean_shifts(
            stress[q],
            line(from_west, q) if lon else zero_line,
            line(from_east, q) if lon else zero_line,
            from_south[:, q - 1 : q] if lat else zero_end,
            from_north[:, q - 1 : q] if lat else zero_end,
        )
        grad.append((0.5 * (after - before), 0.5 * (above - below)))
    force_x = -(grad[0][0] + grad[1][1])
    force_y = -(grad[1][0] + grad[2][1])
    maskf = mask[...].astype(F32)
    half = 0.5 * coriolis[...]
    add_u = maskf * (half * drift[1] + 0.5 * force_x)
    add_v = maskf * (0.5 * force_y - half * drift[0])
    for level in range(levels):
        decay = np.float32(np.exp(np.float32(-level / 3.0)))
        new_u[level] = base_u[level] + decay * add_u
        new_v[level] = base_v[level] + decay * add_v


def ocean_final(stress, drift, halos, base_u, base_v, mask, coriolis):
    return pl.pallas_call(
        ocean_final_kernel,
        out_shape=[jax.ShapeDtypeStruct(base_u.shape, F32)] * 2,
        in_specs=[VMEM] * 10,
        out_specs=[VMEM] * 2,
        compiler_params=PARAMS,
        name="ocean_final",
    )(stress, drift, *halos, base_u, base_v, mask, coriolis)


def send(value, axis, step, wrap):
    count = lax.axis_size(axis)
    pairs = [(i, (i + step) % count) for i in range(count) if wrap or 0 <= i + step < count]
    return lax.ppermute(value, axis, pairs)


def exchange(east, west, north, south):
    from_west = send(east, "lon", 1, True)
    from_east = send(west, "lon", -1, True)
    from_south = send(north, "lat", 1, False)
    from_north = send(south, "lat", -1, False)
    return from_west, from_east, from_south, from_north


def local(
    spectrum,
    sea_mask,
    transfer,
    bulk_weight,
    remap_cell,
    remap_weight,
    ocean_u,
    ocean_v,
    ocean_mask,
    coriolis,
):
    comps, width_x, width_y = spectrum.shape
    plan = Plan(comps)
    spec4 = spectrum.reshape(comps, width_x, 1, width_y)
    east, west = pack_lon(plan, spec4, sea_mask, ocean_u, ocean_v)
    north, south = pack_lat(plan, spec4, sea_mask, ocean_u, ocean_v)
    from_west, from_east, from_south, from_north = exchange(east, west, north, south)

    coefs = jnp.concatenate([jnp.asarray(plan.coef), bulk_weight.T], axis=1)
    total_y = width_y * lax.axis_size("lat")
    taps_first = remap_cell.transpose(2, 0, 1)
    offset = taps_first // total_y
    cell = taps_first - offset * total_y - lax.axis_index("lat") * width_y
    weight = remap_weight.transpose(2, 0, 1)
    line = coriolis[None, :]

    middle, part, up, down = interior(plan, 0, (spec4,), from_south, from_north, transfer, coefs, sea_mask)
    base_u, base_v = ocean_base(
        plan, ocean_u, ocean_v, from_west, from_east, from_south, from_north, ocean_mask, line
    )
    sides, east, west, north, south = edges(
        plan, 0, part, from_west, from_east, transfer, coefs, sea_mask, up, down
    )
    from_west, from_east, from_south, from_north = exchange(east, west, north, south)
    out4, part, bulk = interior(plan, 1, (sides, middle), from_south, from_north, transfer, coefs, sea_mask)
    sides, bulk = edges(plan, 1, part, from_west, from_east, transfer, coefs, sea_mask, bulk)
    left = send(bulk, "lon", 1, True)
    right = send(bulk, "lon", -1, True)
    state = finish(sides, out4).reshape(spectrum.shape)
    stress, drift, east, west, north, south = remap(bulk, left, right, cell, offset, weight)
    halos = exchange(east, west, north, south)
    new_u, new_v = ocean_final(stress, drift, halos, base_u, base_v, ocean_mask, line)
    return (state, new_u, new_v)


def solution(mesh):
    placed = (
        P(None, "lon", "lat"),
        P("lon", "lat"),
        P(),
        P(),
        P("lon", "lat", None),
        P("lon", "lat", None),
        P(None, "lon", "lat"),
        P(None, "lon", "lat"),
        P("lon", "lat"),
        P("lat"),
    )
    return jax.shard_map(
        local,
        mesh=mesh,
        in_specs=placed,
        out_specs=(P(None, "lon", "lat"), P(None, "lon", "lat"), P(None, "lon", "lat")),
        check_vma=False,
    )
```

```python
import functools

import jax
import jax.numpy as jnp
import numpy as np
from jax import lax
from jax.experimental import pallas as pl
from jax.experimental.pallas import tpu as pltpu
from jax.sharding import PartitionSpec as P

NFREQ = 36
STEP = 16
LANES = 128
BULK = 5
GROUPS = 4
OFFSETS = 17
BLOCK = 80
F32 = jnp.float32
VMEM = pl.BlockSpec(memory_space=pltpu.VMEM)
ANY = pl.BlockSpec(memory_space=pl.ANY)
HBM = pl.BlockSpec(memory_space=pltpu.HBM)
PARAMS = pltpu.CompilerParams(vmem_limit_bytes=24 << 20)
CHEAP = pl.CostEstimate(flops=1, bytes_accessed=1, transcendentals=0)


def pinned(*arrays):
    return [pltpu.with_memory_space_constraint(x, pltpu.HBM) for x in arrays]


class Plan:
    def __init__(self, comps):
        dirs = comps // NFREQ
        k = np.arange(comps)
        theta = 2.0 * np.pi * ((k // NFREQ) + 0.5) / dirs
        speed = 1.1 ** (-(k % NFREQ).astype(np.float64))
        cx = 0.45 * speed * np.cos(theta)
        cy = 0.45 * speed * np.sin(theta)
        self.comps = comps
        self.coef = np.stack([1.0 - np.abs(cx) - np.abs(cy), np.abs(cx), np.abs(cy)], 1).astype(np.float32)
        self.flag = {"x": cx > 0, "y": cy > 0}
        self.seg = {}
        for axis, step in (("x", 8), ("y", STEP)):
            for sign in (True, False):
                self.seg[axis, sign] = self.runs(self.flag[axis] == sign, step)

    def runs(self, flag, step):
        out = []
        for n in np.flatnonzero(flag.reshape(-1, step).any(1)):
            if out and out[-1][1] == n * step:
                out[-1][1] = int(n + 1) * step
            else:
                out.append([int(n) * step, int(n + 1) * step])
        return [(a, b) for a, b in out]

    def rows(self, axis, sign):
        return sum(b - a for a, b in self.seg[axis, sign])

    def lat_rows(self, sign):
        ((a, b),) = self.seg["y", sign]
        return -(-(b - a) // (GROUPS * STEP)) * STEP

    def lat_cuts(self):
        cuts = set()
        for sign in (True, False):
            ((a, b),) = self.seg["y", sign]
            cuts |= set(range(a, b, self.lat_rows(sign))) | {b}
        return cuts

    def lat_place(self, sign, first, last, width):
        ((a, _),) = self.seg["y", sign]
        group, row = divmod(first - a, self.lat_rows(sign))
        assert row + last - first <= self.lat_rows(sign) and (group + 1) * width <= LANES
        return slice(row, row + last - first), group * width

    def lat_blocks(self, sign, first=0, last=None):
        ((a, b),) = self.seg["y", sign]
        a, b = (max(a, first), b if last is None else min(b, last))
        return split(a, b, self.lat_cuts()) if a < b else []

    def shift(self, axis, sign, first):
        used = np.flatnonzero(self.flag[axis][first : first + STEP] == sign) + first
        if not len(used):
            return None
        base = 0
        for a, b in self.seg[axis, sign]:
            if a <= used[0] < b:
                at = base + first - a
                assert used[-1] < b and 0 <= at <= self.rows(axis, sign) - STEP
                return base - a
            base += b - a
        raise ValueError("no segment")

    def blocks(self):
        cuts = self.lat_cuts()
        return [(a, b, *rest) for first, last, *rest in self.regions() for a, b in split(first, last, cuts)]

    def regions(self):
        out = []
        for r in range(0, self.comps, STEP):
            sign = {}
            for axis in "xy":
                part = self.flag[axis][r : r + STEP]
                sign[axis] = 1 if part.all() else (0 if part.any() else -1)
            shifts = {(axis, s): self.shift(axis, s, r) for axis in "xy" for s in (True, False)}
            if out and sign["x"] and sign["y"] and out[-1][2:] == [sign["x"], sign["y"], shifts]:
                out[-1][1] = r + STEP
            else:
                out.append([r, r + STEP, sign["x"], sign["y"], shifts])
        return out


def split(first, last, cuts=(), most=BLOCK):
    out = []
    edges = [first] + sorted(c for c in cuts if first < c < last) + [last]
    for start, stop in zip(edges[:-1], edges[1:]):
        chunks = (stop - start) // STEP
        count = -(-chunks * STEP // most)
        at = [start + chunks * n // count * STEP for n in range(count + 1)]
        out += list(zip(at[:-1], at[1:]))
    return out


def lanes_of(rows):
    return lax.broadcasted_iota(jnp.int32, (rows, LANES), 1)


def picked(flag, first):
    row = lax.broadcasted_iota(jnp.int32, (STEP, LANES), 0)
    part = flag[first : first + STEP]
    out, n = (None, 0)
    while n < STEP:
        if not part[n]:
            n += 1
            continue
        m = n
        while m < STEP and part[m]:
            m += 1
        here = (row >= n) & (row < m)
        out = here if out is None else out | here
        n = m
    return out


def upwind(plan, axis, sign, first, from_plus, from_minus):
    if sign > 0:
        return from_plus()
    if sign < 0:
        return from_minus()
    plus, minus = (from_plus(), from_minus())
    where = picked(plan.flag[axis], first)
    zero = jnp.zeros((STEP, LANES), F32)
    if plus is None and minus is None:
        return None
    return jnp.where(where, zero if plus is None else plus, zero if minus is None else minus)


def pack_lon_kernel(plan, spec, mask, u, v, east, west, sides, maskv, sem):
    last_col, last_row, levels = (spec.shape[1] - 1, u.shape[1] - 8, u.shape[0])
    copies = [pltpu.make_async_copy(mask, maskv, sem.at[0])]
    for out, sign, col in ((east, True, last_col), (west, False, 0)):
        at = 0
        for a, b in plan.seg["x", sign]:
            copies.append(
                pltpu.make_async_copy(
                    spec.at[pl.ds(a, b - a), col, 0, :], out.at[pl.ds(at, b - a), :], sem.at[len(copies)]
                )
            )
            at += b - a
    for f, field in enumerate((u, v)):
        for side, row in enumerate((last_row, 0)):
            copies.append(
                pltpu.make_async_copy(field.at[:, pl.ds(row, 8), :], sides.at[f, side], sem.at[len(copies)])
            )
    for c in copies:
        c.start()
    for c in copies:
        c.wait()
    for side, (out, sign, col) in enumerate(((east, True, last_col), (west, False, 0))):
        at = plan.rows("x", sign)
        out[:at, :] = out[:at, :] * maskv[col : col + 1, :].astype(F32)
        for f in range(2):
            for m in range(u.shape[2] // LANES):
                out[at : at + levels, :] = sides[f, side, :, 7 - 7 * side, m * LANES : (m + 1) * LANES]
                at += levels


def pack_lon(plan, spec4, mask, u, v):
    extra = 2 * u.shape[0] * u.shape[2] // LANES
    segments = sum(len(plan.seg["x", s]) for s in (True, False))
    return pl.pallas_call(
        functools.partial(pack_lon_kernel, plan),
        out_shape=[jax.ShapeDtypeStruct((plan.rows("x", s) + extra, LANES), F32) for s in (True, False)],
        in_specs=[HBM] * 4,
        out_specs=[VMEM, VMEM],
        scratch_shapes=[
            pltpu.VMEM((2, 2, u.shape[0], 8, u.shape[2]), F32),
            pltpu.VMEM(mask.shape, mask.dtype),
            pltpu.SemaphoreType.DMA((segments + 5,)),
        ],
        compiler_params=PARAMS,
        name="pack_lon",
    )(*pinned(spec4, mask, u, v))


def to_lane(acc, column, source, lane, lanes):
    return jnp.where(lanes == lane, pltpu.roll(column, (lane - source) % LANES, 1), acc)


def pack_lat_kernel(plan, spec_hbm, mask, u_hbm, v_hbm, after, north, south, spec, u, v, maskv, sem):
    del after
    width_x = mask.shape[0]
    levels, ocean_x, ocean_y = u.shape
    last = ocean_y - LANES
    first = pltpu.make_async_copy(mask, maskv, sem.at[0])
    first.start()
    cuts = [a for a, _ in split(0, plan.comps)] + [plan.comps]
    parts = []
    for n in range(len(cuts) - 1):
        rows = pl.ds(cuts[n] * width_x, (cuts[n + 1] - cuts[n]) * width_x)
        parts.append(pltpu.make_async_copy(spec_hbm.at[rows, :], spec.at[rows, :], sem.at[3 + n]))
        parts[-1].start()
    fields = [pltpu.make_async_copy(x, y, sem.at[1 + n]) for n, (x, y) in enumerate(((u_hbm, u), (v_hbm, v)))]
    for c in fields:
        c.start()
    first.wait()
    maskf = maskv[...].astype(F32)
    here = 0
    for out, source, sign in ((north, LANES - 1, True), (south, 0, False)):
        for a, b in plan.lat_blocks(sign):
            while cuts[here] < b:
                parts[here].wait()
                here += 1
            rows, lane = plan.lat_place(sign, a, b, width_x)
            acc = out[rows, :] if lane else jnp.zeros((b - a, LANES), F32)
            for i in range(width_x):
                x = spec[pl.ds(a * width_x + i, b - a, stride=width_x), :] * maskf[i : i + 1, :]
                acc = to_lane(acc, x, source, lane + i, lanes_of(b - a))
            out[rows, :] = acc
    assert here == len(parts)
    for c in fields:
        c.wait()
    for out, source, sign, m in ((north, LANES - 1, True, last), (south, 0, False, 0)):
        at = plan.lat_rows(sign)
        acc = jnp.zeros((ocean_x, LANES), F32)
        for f in range(2 * levels):
            field = (u, v)[f // levels]
            acc = to_lane(acc, field[f % levels, :, m : m + LANES], source, f, lanes_of(ocean_x))
        out[at : at + ocean_x, :] = acc


def pack_lat(plan, spec2, mask, u, v, after):
    extra = u.shape[1]
    return pl.pallas_call(
        functools.partial(pack_lat_kernel, plan),
        out_shape=[jax.ShapeDtypeStruct((plan.lat_rows(s) + extra, LANES), F32) for s in (True, False)],
        in_specs=[HBM] * 4 + [ANY],
        out_specs=[VMEM] * 2,
        cost_estimate=CHEAP,
        scratch_shapes=[pltpu.VMEM(x.shape, F32) for x in (spec2, u, v)]
        + [
            pltpu.VMEM(mask.shape, mask.dtype),
            pltpu.SemaphoreType.DMA((3 + len(split(0, plan.comps)),)),
        ],
        compiler_params=PARAMS,
        name="pack_lat",
    )(*pinned(spec2, mask, u, v), after)


def advect_kernel(plan, step, *refs):
    if step == 0:
        state_hbm, transfer_hbm, coefs, mask, part, transfer, state, sem = refs
    else:
        state_hbm, transfer_hbm, coefs, sides, part, transfer, state, sem = refs
    width = part.shape[0]
    blocks = plan.blocks()
    parts = []
    for first, last, *_ in blocks:
        if step == 0:
            rows = pl.ds(first * width, (last - first) * width)
            copy = pltpu.make_async_copy(state_hbm.at[rows, :], state.at[rows, :], sem.at[1 + len(parts)])
        else:
            rows = pl.ds(first, last - first)
            copy = pltpu.make_async_copy(state_hbm.at[:, rows, :], state.at[:, rows, :], sem.at[1 + len(parts)])
        copy.start()
        parts.append(copy)
    fetch = pltpu.make_async_copy(transfer_hbm, transfer, sem.at[0])
    fetch.start()
    if step == 0:
        maskf = mask[...].astype(F32)

    def column(i, first, last):
        if step == 0:
            return state[pl.ds(first * width + i, last - first, stride=width), :] * maskf[i : i + 1, :]
        if i in (0, width - 1):
            return sides[min(i, 1), first:last, :]
        return state[i - 1, first:last, :]

    for copy, (first, last, xs, ys, _) in zip(parts, blocks):
        count = last - first
        keep, east, up = (jnp.broadcast_to(coefs[first:last, q : q + 1], (count, LANES)) for q in range(3))
        lanes = lanes_of(count)
        copy.wait()
        x = [column(i, first, last) for i in range(width)]
        for i in range(width):
            lat = upwind(
                plan, "y", ys, first,
                lambda: jnp.where(lanes == 0, 0.0, pltpu.roll(x[i], 1, 1)),
                lambda: jnp.where(lanes == LANES - 1, 0.0, pltpu.roll(x[i], LANES - 1, 1)),
            )
            lon = upwind(
                plan, "x", xs, first,
                lambda: x[i - 1] if i else None,
                lambda: x[i + 1] if i + 1 < width else None,
            )
            a = keep * x[i] + up * lat
            if lon is not None:
                a = a + east * lon
            part[i, first:last, :] = a
    fetch.wait()


def advect(plan, step, state, transfer, coefs, more):
    comps, width = (plan.comps, state.shape[0] // plan.comps if step == 0 else state.shape[0] + 2)
    hbm_state, hbm_transfer = pinned(state, transfer)
    return pl.pallas_call(
        functools.partial(advect_kernel, plan, step),
        out_shape=[
            jax.ShapeDtypeStruct((width, comps, LANES), F32),
            jax.ShapeDtypeStruct(transfer.shape, transfer.dtype),
        ],
        in_specs=[HBM, HBM, VMEM, VMEM],
        out_specs=[VMEM, VMEM],
        scratch_shapes=[pltpu.VMEM(state.shape, F32), pltpu.SemaphoreType.DMA((1 + len(plan.blocks()),))],
        compiler_params=PARAMS,
        cost_estimate=CHEAP,
        name="advect",
    )(hbm_state, hbm_transfer, coefs, more)


def block_rows(comps):
    return max(b for b in range(STEP, 449, STEP) if comps % b == 0)


def source_blocks(transfer, moved, comps, body):
    block = block_rows(comps)

    for n in range(comps // block):
        rows = slice(n * block, (n + 1) * block)
        body(n, rows, jnp.dot(transfer[rows, :], moved[...], preferred_element_type=F32))


def add_bulk(coefs, weights, rows, state, total):
    count = rows.stop - rows.start
    for q in range(BULK):
        if coefs is None:
            w = weights[q, rows, :]
        else:
            w = jnp.broadcast_to(coefs[rows, 3 + q : 4 + q], (count, LANES))
            weights[q, rows, :] = w
        for i in range(state.shape[0]):
            part = (w * state[i, rows, :]).reshape(count // 8, 8, LANES).sum(0)
            total[q, i] = total[q, i] + part


def interior_kernel(plan, step, *refs):
    part, south, north, transfer, coefs, mask = refs[:6]
    if step == 0:
        out, edge, up, down = refs[6:10]
        inner, full, moved, sem = refs[10:]
    else:
        out, edge, bulk, weights = refs[6:10]
        inner, full, moved, total, sem = refs[10:]
        total[...] = jnp.zeros_like(total)
    width = part.shape[0]
    maskf = mask[...].astype(F32)
    for first, last, _, ys, shifts in plan.blocks():
        rows, count = (slice(first, last), last - first)
        lanes = lanes_of(count)
        speed = jnp.broadcast_to(coefs[rows, 2:3], (count, LANES))
        halos = []
        for sign, buffer, lane in ((True, south, 0), (False, north, LANES - 1)):
            if shifts["y", sign] is not None:
                at, base = plan.lat_place(sign, first, last, width)
                here = lanes == lane
                if ys == 0:
                    here = here & picked(plan.flag["y"] == sign, first)
                halos.append((buffer[at, :] * speed, here, lane, base))
        for i in range(width):
            a = part[i, rows, :]
            for halo, here, lane, base in halos:
                a = a + jnp.where(here, pltpu.roll(halo, (lane - base - i) % LANES, 1), 0.0)
            if i in (0, width - 1):
                edge[min(i, 1), rows, :] = a
            else:
                full[i - 1, rows, :] = a
                moved[rows, (i - 1) * LANES : i * LANES] = a.astype(jnp.bfloat16)
    copies = []

    def done(n, rows, added):
        span = pl.ds(rows.start, rows.stop - rows.start)
        for i in range(1, width - 1):
            s = maskf[i : i + 1, :] * (full[i - 1, rows, :] + 0.5 * added[:, (i - 1) * LANES : i * LANES])
            inner[i - 1, rows, :] = s
            to = out.at[span, i, 0, :] if step else out.at[i - 1, span, :]
            copies.append(pltpu.make_async_copy(inner.at[i - 1, span, :], to, sem.at[len(copies)]))
            copies[-1].start()
        if step:
            add_bulk(coefs, weights, rows, inner, total)
            return
        for packed, source, sign in ((up, LANES - 1, True), (down, 0, False)):
            for a, b in plan.lat_blocks(sign, rows.start, rows.stop):
                at, base = plan.lat_place(sign, a, b, width)
                acc = packed[at, :] if base else jnp.zeros((b - a, LANES), F32)
                for i in range(1, width - 1):
                    acc = to_lane(acc, inner[i - 1, a:b, :], source, base + i, lanes_of(b - a))
                packed[at, :] = acc

    source_blocks(transfer, moved, plan.comps, done)
    if step:
        for q in range(BULK):
            for i in range(1, width - 1):
                bulk[q, i : i + 1, :] = total[q, i - 1].sum(0, keepdims=True)
            bulk[q, 0:1, :] = jnp.zeros((1, LANES), F32)
            bulk[q, width - 1 : width, :] = jnp.zeros((1, LANES), F32)
    for c in copies:
        c.wait()


def interior(plan, step, part, south, north, transfer, coefs, mask):
    comps, width = (plan.comps, mask.shape[0])
    middle = (width - 2, comps, LANES)
    edge = jax.ShapeDtypeStruct((2, comps, LANES), F32)
    scratch = [
        pltpu.VMEM(middle, F32),
        pltpu.VMEM(middle, F32),
        pltpu.VMEM((comps, (width - 2) * LANES), jnp.bfloat16),
    ]
    if step == 0:
        outs = [pltpu.HBM(middle, F32), edge]
        outs += [jax.ShapeDtypeStruct((plan.lat_rows(s), LANES), F32) for s in (True, False)]
    else:
        outs = [pltpu.HBM((comps, width, 1, LANES), F32), edge, jax.ShapeDtypeStruct((BULK, width, LANES), F32)]
        outs += [jax.ShapeDtypeStruct((BULK, comps, LANES), F32)]
        scratch += [pltpu.VMEM((BULK, width - 2, 8, LANES), F32)]
    scratch += [pltpu.SemaphoreType.DMA(((width - 2) * comps // block_rows(comps),))]
    return pl.pallas_call(
        functools.partial(interior_kernel, plan, step),
        out_shape=outs,
        in_specs=[VMEM] * 6,
        out_specs=[HBM] + [VMEM] * (len(outs) - 1),
        scratch_shapes=scratch,
        compiler_params=PARAMS,
        cost_estimate=CHEAP,
        name="interior",
    )(part, south, north, transfer, coefs, mask)


def edges_kernel(plan, step, *refs):
    refs = list(refs)
    part, from_west, from_east, transfer, coefs, mask = refs[:6]
    if step == 0:
        state, east, west = refs[6:9]
        full, moved = refs[9:]
    else:
        bulk_in, weights = refs[6:8]
        state, bulk = refs[8:10]
        full, moved, total = refs[10:]
    width = mask.shape[0]
    maskf = jnp.concatenate([mask[0:1, :], mask[width - 1 : width, :]], axis=0).astype(F32)

    for first, last, xs, ys, shifts in plan.blocks():
        rows, count = (slice(first, last), last - first)
        speed = jnp.broadcast_to(coefs[rows, 1:2], (count, LANES))
        for side, sign, buffer in ((0, True, from_west), (1, False, from_east)):
            a = part[side, rows, :]
            shift = shifts["x", sign]
            if shift is not None:
                halo = buffer[first + shift : last + shift, :]
                if xs == 0:
                    halo = jnp.where(picked(plan.flag["x"] == sign, first), halo, 0.0)
                a = a + speed * halo
            full[side, rows, :] = a
            moved[rows, side * LANES : (side + 1) * LANES] = a.astype(jnp.bfloat16)
    if step:
        total[...] = jnp.zeros_like(total)

    def done(n, rows, added):
        for side in range(2):
            s = maskf[side : side + 1, :] * (full[side, rows, :] + 0.5 * added[:, side * LANES : (side + 1) * LANES])
            state[side, rows, :] = s
        if step:
            add_bulk(None, weights, rows, state, total)

    source_blocks(transfer, moved, plan.comps, done)
    if step:
        for q in range(BULK):
            bulk[q] = bulk_in[q]
            bulk[q, 0:1, :] = total[q, 0].sum(0, keepdims=True)
            bulk[q, width - 1 : width, :] = total[q, 1].sum(0, keepdims=True)
        return
    for out, side, sign in ((east, 1, True), (west, 0, False)):
        at = 0
        for a, b in plan.seg["x", sign]:
            out[at : at + b - a, :] = state[side, a:b, :]
            at += b - a


def merge_lat_kernel(plan, width, state, up_in, down_in, up, down):
    for out, given, source, sign in ((up, up_in, LANES - 1, True), (down, down_in, 0, False)):
        for a, b in plan.lat_blocks(sign):
            at, base = plan.lat_place(sign, a, b, width)
            acc = out[at, :] if base else given[at, :]
            for side, lane in ((0, base), (1, base + width - 1)):
                acc = to_lane(acc, state[side, a:b, :], source, lane, lanes_of(b - a))
            out[at, :] = acc


def merge_lat(plan, width, state, up, down):
    return pl.pallas_call(
        functools.partial(merge_lat_kernel, plan, width),
        out_shape=[jax.ShapeDtypeStruct(x.shape, F32) for x in (up, down)],
        in_specs=[VMEM] * 3,
        out_specs=[VMEM] * 2,
        compiler_params=PARAMS,
        cost_estimate=CHEAP,
        name="merge_lat",
    )(state, up, down)


def edges(plan, step, part, from_west, from_east, transfer, coefs, mask, *more):
    comps, width = (plan.comps, mask.shape[0])
    outs = [jax.ShapeDtypeStruct((2, comps, LANES), F32)]
    scratch = [pltpu.VMEM((2, comps, LANES), F32), pltpu.VMEM((comps, 2 * LANES), jnp.bfloat16)]
    if step == 0:
        outs += [jax.ShapeDtypeStruct((plan.rows("x", s), LANES), F32) for s in (True, False)]
    else:
        outs += [jax.ShapeDtypeStruct((BULK, width, LANES), F32)]
        scratch += [pltpu.VMEM((BULK, 2, 8, LANES), F32)]
    return pl.pallas_call(
        functools.partial(edges_kernel, plan, step),
        out_shape=outs,
        in_specs=[VMEM] * (6 + len(more)),
        out_specs=[VMEM] * len(outs),
        scratch_shapes=scratch,
        compiler_params=PARAMS,
        cost_estimate=CHEAP,
        name="edges",
    )(part, from_west, from_east, transfer, coefs, mask, *more)


def finish_kernel(state, given, out, sem):
    width = out.shape[1]
    copies = [
        pltpu.make_async_copy(state.at[side], out.at[:, col, 0, :], sem.at[side])
        for side, col in ((0, 0), (1, width - 1))
    ]
    for c in copies:
        c.start()
    for c in copies:
        c.wait()


def finish(state, out4):
    return pl.pallas_call(
        finish_kernel,
        out_shape=jax.ShapeDtypeStruct(out4.shape, F32),
        in_specs=[ANY, ANY],
        out_specs=ANY,
        scratch_shapes=[pltpu.SemaphoreType.DMA((2,))],
        input_output_aliases={1: 0},
        compiler_params=PARAMS,
        name="finish",
    )(state, out4)


def ocean_shifts(q, west, east, south, north):
    rows, lanes = q.shape
    row = lax.broadcasted_iota(jnp.int32, q.shape, 0)
    lane = lax.broadcasted_iota(jnp.int32, q.shape, 1)
    before = jnp.where(row == 0, west, pltpu.roll(q, 1, 0))
    after = jnp.where(row == rows - 1, east, pltpu.roll(q, rows - 1, 0))
    below = jnp.where(lane == 0, south, pltpu.roll(q, 1, 1))
    above = jnp.where(lane == lanes - 1, north, pltpu.roll(q, lanes - 1, 1))
    return before, after, below, above


def ocean_base_kernel(plan, u, v, from_west, from_east, from_south, from_north, mask, coriolis, base_u, base_v):
    levels, ocean_x, ocean_y = u.shape
    tiles = ocean_y // LANES
    maskf = mask[...].astype(F32)
    half = 0.5 * coriolis[...]
    west_at, east_at = (plan.rows("x", s) for s in (True, False))
    south_at, north_at = (plan.lat_rows(s) for s in (True, False))
    for f, (field, other, out, sign) in enumerate(((u, v, base_u, 1.0), (v, u, base_v, -1.0))):
        for level in range(levels):
            q = field[level]

            def line(buffer, at):
                parts = [buffer[at + (f * tiles + m) * levels + level, :][None, :] for m in range(tiles)]
                return jnp.concatenate(parts, axis=1)

            lane = f * levels + level
            before, after, below, above = ocean_shifts(
                q,
                line(from_west, west_at),
                line(from_east, east_at),
                from_south[south_at : south_at + ocean_x, lane : lane + 1],
                from_north[north_at : north_at + ocean_x, lane : lane + 1],
            )
            lap = before + after + below + above - 4.0 * q
            out[level] = maskf * (q + sign * half * other[level] + 0.1 * lap)


def ocean_base(plan, u, v, from_west, from_east, from_south, from_north, mask, coriolis):
    return pl.pallas_call(
        functools.partial(ocean_base_kernel, plan),
        out_shape=[jax.ShapeDtypeStruct(u.shape, F32)] * 2,
        in_specs=[VMEM] * 8,
        out_specs=[VMEM] * 2,
        compiler_params=PARAMS,
        name="ocean_base",
    )(u, v, from_west, from_east, from_south, from_north, mask, coriolis)


def gathered(slabs, at, off, weight, count):
    acc = [0.0] * count
    for o in range(OFFSETS):
        rows = [slabs(o, q) for q in range(count)]
        for p in range(len(at)):
            w = jnp.where(off[p] == o, weight[p], 0.0)
            for q in range(count):
                acc[q] = acc[q] + w * jnp.take_along_axis(rows[q], at[p], axis=1, mode="promise_in_bounds")
    return acc


def fill_table(table, left, own, right, ratio, fields):
    width = own.shape[1]
    for q in fields:
        for b, ref in enumerate((left, own, right)):
            for r in range(ratio):
                table[q, pl.ds(b * width * ratio + r, width, stride=ratio), :] = ref[q]


def remap_lon_kernel(own, left, right, cell, offset, weight, east, west, rows):
    taps, ocean_x, ocean_y = cell.shape
    width = own.shape[1]
    tiles = ocean_y // LANES
    last_row = ocean_x - 8
    for b, ref in enumerate((left, own, right)):
        rows[:, b * width : (b + 1) * width, :] = ref[0:2]
    first_half = lax.broadcasted_iota(jnp.int32, (8, LANES), 0) < 4
    for m in range(tiles):
        lanes = slice(m * LANES, (m + 1) * LANES)
        at, off, w = (
            [jnp.where(first_half, x[p, 0:8, lanes], x[p, last_row : last_row + 8, lanes]) for p in range(taps)]
            for x in (cell, offset, weight)
        )
        acc = gathered(lambda o, q: rows[q, o : o + 8, :], at, off, w, 2)
        for q in range(2):
            n = q * tiles + m
            east[n : n + 1, :] = acc[q][7:8, :]
            west[n : n + 1, :] = acc[q][0:1, :]
    if 2 * tiles < east.shape[0]:
        for out in (east, west):
            out[2 * tiles :, :] = jnp.zeros((out.shape[0] - 2 * tiles, LANES), F32)


def remap_lat_kernel(own, left, right, cell, offset, weight, after, north, south, table):
    del after
    taps, ocean_x, ocean_y = cell.shape
    ratio = ocean_x // own.shape[1]
    last_lane = ocean_y - LANES
    fill_table(table, left, own, right, ratio, range(1, 3))
    lanes = lanes_of(8)
    for t in range(ocean_x // 8):
        here = slice(8 * t, 8 * t + 8)
        at, off, w = (
            [jnp.where(lanes < LANES // 2, x[p, here, 0:LANES], x[p, here, last_lane:]) for p in range(taps)]
            for x in (cell, offset, weight)
        )
        acc = gathered(lambda o, q: table[1 + q, 8 * t + ratio * o : 8 * t + ratio * o + 8, :], at, off, w, 2)
        for out, source in ((north, LANES - 1), (south, 0)):
            packed = jnp.zeros((8, LANES), F32)
            for q in range(2):
                packed = to_lane(packed, acc[q], source, q, lanes)
            out[here, :] = packed


def remap_lon(own, left, right, cell, offset, weight):
    _, ocean_x, ocean_y = cell.shape
    width = own.shape[1]
    assert width == 8 and ocean_x % width == 0
    side = jax.ShapeDtypeStruct((8 * pl.cdiv(2 * ocean_y // LANES, 8), LANES), F32)
    return pl.pallas_call(
        remap_lon_kernel,
        out_shape=[side, side],
        in_specs=[VMEM] * 6,
        out_specs=[VMEM] * 2,
        scratch_shapes=[pltpu.VMEM((2, 3 * width, LANES), F32)],
        compiler_params=PARAMS,
        cost_estimate=CHEAP,
        name="remap_lon",
    )(own, left, right, cell, offset, weight)


def remap_lat(own, left, right, cell, offset, weight, after):
    ocean_x = cell.shape[1]
    end = jax.ShapeDtypeStruct((ocean_x, LANES), F32)
    return pl.pallas_call(
        remap_lat_kernel,
        out_shape=[end, end],
        in_specs=[VMEM] * 6 + [ANY],
        out_specs=[VMEM] * 2,
        scratch_shapes=[pltpu.VMEM((BULK, 3 * ocean_x, LANES), F32)],
        compiler_params=PARAMS,
        cost_estimate=CHEAP,
        name="remap_lat",
    )(own, left, right, cell, offset, weight, after)


def remap_kernel(own, left, right, cell, offset, weight, stress, drift, table):
    taps, ocean_x, ocean_y = cell.shape
    ratio = ocean_x // own.shape[1]
    fill_table(table, left, own, right, ratio, range(BULK))
    for t in range(ocean_x // 8):
        for m in range(ocean_y // LANES):
            rows, lanes = (slice(8 * t, 8 * t + 8), slice(m * LANES, (m + 1) * LANES))
            at, off, w = ([x[p, rows, lanes] for p in range(taps)] for x in (cell, offset, weight))
            acc = gathered(
                lambda o, q: table[q, 8 * t + ratio * o : 8 * t + ratio * o + 8, :], at, off, w, BULK
            )
            for q in range(3):
                stress[q, rows, lanes] = acc[q]
            for q in range(2):
                drift[q, rows, lanes] = acc[3 + q]


def remap(own, left, right, cell, offset, weight):
    _, ocean_x, ocean_y = cell.shape
    return pl.pallas_call(
        remap_kernel,
        out_shape=[jax.ShapeDtypeStruct((n, ocean_x, ocean_y), F32) for n in (3, 2)],
        in_specs=[VMEM] * 6,
        out_specs=[VMEM] * 2,
        scratch_shapes=[pltpu.VMEM((BULK, 3 * ocean_x, LANES), F32)],
        compiler_params=PARAMS,
        cost_estimate=CHEAP,
        name="remap",
    )(own, left, right, cell, offset, weight)


def ocean_final_kernel(stress, drift, from_west, from_east, from_south, from_north, base_u, base_v, mask, coriolis, new_u, new_v):
    levels, ocean_x, ocean_y = base_u.shape
    tiles = ocean_y // LANES

    def line(buffer, q):
        return jnp.concatenate([buffer[q * tiles + m : q * tiles + m + 1, :] for m in range(tiles)], axis=1)

    zero_line = jnp.zeros((1, ocean_y), F32)
    zero_end = jnp.zeros((ocean_x, 1), F32)
    grad = []
    for q in range(3):
        lon = q < 2
        lat = q > 0
        before, after, below, above = ocean_shifts(
            stress[q],
            line(from_west, q) if lon else zero_line,
            line(from_east, q) if lon else zero_line,
            from_south[:, q - 1 : q] if lat else zero_end,
            from_north[:, q - 1 : q] if lat else zero_end,
        )
        grad.append((0.5 * (after - before), 0.5 * (above - below)))
    force_x = -(grad[0][0] + grad[1][1])
    force_y = -(grad[1][0] + grad[2][1])
    maskf = mask[...].astype(F32)
    half = 0.5 * coriolis[...]
    add_u = maskf * (half * drift[1] + 0.5 * force_x)
    add_v = maskf * (0.5 * force_y - half * drift[0])
    for level in range(levels):
        decay = np.float32(np.exp(np.float32(-level / 3.0)))
        new_u[level] = base_u[level] + decay * add_u
        new_v[level] = base_v[level] + decay * add_v


def ocean_final(stress, drift, halos, base_u, base_v, mask, coriolis):
    return pl.pallas_call(
        ocean_final_kernel,
        out_shape=[jax.ShapeDtypeStruct(base_u.shape, F32)] * 2,
        in_specs=[VMEM] * 10,
        out_specs=[VMEM] * 2,
        compiler_params=PARAMS,
        name="ocean_final",
    )(stress, drift, *halos, base_u, base_v, mask, coriolis)


def send(value, axis, step, wrap):
    count = lax.axis_size(axis)
    pairs = [(i, (i + step) % count) for i in range(count) if wrap or 0 <= i + step < count]
    return lax.ppermute(value, axis, pairs)


def exchange(east, west, north, south):
    from_south = send(north, "lat", 1, False)
    from_north = send(south, "lat", -1, False)
    from_west = send(east, "lon", 1, True)
    from_east = send(west, "lon", -1, True)
    return from_west, from_east, from_south, from_north


def local(
    spectrum,
    sea_mask,
    transfer,
    bulk_weight,
    remap_cell,
    remap_weight,
    ocean_u,
    ocean_v,
    ocean_mask,
    coriolis,
):
    comps, width_x, width_y = spectrum.shape
    plan = Plan(comps)
    spec2 = spectrum.reshape(comps * width_x, width_y)
    east, west = pack_lon(plan, spectrum.reshape(comps, width_x, 1, width_y), sea_mask, ocean_u, ocean_v)
    north, south = pack_lat(plan, spec2, sea_mask, ocean_u, ocean_v, east)
    from_west, from_east, from_south, from_north = exchange(east, west, north, south)

    coefs = jnp.concatenate([jnp.asarray(plan.coef), bulk_weight.T], axis=1)
    total_y = width_y * lax.axis_size("lat")
    taps_first = remap_cell.transpose(2, 0, 1)
    offset = taps_first // total_y
    cell = taps_first - offset * total_y - lax.axis_index("lat") * width_y
    weight = remap_weight.transpose(2, 0, 1)
    line = coriolis[None, :]

    part, held = advect(plan, 0, spec2, transfer, coefs, sea_mask)
    middle, edge, up, down = interior(plan, 0, part, from_south, from_north, held, coefs, sea_mask)
    base_u, base_v = ocean_base(
        plan, ocean_u, ocean_v, from_west, from_east, from_south, from_north, ocean_mask, line
    )
    sides, east, west = edges(plan, 0, edge, from_west, from_east, held, coefs, sea_mask)
    north, south = merge_lat(plan, width_x, sides, up, down)
    from_west, from_east, from_south, from_north = exchange(east, west, north, south)

    part, held = advect(plan, 1, middle, transfer, coefs, sides)
    out4, edge, bulk, weights = interior(plan, 1, part, from_south, from_north, held, coefs, sea_mask)
    sides, bulk = edges(plan, 1, edge, from_west, from_east, held, coefs, sea_mask, bulk, weights)
    left = send(bulk, "lon", 1, True)
    right = send(bulk, "lon", -1, True)
    state = finish(sides, out4).reshape(spectrum.shape)

    remapped = (bulk, left, right, cell, offset, weight)
    east, west = remap_lon(*remapped)
    north, south = remap_lat(*remapped, east)
    halos = exchange(east, west, north, south)
    stress, drift = remap(*remapped)
    new_u, new_v = ocean_final(stress, drift, halos, base_u, base_v, ocean_mask, line)
    return (state, new_u, new_v)


def solution(mesh):
    placed = (
        P(None, "lon", "lat"),
        P("lon", "lat"),
        P(),
        P(),
        P("lon", "lat", None),
        P("lon", "lat", None),
        P(None, "lon", "lat"),
        P(None, "lon", "lat"),
        P("lon", "lat"),
        P("lat"),
    )
    return jax.shard_map(
        local,
        mesh=mesh,
        in_specs=placed,
        out_specs=(P(None, "lon", "lat"), P(None, "lon", "lat"), P(None, "lon", "lat")),
        check_vma=False,
    )
```

```python
import functools

import jax
import jax.numpy as jnp
import numpy as np
from jax import lax
from jax.experimental import pallas as pl
from jax.experimental.pallas import tpu as pltpu
from jax.sharding import PartitionSpec as P

NFREQ = 36
STEP = 16
LANES = 128
BULK = 5
GROUPS = 4
OFFSETS = 17
BLOCK = 80
F32 = jnp.float32
VMEM = pl.BlockSpec(memory_space=pltpu.VMEM)
ANY = pl.BlockSpec(memory_space=pl.ANY)
HBM = pl.BlockSpec(memory_space=pltpu.HBM)
PARAMS = pltpu.CompilerParams(vmem_limit_bytes=24 << 20)
CHEAP = pl.CostEstimate(flops=1, bytes_accessed=1, transcendentals=0)


def pinned(*arrays):
    return [pltpu.with_memory_space_constraint(x, pltpu.HBM) for x in arrays]


def kept(array):
    return pltpu.with_memory_space_constraint(array, pltpu.VMEM)


def parity():
    return lax.rem(lax.axis_index("lat"), 2)


class Plan:
    def __init__(self, comps):
        dirs = comps // NFREQ
        k = np.arange(comps)
        theta = 2.0 * np.pi * ((k // NFREQ) + 0.5) / dirs
        speed = 1.1 ** (-(k % NFREQ).astype(np.float64))
        cx = 0.45 * speed * np.cos(theta)
        cy = 0.45 * speed * np.sin(theta)
        self.comps = comps
        self.coef = np.stack([1.0 - np.abs(cx) - np.abs(cy), np.abs(cx), np.abs(cy)], 1).astype(np.float32)
        self.flag = {"x": cx > 0, "y": cy > 0}
        self.seg = {}
        for axis, step in (("x", 8), ("y", STEP)):
            for sign in (True, False):
                self.seg[axis, sign] = self.runs(self.flag[axis] == sign, step)

    def runs(self, flag, step):
        out = []
        for n in np.flatnonzero(flag.reshape(-1, step).any(1)):
            if out and out[-1][1] == n * step:
                out[-1][1] = int(n + 1) * step
            else:
                out.append([int(n) * step, int(n + 1) * step])
        return [(a, b) for a, b in out]

    def rows(self, axis, sign):
        return sum(b - a for a, b in self.seg[axis, sign])

    def lat_rows(self, sign):
        ((a, b),) = self.seg["y", sign]
        return -(-(b - a) // (GROUPS * STEP)) * STEP

    def lat_cuts(self):
        cuts = set()
        for sign in (True, False):
            ((a, b),) = self.seg["y", sign]
            cuts |= set(range(a, b, self.lat_rows(sign))) | {b}
        return cuts

    def lat_place(self, sign, first, last, width):
        ((a, _),) = self.seg["y", sign]
        group, row = divmod(first - a, self.lat_rows(sign))
        assert row + last - first <= self.lat_rows(sign) and (group + 1) * width <= LANES
        return slice(row, row + last - first), group * width

    def lat_blocks(self, sign, first=0, last=None):
        ((a, b),) = self.seg["y", sign]
        a, b = (max(a, first), b if last is None else min(b, last))
        return split(a, b, self.lat_cuts()) if a < b else []

    def shift(self, axis, sign, first):
        used = np.flatnonzero(self.flag[axis][first : first + STEP] == sign) + first
        if not len(used):
            return None
        base = 0
        for a, b in self.seg[axis, sign]:
            if a <= used[0] < b:
                at = base + first - a
                assert used[-1] < b and 0 <= at <= self.rows(axis, sign) - STEP
                return base - a
            base += b - a
        raise ValueError("no segment")

    def blocks(self):
        cuts = self.lat_cuts()
        return [(a, b, *rest) for first, last, *rest in self.regions() for a, b in split(first, last, cuts)]

    def regions(self):
        out = []
        for r in range(0, self.comps, STEP):
            sign = {}
            for axis in "xy":
                part = self.flag[axis][r : r + STEP]
                sign[axis] = 1 if part.all() else (0 if part.any() else -1)
            shifts = {(axis, s): self.shift(axis, s, r) for axis in "xy" for s in (True, False)}
            if out and sign["x"] and sign["y"] and out[-1][2:] == [sign["x"], sign["y"], shifts]:
                out[-1][1] = r + STEP
            else:
                out.append([r, r + STEP, sign["x"], sign["y"], shifts])
        return out


def split(first, last, cuts=(), most=BLOCK):
    out = []
    edges = [first] + sorted(c for c in cuts if first < c < last) + [last]
    for start, stop in zip(edges[:-1], edges[1:]):
        chunks = (stop - start) // STEP
        count = -(-chunks * STEP // most)
        at = [start + chunks * n // count * STEP for n in range(count + 1)]
        out += list(zip(at[:-1], at[1:]))
    return out


def lanes_of(rows):
    return lax.broadcasted_iota(jnp.int32, (rows, LANES), 1)


def picked(flag, first):
    row = lax.broadcasted_iota(jnp.int32, (STEP, LANES), 0)
    part = flag[first : first + STEP]
    out, n = (None, 0)
    while n < STEP:
        if not part[n]:
            n += 1
            continue
        m = n
        while m < STEP and part[m]:
            m += 1
        here = (row >= n) & (row < m)
        out = here if out is None else out | here
        n = m
    return out


def upwind(plan, axis, sign, first, from_plus, from_minus):
    if sign > 0:
        return from_plus()
    if sign < 0:
        return from_minus()
    plus, minus = (from_plus(), from_minus())
    where = picked(plan.flag[axis], first)
    zero = jnp.zeros((STEP, LANES), F32)
    if plus is None and minus is None:
        return None
    return jnp.where(where, zero if plus is None else plus, zero if minus is None else minus)


def columns_kernel(coef, bulk_weight, columns, rows):
    rows[...] = jnp.zeros_like(rows)
    rows[3 : 3 + BULK, : bulk_weight.shape[1]] = bulk_weight[...]
    for at in range(0, rows.shape[1], LANES):
        count = min(LANES, columns.shape[0] - at)
        turned = rows[:, at : at + LANES].T
        columns[at : at + count, :] = coef[at : at + count, :] + turned[:count, :]


def columns_of(plan, bulk_weight):
    comps = plan.comps
    coef = np.zeros((comps, 3 + BULK), np.float32)
    coef[:, :3] = plan.coef
    return pl.pallas_call(
        columns_kernel,
        out_shape=jax.ShapeDtypeStruct(coef.shape, F32),
        in_specs=[VMEM] * 2,
        out_specs=VMEM,
        scratch_shapes=[pltpu.VMEM((3 + BULK, -(-comps // LANES) * LANES), F32)],
        compiler_params=PARAMS,
        cost_estimate=CHEAP,
        name="columns",
    )(jnp.asarray(coef), bulk_weight)


def pack_lon_kernel(plan, spec, mask, u, v, east, west, sides, maskv, sem):
    last_col, last_row, levels = (spec.shape[1] - 1, u.shape[1] - 8, u.shape[0])
    copies = [pltpu.make_async_copy(mask, maskv, sem.at[0])]
    for out, sign, col in ((east, True, last_col), (west, False, 0)):
        at = 0
        for a, b in plan.seg["x", sign]:
            copies.append(
                pltpu.make_async_copy(
                    spec.at[pl.ds(a, b - a), col, 0, :], out.at[pl.ds(at, b - a), :], sem.at[len(copies)]
                )
            )
            at += b - a
    for f, field in enumerate((u, v)):
        for side, row in enumerate((last_row, 0)):
            copies.append(
                pltpu.make_async_copy(field.at[:, pl.ds(row, 8), :], sides.at[f, side], sem.at[len(copies)])
            )
    for c in copies:
        c.start()
    for c in copies:
        c.wait()
    for side, (out, sign, col) in enumerate(((east, True, last_col), (west, False, 0))):
        at = plan.rows("x", sign)
        out[:at, :] = out[:at, :] * maskv[col : col + 1, :].astype(F32)
        for f in range(2):
            for m in range(u.shape[2] // LANES):
                out[at : at + levels, :] = sides[f, side, :, 7 - 7 * side, m * LANES : (m + 1) * LANES]
                at += levels


def pack_lon(plan, spec4, mask, u, v):
    extra = 2 * u.shape[0] * u.shape[2] // LANES
    segments = sum(len(plan.seg["x", s]) for s in (True, False))
    return pl.pallas_call(
        functools.partial(pack_lon_kernel, plan),
        out_shape=[jax.ShapeDtypeStruct((plan.rows("x", s) + extra, LANES), F32) for s in (True, False)],
        in_specs=[HBM] * 4,
        out_specs=[VMEM, VMEM],
        scratch_shapes=[
            pltpu.VMEM((2, 2, u.shape[0], 8, u.shape[2]), F32),
            pltpu.VMEM(mask.shape, mask.dtype),
            pltpu.SemaphoreType.DMA((segments + 5,)),
        ],
        compiler_params=PARAMS,
        name="pack_lon",
    )(*pinned(spec4, mask, u, v))


def to_lane(acc, column, source, lane, lanes):
    return jnp.where(lanes == lane, pltpu.roll(column, (lane - source) % LANES, 1), acc)


def pack_lat_kernel(plan, spec_hbm, mask, u_hbm, v_hbm, after, odd, even, spec, u, v, maskv, both, sem):
    del after
    north, south = (both.at[parity()], both.at[1 - parity()])
    width_x = mask.shape[0]
    levels, ocean_x, ocean_y = u.shape
    last = ocean_y - LANES
    first = pltpu.make_async_copy(mask, maskv, sem.at[0])
    first.start()
    cuts = [a for a, _ in split(0, plan.comps)] + [plan.comps]
    parts = []
    for n in range(len(cuts) - 1):
        rows = pl.ds(cuts[n] * width_x, (cuts[n + 1] - cuts[n]) * width_x)
        parts.append(pltpu.make_async_copy(spec_hbm.at[rows, :], spec.at[rows, :], sem.at[3 + n]))
        parts[-1].start()
    fields = [pltpu.make_async_copy(x, y, sem.at[1 + n]) for n, (x, y) in enumerate(((u_hbm, u), (v_hbm, v)))]
    for c in fields:
        c.start()
    first.wait()
    maskf = maskv[...].astype(F32)
    here = 0
    for out, source, sign in ((north, LANES - 1, True), (south, 0, False)):
        for a, b in plan.lat_blocks(sign):
            while cuts[here] < b:
                parts[here].wait()
                here += 1
            rows, lane = plan.lat_place(sign, a, b, width_x)
            acc = out[rows, :] if lane else jnp.zeros((b - a, LANES), F32)
            for i in range(width_x):
                x = spec[pl.ds(a * width_x + i, b - a, stride=width_x), :] * maskf[i : i + 1, :]
                acc = to_lane(acc, x, source, lane + i, lanes_of(b - a))
            out[rows, :] = acc
    assert here == len(parts)
    for c in fields:
        c.wait()
    for out, source, sign, m in ((north, LANES - 1, True, last), (south, 0, False, 0)):
        at = plan.lat_rows(sign)
        acc = jnp.zeros((ocean_x, LANES), F32)
        for f in range(2 * levels):
            field = (u, v)[f // levels]
            acc = to_lane(acc, field[f % levels, :, m : m + LANES], source, f, lanes_of(ocean_x))
        out[at : at + ocean_x, :] = acc
    odd[...] = both[0]
    even[...] = both[1]


def pack_lat(plan, spec2, mask, u, v, after):
    assert plan.lat_rows(True) == plan.lat_rows(False)
    shape = (plan.lat_rows(True) + u.shape[1], LANES)
    return pl.pallas_call(
        functools.partial(pack_lat_kernel, plan),
        out_shape=[jax.ShapeDtypeStruct(shape, F32)] * 2 + [pltpu.VMEM(spec2.shape, F32)],
        in_specs=[HBM] * 4 + [ANY],
        out_specs=[VMEM] * 3,
        cost_estimate=CHEAP,
        scratch_shapes=[pltpu.VMEM(x.shape, F32) for x in (u, v)]
        + [
            pltpu.VMEM(mask.shape, mask.dtype),
            pltpu.VMEM((2, *shape), F32),
            pltpu.SemaphoreType.DMA((3 + len(split(0, plan.comps)),)),
        ],
        compiler_params=PARAMS,
        name="pack_lat",
    )(*pinned(spec2, mask, u, v), after)


def advect_kernel(plan, step, state, coefs, more, part):
    width = part.shape[0]
    if step == 0:
        maskf = more[...].astype(F32)

    def column(i, first, last):
        if step == 0:
            return state[pl.ds(first * width + i, last - first, stride=width), :] * maskf[i : i + 1, :]
        if i in (0, width - 1):
            return more[min(i, 1), first:last, :]
        return state[i - 1, first:last, :]

    for first, last, xs, ys, _ in plan.blocks():
        count = last - first
        keep, east, up = (jnp.broadcast_to(coefs[first:last, q : q + 1], (count, LANES)) for q in range(3))
        lanes = lanes_of(count)
        x = [column(i, first, last) for i in range(width)]
        for i in range(width):
            lat = upwind(
                plan, "y", ys, first,
                lambda: jnp.where(lanes == 0, 0.0, pltpu.roll(x[i], 1, 1)),
                lambda: jnp.where(lanes == LANES - 1, 0.0, pltpu.roll(x[i], LANES - 1, 1)),
            )
            lon = upwind(
                plan, "x", xs, first,
                lambda: x[i - 1] if i else None,
                lambda: x[i + 1] if i + 1 < width else None,
            )
            a = keep * x[i] + up * lat
            if lon is not None:
                a = a + east * lon
            part[i, first:last, :] = a


def advect(plan, step, state, coefs, more):
    comps, width = (plan.comps, state.shape[0] // plan.comps if step == 0 else state.shape[0] + 2)
    return pl.pallas_call(
        functools.partial(advect_kernel, plan, step),
        out_shape=jax.ShapeDtypeStruct((width, comps, LANES), F32),
        in_specs=[VMEM] * 3,
        out_specs=VMEM,
        compiler_params=PARAMS,
        cost_estimate=CHEAP,
        name="advect",
    )(kept(state), coefs, more)


def block_rows(comps):
    return max(b for b in range(STEP, 449, STEP) if comps % b == 0)


def source_blocks(transfer, moved, comps, body):
    block = block_rows(comps)

    for n in range(comps // block):
        rows = slice(n * block, (n + 1) * block)
        body(n, rows, jnp.dot(transfer[rows, :], moved[...], preferred_element_type=F32))


def add_bulk(coefs, weights, rows, state, total):
    count = rows.stop - rows.start
    for q in range(BULK):
        if coefs is None:
            w = weights[q, rows, :]
        else:
            w = jnp.broadcast_to(coefs[rows, 3 + q : 4 + q], (count, LANES))
            weights[q, rows, :] = w
        for i in range(state.shape[0]):
            part = (w * state[i, rows, :]).reshape(count // 8, 8, LANES).sum(0)
            total[q, i] = total[q, i] + part


def interior_kernel(plan, step, *refs):
    part, from_odd, from_even, transfer, coefs, mask = refs[:6]
    if step == 0:
        inner, edge, up, down = refs[6:10]
        full, moved, both = refs[10:]
    else:
        out, edge, bulk, weights = refs[6:10]
        inner, full, moved, both, total, sem = refs[10:]
        total[...] = jnp.zeros_like(total)
    width = part.shape[0]
    maskf = mask[...].astype(F32)
    both[0] = from_odd[: both.shape[1], :]
    both[1] = from_even[: both.shape[1], :]
    north, south = (both.at[parity()], both.at[1 - parity()])
    for first, last, _, ys, shifts in plan.blocks():
        rows, count = (slice(first, last), last - first)
        lanes = lanes_of(count)
        speed = jnp.broadcast_to(coefs[rows, 2:3], (count, LANES))
        halos = []
        for sign, buffer, lane in ((True, south, 0), (False, north, LANES - 1)):
            if shifts["y", sign] is not None:
                at, base = plan.lat_place(sign, first, last, width)
                here = lanes == lane
                if ys == 0:
                    here = here & picked(plan.flag["y"] == sign, first)
                halos.append((buffer[at, :] * speed, here, lane, base))
        for i in range(width):
            a = part[i, rows, :]
            for halo, here, lane, base in halos:
                a = a + jnp.where(here, pltpu.roll(halo, (lane - base - i) % LANES, 1), 0.0)
            if i in (0, width - 1):
                edge[min(i, 1), rows, :] = a
            else:
                full[i - 1, rows, :] = a
                moved[rows, (i - 1) * LANES : i * LANES] = a.astype(jnp.bfloat16)
    copies = []

    def done(n, rows, added):
        span = pl.ds(rows.start, rows.stop - rows.start)
        for i in range(1, width - 1):
            s = maskf[i : i + 1, :] * (full[i - 1, rows, :] + 0.5 * added[:, (i - 1) * LANES : i * LANES])
            inner[i - 1, rows, :] = s
            if step:
                to = out.at[span, i, 0, :]
                copies.append(pltpu.make_async_copy(inner.at[i - 1, span, :], to, sem.at[len(copies)]))
                copies[-1].start()
        if step:
            add_bulk(coefs, weights, rows, inner, total)
            return
        for packed, source, sign in ((up, LANES - 1, True), (down, 0, False)):
            for a, b in plan.lat_blocks(sign, rows.start, rows.stop):
                at, base = plan.lat_place(sign, a, b, width)
                acc = packed[at, :] if base else jnp.zeros((b - a, LANES), F32)
                for i in range(1, width - 1):
                    acc = to_lane(acc, inner[i - 1, a:b, :], source, base + i, lanes_of(b - a))
                packed[at, :] = acc

    source_blocks(transfer, moved, plan.comps, done)
    if step:
        for q in range(BULK):
            for i in range(1, width - 1):
                bulk[q, i : i + 1, :] = total[q, i - 1].sum(0, keepdims=True)
            bulk[q, 0:1, :] = jnp.zeros((1, LANES), F32)
            bulk[q, width - 1 : width, :] = jnp.zeros((1, LANES), F32)
    for c in copies:
        c.wait()


def interior(plan, step, part, from_odd, from_even, transfer, coefs, mask):
    comps, width = (plan.comps, mask.shape[0])
    middle = (width - 2, comps, LANES)
    edge = jax.ShapeDtypeStruct((2, comps, LANES), F32)
    scratch = [
        pltpu.VMEM(middle, F32),
        pltpu.VMEM((comps, (width - 2) * LANES), jnp.bfloat16),
        pltpu.VMEM((2, plan.lat_rows(True), LANES), F32),
    ]
    if step == 0:
        outs = [pltpu.VMEM(middle, F32), edge]
        outs += [jax.ShapeDtypeStruct((plan.lat_rows(s), LANES), F32) for s in (True, False)]
    else:
        outs = [pltpu.HBM((comps, width, 1, LANES), F32), edge, jax.ShapeDtypeStruct((BULK, width, LANES), F32)]
        outs += [jax.ShapeDtypeStruct((BULK, comps, LANES), F32)]
        scratch = [pltpu.VMEM(middle, F32)] + scratch + [pltpu.VMEM((BULK, width - 2, 8, LANES), F32)]
        scratch += [pltpu.SemaphoreType.DMA(((width - 2) * comps // block_rows(comps),))]
    return pl.pallas_call(
        functools.partial(interior_kernel, plan, step),
        out_shape=outs,
        in_specs=[VMEM] * 6,
        out_specs=[HBM if step else VMEM] + [VMEM] * (len(outs) - 1),
        scratch_shapes=scratch,
        compiler_params=PARAMS,
        cost_estimate=CHEAP,
        name="interior",
    )(part, from_odd, from_even, transfer, coefs, mask)


def edges_kernel(plan, step, *refs):
    refs = list(refs)
    part, from_west, from_east, transfer, coefs, mask = refs[:6]
    if step == 0:
        state, east, west = refs[6:9]
        full, moved = refs[9:]
    else:
        bulk_in, weights = refs[6:8]
        state, bulk = refs[8:10]
        full, moved, total = refs[10:]
    width = mask.shape[0]
    maskf = jnp.concatenate([mask[0:1, :], mask[width - 1 : width, :]], axis=0).astype(F32)

    for first, last, xs, ys, shifts in plan.blocks():
        rows, count = (slice(first, last), last - first)
        speed = jnp.broadcast_to(coefs[rows, 1:2], (count, LANES))
        for side, sign, buffer in ((0, True, from_west), (1, False, from_east)):
            a = part[side, rows, :]
            shift = shifts["x", sign]
            if shift is not None:
                halo = buffer[first + shift : last + shift, :]
                if xs == 0:
                    halo = jnp.where(picked(plan.flag["x"] == sign, first), halo, 0.0)
                a = a + speed * halo
            full[side, rows, :] = a
            moved[rows, side * LANES : (side + 1) * LANES] = a.astype(jnp.bfloat16)
    if step:
        total[...] = jnp.zeros_like(total)

    def done(n, rows, added):
        for side in range(2):
            s = maskf[side : side + 1, :] * (full[side, rows, :] + 0.5 * added[:, side * LANES : (side + 1) * LANES])
            state[side, rows, :] = s
        if step:
            add_bulk(None, weights, rows, state, total)

    source_blocks(transfer, moved, plan.comps, done)
    if step:
        for q in range(BULK):
            bulk[q] = bulk_in[q]
            bulk[q, 0:1, :] = total[q, 0].sum(0, keepdims=True)
            bulk[q, width - 1 : width, :] = total[q, 1].sum(0, keepdims=True)
        return
    for out, side, sign in ((east, 1, True), (west, 0, False)):
        at = 0
        for a, b in plan.seg["x", sign]:
            out[at : at + b - a, :] = state[side, a:b, :]
            at += b - a


def merge_lat_kernel(plan, width, state, up_in, down_in, odd, even, both):
    up, down = (both.at[parity()], both.at[1 - parity()])
    for out, given, source, sign in ((up, up_in, LANES - 1, True), (down, down_in, 0, False)):
        for a, b in plan.lat_blocks(sign):
            at, base = plan.lat_place(sign, a, b, width)
            acc = out[at, :] if base else given[at, :]
            for side, lane in ((0, base), (1, base + width - 1)):
                acc = to_lane(acc, state[side, a:b, :], source, lane, lanes_of(b - a))
            out[at, :] = acc
    odd[...] = both[0]
    even[...] = both[1]


def merge_lat(plan, width, state, up, down):
    return pl.pallas_call(
        functools.partial(merge_lat_kernel, plan, width),
        out_shape=[jax.ShapeDtypeStruct(x.shape, F32) for x in (up, down)],
        in_specs=[VMEM] * 3,
        out_specs=[VMEM] * 2,
        scratch_shapes=[pltpu.VMEM((2, *up.shape), F32)],
        compiler_params=PARAMS,
        cost_estimate=CHEAP,
        name="merge_lat",
    )(state, up, down)


def edges(plan, step, part, from_west, from_east, transfer, coefs, mask, *more):
    comps, width = (plan.comps, mask.shape[0])
    outs = [jax.ShapeDtypeStruct((2, comps, LANES), F32)]
    scratch = [pltpu.VMEM((2, comps, LANES), F32), pltpu.VMEM((comps, 2 * LANES), jnp.bfloat16)]
    if step == 0:
        outs += [jax.ShapeDtypeStruct((plan.rows("x", s), LANES), F32) for s in (True, False)]
    else:
        outs += [jax.ShapeDtypeStruct((BULK, width, LANES), F32)]
        scratch += [pltpu.VMEM((BULK, 2, 8, LANES), F32)]
    return pl.pallas_call(
        functools.partial(edges_kernel, plan, step),
        out_shape=outs,
        in_specs=[VMEM] * (6 + len(more)),
        out_specs=[VMEM] * len(outs),
        scratch_shapes=scratch,
        compiler_params=PARAMS,
        cost_estimate=CHEAP,
        name="edges",
    )(part, from_west, from_east, transfer, coefs, mask, *more)


def finish_kernel(state, given, out, sem):
    width = out.shape[1]
    copies = [
        pltpu.make_async_copy(state.at[side], out.at[:, col, 0, :], sem.at[side])
        for side, col in ((0, 0), (1, width - 1))
    ]
    for c in copies:
        c.start()
    for c in copies:
        c.wait()


def finish(state, out4):
    return pl.pallas_call(
        finish_kernel,
        out_shape=jax.ShapeDtypeStruct(out4.shape, F32),
        in_specs=[ANY, ANY],
        out_specs=ANY,
        scratch_shapes=[pltpu.SemaphoreType.DMA((2,))],
        input_output_aliases={1: 0},
        compiler_params=PARAMS,
        cost_estimate=CHEAP,
        name="finish",
    )(state, out4)


def ocean_shifts(q, west, east, south, north):
    rows, lanes = q.shape
    row = lax.broadcasted_iota(jnp.int32, q.shape, 0)
    lane = lax.broadcasted_iota(jnp.int32, q.shape, 1)
    before = jnp.where(row == 0, west, pltpu.roll(q, 1, 0))
    after = jnp.where(row == rows - 1, east, pltpu.roll(q, rows - 1, 0))
    below = jnp.where(lane == 0, south, pltpu.roll(q, 1, 1))
    above = jnp.where(lane == lanes - 1, north, pltpu.roll(q, lanes - 1, 1))
    return before, after, below, above


def ocean_base_kernel(plan, u, v, from_west, from_east, from_odd, from_even, mask, coriolis, base_u, base_v, both):
    levels, ocean_x, ocean_y = u.shape
    start = plan.lat_rows(True)
    both[0] = from_odd[start : start + ocean_x, :]
    both[1] = from_even[start : start + ocean_x, :]
    from_north, from_south = (both.at[parity()], both.at[1 - parity()])
    tiles = ocean_y // LANES
    maskf = mask[...].astype(F32)
    half = 0.5 * coriolis[...]
    west_at, east_at = (plan.rows("x", s) for s in (True, False))
    for f, (field, other, out, sign) in enumerate(((u, v, base_u, 1.0), (v, u, base_v, -1.0))):
        for level in range(levels):
            q = field[level]

            def line(buffer, at):
                parts = [buffer[at + (f * tiles + m) * levels + level, :][None, :] for m in range(tiles)]
                return jnp.concatenate(parts, axis=1)

            lane = f * levels + level
            before, after, below, above = ocean_shifts(
                q,
                line(from_west, west_at),
                line(from_east, east_at),
                from_south[:, lane : lane + 1],
                from_north[:, lane : lane + 1],
            )
            lap = before + after + below + above - 4.0 * q
            out[level] = maskf * (q + sign * half * other[level] + 0.1 * lap)


def ocean_base(plan, u, v, from_west, from_east, from_odd, from_even, mask, coriolis):
    return pl.pallas_call(
        functools.partial(ocean_base_kernel, plan),
        out_shape=[jax.ShapeDtypeStruct(u.shape, F32)] * 2,
        in_specs=[VMEM] * 8,
        out_specs=[VMEM] * 2,
        scratch_shapes=[pltpu.VMEM((2, u.shape[1], LANES), F32)],
        cost_estimate=CHEAP,
        compiler_params=PARAMS,
        name="ocean_base",
    )(u, v, from_west, from_east, from_odd, from_even, mask, coriolis)


def gathered(slabs, at, off, weight, count, acc=None, offsets=range(OFFSETS)):
    acc = [0.0] * count if acc is None else acc
    for o in offsets:
        rows = [slabs(o, q) for q in range(count)]
        for p in range(len(at)):
            w = jnp.where(off[p] == o, weight[p], 0.0)
            for q in range(count):
                acc[q] = acc[q] + w * jnp.take_along_axis(rows[q], at[p], axis=1, mode="promise_in_bounds")
    return acc


def fill_table(table, left, own, right, ratio, fields):
    width = table.shape[1] // (3 * ratio)
    for q in fields:
        for b, ref in enumerate((left, own, right)):
            for r in range(ratio):
                rows = pl.ds(b * width * ratio + r, width, stride=ratio)
                table[q, rows, :] = jnp.zeros((width, LANES), F32) if ref is None else ref[q]


def remap_lon_kernel(own, left, right, cell, offset, weight, *refs):
    east, west, rows = refs[-3:]
    taps, ocean_x, ocean_y = cell.shape
    width = own.shape[1]
    tiles = ocean_y // LANES
    last_row = ocean_x - 8
    for b, ref in enumerate((left, own, right)):
        rows[:, b * width : (b + 1) * width, :] = ref[0:2]
    first_half = lax.broadcasted_iota(jnp.int32, (8, LANES), 0) < 4
    for m in range(tiles):
        lanes = slice(m * LANES, (m + 1) * LANES)
        at, off, w = (
            [jnp.where(first_half, x[p, 0:8, lanes], x[p, last_row : last_row + 8, lanes]) for p in range(taps)]
            for x in (cell, offset, weight)
        )
        acc = gathered(lambda o, q: rows[q, o : o + 8, :], at, off, w, 2)
        for q in range(2):
            n = q * tiles + m
            east[n : n + 1, :] = acc[q][7:8, :]
            west[n : n + 1, :] = acc[q][0:1, :]
    if 2 * tiles < east.shape[0]:
        for out in (east, west):
            out[2 * tiles :, :] = jnp.zeros((out.shape[0] - 2 * tiles, LANES), F32)


def remap_lat_kernel(own, left, right, cell, offset, weight, after, odd, even, table, both):
    del after
    north, south = (both.at[parity()], both.at[1 - parity()])
    taps, ocean_x, ocean_y = cell.shape
    ratio = ocean_x // own.shape[1]
    last_lane = ocean_y - LANES
    fill_table(table, left, own, right, ratio, range(1, 3))
    lanes = lanes_of(8)
    for t in range(ocean_x // 8):
        here = slice(8 * t, 8 * t + 8)
        at, off, w = (
            [jnp.where(lanes < LANES // 2, x[p, here, 0:LANES], x[p, here, last_lane:]) for p in range(taps)]
            for x in (cell, offset, weight)
        )
        acc = gathered(lambda o, q: table[1 + q, 8 * t + ratio * o : 8 * t + ratio * o + 8, :], at, off, w, 2)
        for out, source in ((north, LANES - 1), (south, 0)):
            packed = jnp.zeros((8, LANES), F32)
            for q in range(2):
                packed = to_lane(packed, acc[q], source, q, lanes)
            out[here, :] = packed
    odd[...] = both[0]
    even[...] = both[1]


def remap_lon(own, left, right, cell, offset, weight, *after):
    _, ocean_x, ocean_y = cell.shape
    width = own.shape[1]
    assert width == 8 and ocean_x % width == 0
    side = jax.ShapeDtypeStruct((max(ocean_x + 8, 8 * pl.cdiv(2 * ocean_y // LANES, 8)), LANES), F32)
    return pl.pallas_call(
        remap_lon_kernel,
        out_shape=[side, side],
        in_specs=[VMEM] * 6 + [ANY] * len(after),
        out_specs=[VMEM] * 2,
        scratch_shapes=[pltpu.VMEM((2, 3 * width, LANES), F32)],
        compiler_params=PARAMS,
        cost_estimate=CHEAP,
        name="remap_lon",
    )(own, left, right, cell, offset, weight, *after)


def remap_lat(own, left, right, cell, offset, weight, after):
    ocean_x = cell.shape[1]
    end = jax.ShapeDtypeStruct((ocean_x, LANES), F32)
    return pl.pallas_call(
        remap_lat_kernel,
        out_shape=[end, end],
        in_specs=[VMEM] * 6 + [ANY],
        out_specs=[VMEM] * 2,
        scratch_shapes=[pltpu.VMEM((BULK, 3 * ocean_x, LANES), F32), pltpu.VMEM((2, ocean_x, LANES), F32)],
        compiler_params=PARAMS,
        cost_estimate=CHEAP,
        name="remap_lat",
    )(own, left, right, cell, offset, weight, after)


def remap_kernel(mine, *refs):
    if mine:
        own, cell, offset, weight, forcing, table = refs
        left = right = None
    else:
        left, right, cell, offset, weight, begun, forcing, table = refs
        own = None
    taps, ocean_x, ocean_y = cell.shape
    ratio = table.shape[1] // ocean_x
    width = ocean_x // ratio
    fill_table(table, left, own, right, ratio, range(BULK))
    for t in range(ocean_x // 8):
        used = []
        for o in range(OFFSETS):
            inside = [0 <= i // ratio + o - width < width for i in range(8 * t, 8 * t + 8)]
            if any(inside) if mine else not all(inside):
                used.append(o)
        for m in range(ocean_y // LANES):
            rows, lanes = (slice(8 * t, 8 * t + 8), slice(m * LANES, (m + 1) * LANES))
            at, off, w = ([x[p, rows, lanes] for p in range(taps)] for x in (cell, offset, weight))
            acc = gathered(
                lambda o, q: table[q, 8 * t + ratio * o : 8 * t + ratio * o + 8, :],
                at, off, w, BULK,
                None if mine else [begun[q, rows, lanes] for q in range(BULK)],
                used,
            )
            for q in range(BULK):
                forcing[q, rows, lanes] = acc[q]


def remap(mine, *args):
    cell = args[1] if mine else args[2]
    _, ocean_x, ocean_y = cell.shape
    return pl.pallas_call(
        functools.partial(remap_kernel, mine),
        out_shape=jax.ShapeDtypeStruct((BULK, ocean_x, ocean_y), F32),
        in_specs=[VMEM] * len(args),
        out_specs=VMEM,
        scratch_shapes=[pltpu.VMEM((BULK, 3 * ocean_x, LANES), F32)],
        compiler_params=PARAMS,
        cost_estimate=CHEAP,
        name="remap_own" if mine else "remap_rest",
    )(*args)


def ocean_final_kernel(
    forcing, from_west, from_east, from_odd, from_even, base_u, base_v, mask, coriolis, new_u, new_v, both
):
    levels, ocean_x, ocean_y = base_u.shape
    both[0] = from_odd[...]
    both[1] = from_even[...]
    from_north, from_south = (both.at[parity()], both.at[1 - parity()])
    tiles = ocean_y // LANES

    def line(buffer, q):
        return jnp.concatenate([buffer[q * tiles + m : q * tiles + m + 1, :] for m in range(tiles)], axis=1)

    zero_line = jnp.zeros((1, ocean_y), F32)
    zero_end = jnp.zeros((ocean_x, 1), F32)
    grad = []
    for q in range(3):
        lon = q < 2
        lat = q > 0
        before, after, below, above = ocean_shifts(
            forcing[q],
            line(from_west, q) if lon else zero_line,
            line(from_east, q) if lon else zero_line,
            from_south[:, q - 1 : q] if lat else zero_end,
            from_north[:, q - 1 : q] if lat else zero_end,
        )
        grad.append((0.5 * (after - before), 0.5 * (above - below)))
    force_x = -(grad[0][0] + grad[1][1])
    force_y = -(grad[1][0] + grad[2][1])
    maskf = mask[...].astype(F32)
    half = 0.5 * coriolis[...]
    add_u = maskf * (half * forcing[4] + 0.5 * force_x)
    add_v = maskf * (0.5 * force_y - half * forcing[3])
    for level in range(levels):
        decay = np.float32(np.exp(np.float32(-level / 3.0)))
        new_u[level] = base_u[level] + decay * add_u
        new_v[level] = base_v[level] + decay * add_v


def ocean_final(forcing, halos, base_u, base_v, mask, coriolis):
    return pl.pallas_call(
        ocean_final_kernel,
        out_shape=[jax.ShapeDtypeStruct(base_u.shape, F32)] * 2,
        in_specs=[VMEM] * 9,
        out_specs=[VMEM] * 2,
        scratch_shapes=[pltpu.VMEM((2, base_u.shape[1], LANES), F32)],
        compiler_params=PARAMS,
        cost_estimate=CHEAP,
        name="ocean_final",
    )(forcing, *halos, base_u, base_v, mask, coriolis)


def shifted(value, axis, step):
    count = lax.axis_size(axis)
    return lax.ppermute(value, axis, [(i, (i + step) % count) for i in range(count)])


def swapped(value, axis, first):
    count = lax.axis_size(axis)
    pairs = [(i, i + 1) for i in range(first, count - 1, 2)]
    return lax.ppermute(value, axis, pairs + [(j, i) for i, j in pairs])


def exchange(east, west, odd, even):
    from_odd = swapped(odd, "lat", 0)
    from_even = swapped(even, "lat", 1)
    from_west = shifted(east, "lon", 1)
    from_east = shifted(west, "lon", -1)
    return from_west, from_east, from_odd, from_even


def local(
    spectrum,
    sea_mask,
    transfer,
    bulk_weight,
    remap_cell,
    remap_weight,
    ocean_u,
    ocean_v,
    ocean_mask,
    coriolis,
):
    comps, width_x, width_y = spectrum.shape
    plan = Plan(comps)
    spec2 = spectrum.reshape(comps * width_x, width_y)
    east, west = pack_lon(plan, spectrum.reshape(comps, width_x, 1, width_y), sea_mask, ocean_u, ocean_v)
    odd, even, spec2 = pack_lat(plan, spec2, sea_mask, ocean_u, ocean_v, east)
    begun = exchange(east, west, odd, even)

    coefs = columns_of(plan, bulk_weight)
    total_y = width_y * lax.axis_size("lat")
    taps_first = remap_cell.transpose(2, 0, 1)
    offset = taps_first // total_y
    cell = taps_first % width_y
    weight = remap_weight.transpose(2, 0, 1)
    line = coriolis[None, :]

    part = advect(plan, 0, spec2, coefs, sea_mask)
    middle, edge, up, down = interior(plan, 0, part, *begun[2:], transfer, coefs, sea_mask)
    sides, east, west = edges(plan, 0, edge, *begun[:2], transfer, coefs, sea_mask)
    halos = exchange(east, west, *merge_lat(plan, width_x, sides, up, down))

    part = advect(plan, 1, middle, coefs, sides)
    out4, edge, bulk, weights = interior(plan, 1, part, *halos[2:], transfer, coefs, sea_mask)
    sides, bulk = edges(plan, 1, edge, *halos[:2], transfer, coefs, sea_mask, bulk, weights)
    left = shifted(bulk, "lon", 1)
    right = shifted(bulk, "lon", -1)
    state4 = finish(sides, out4)
    state = state4.reshape(spectrum.shape)
    base_u, base_v = ocean_base(plan, ocean_u, ocean_v, *begun, ocean_mask, line)
    forcing = remap(True, bulk, cell, offset, weight)

    remapped = (bulk, left, right, cell, offset, weight)
    east, west = remap_lon(*remapped, forcing, base_u, *pinned(state4))
    odd, even = remap_lat(*remapped, east)
    halos = exchange(east, west, odd, even)
    forcing = remap(False, left, right, cell, offset, weight, forcing)
    new_u, new_v = ocean_final(forcing, halos, base_u, base_v, ocean_mask, line)
    return (state, new_u, new_v)


def solution(mesh):
    placed = (
        P(None, "lon", "lat"),
        P("lon", "lat"),
        P(),
        P(),
        P("lon", "lat", None),
        P("lon", "lat", None),
        P(None, "lon", "lat"),
        P(None, "lon", "lat"),
        P("lon", "lat"),
        P("lat"),
    )
    return jax.shard_map(
        local,
        mesh=mesh,
        in_specs=placed,
        out_specs=(P(None, "lon", "lat"), P(None, "lon", "lat"), P(None, "lon", "lat")),
        check_vma=False,
    )
```

```python
import functools

import jax
import jax.numpy as jnp
import numpy as np
from jax import lax
from jax.experimental import pallas as pl
from jax.experimental.pallas import tpu as pltpu
from jax.sharding import PartitionSpec as P

NFREQ = 36
STEP = 16
LANES = 128
BULK = 5
GROUPS = 4
OFFSETS = 17
BLOCK = 80
F32 = jnp.float32
VMEM = pl.BlockSpec(memory_space=pltpu.VMEM)
ANY = pl.BlockSpec(memory_space=pl.ANY)
HBM = pl.BlockSpec(memory_space=pltpu.HBM)
PARAMS = pltpu.CompilerParams(vmem_limit_bytes=24 << 20)
CHEAP = pl.CostEstimate(flops=1, bytes_accessed=1, transcendentals=0)


def pinned(*arrays):
    return [pltpu.with_memory_space_constraint(x, pltpu.HBM) for x in arrays]


def kept(array):
    return pltpu.with_memory_space_constraint(array, pltpu.VMEM)


def parity(axis):
    return lax.rem(lax.axis_index(axis), 2)


def sides_of(both, axis):
    return both.at[1 - parity(axis)], both.at[parity(axis)]


class Plan:
    def __init__(self, comps):
        dirs = comps // NFREQ
        k = np.arange(comps)
        theta = 2.0 * np.pi * ((k // NFREQ) + 0.5) / dirs
        speed = 1.1 ** (-(k % NFREQ).astype(np.float64))
        cx = 0.45 * speed * np.cos(theta)
        cy = 0.45 * speed * np.sin(theta)
        self.comps = comps
        self.coef = np.stack([1.0 - np.abs(cx) - np.abs(cy), np.abs(cx), np.abs(cy)], 1).astype(np.float32)
        self.flag = {"x": cx > 0, "y": cy > 0}
        self.seg = {}
        for axis, step in (("x", 8), ("y", STEP)):
            for sign in (True, False):
                self.seg[axis, sign] = self.runs(self.flag[axis] == sign, step)

    def runs(self, flag, step):
        out = []
        for n in np.flatnonzero(flag.reshape(-1, step).any(1)):
            if out and out[-1][1] == n * step:
                out[-1][1] = int(n + 1) * step
            else:
                out.append([int(n) * step, int(n + 1) * step])
        return [(a, b) for a, b in out]

    def rows(self, axis, sign):
        return sum(b - a for a, b in self.seg[axis, sign])

    def lat_rows(self, sign):
        ((a, b),) = self.seg["y", sign]
        return -(-(b - a) // (GROUPS * STEP)) * STEP

    def lat_cuts(self):
        cuts = set()
        for sign in (True, False):
            ((a, b),) = self.seg["y", sign]
            cuts |= set(range(a, b, self.lat_rows(sign))) | {b}
        return cuts

    def lat_place(self, sign, first, last, width):
        ((a, _),) = self.seg["y", sign]
        group, row = divmod(first - a, self.lat_rows(sign))
        assert row + last - first <= self.lat_rows(sign) and (group + 1) * width <= LANES
        return slice(row, row + last - first), group * width

    def lat_blocks(self, sign, first=0, last=None):
        ((a, b),) = self.seg["y", sign]
        a, b = (max(a, first), b if last is None else min(b, last))
        return split(a, b, self.lat_cuts()) if a < b else []

    def shift(self, axis, sign, first):
        used = np.flatnonzero(self.flag[axis][first : first + STEP] == sign) + first
        if not len(used):
            return None
        base = 0
        for a, b in self.seg[axis, sign]:
            if a <= used[0] < b:
                at = base + first - a
                assert used[-1] < b and 0 <= at <= self.rows(axis, sign) - STEP
                return base - a
            base += b - a
        raise ValueError("no segment")

    def blocks(self):
        cuts = self.lat_cuts()
        return [(a, b, *rest) for first, last, *rest in self.regions() for a, b in split(first, last, cuts)]

    def regions(self):
        out = []
        for r in range(0, self.comps, STEP):
            sign = {}
            for axis in "xy":
                part = self.flag[axis][r : r + STEP]
                sign[axis] = 1 if part.all() else (0 if part.any() else -1)
            shifts = {(axis, s): self.shift(axis, s, r) for axis in "xy" for s in (True, False)}
            if out and sign["x"] and sign["y"] and out[-1][2:] == [sign["x"], sign["y"], shifts]:
                out[-1][1] = r + STEP
            else:
                out.append([r, r + STEP, sign["x"], sign["y"], shifts])
        return out


def split(first, last, cuts=(), most=BLOCK):
    out = []
    edges = [first] + sorted(c for c in cuts if first < c < last) + [last]
    for start, stop in zip(edges[:-1], edges[1:]):
        chunks = (stop - start) // STEP
        count = -(-chunks * STEP // most)
        at = [start + chunks * n // count * STEP for n in range(count + 1)]
        out += list(zip(at[:-1], at[1:]))
    return out


def lanes_of(rows):
    return lax.broadcasted_iota(jnp.int32, (rows, LANES), 1)


def picked(flag, first):
    row = lax.broadcasted_iota(jnp.int32, (STEP, LANES), 0)
    part = flag[first : first + STEP]
    out, n = (None, 0)
    while n < STEP:
        if not part[n]:
            n += 1
            continue
        m = n
        while m < STEP and part[m]:
            m += 1
        here = (row >= n) & (row < m)
        out = here if out is None else out | here
        n = m
    return out


def upwind(plan, axis, sign, first, from_plus, from_minus):
    if sign > 0:
        return from_plus()
    if sign < 0:
        return from_minus()
    plus, minus = (from_plus(), from_minus())
    where = picked(plan.flag[axis], first)
    zero = jnp.zeros((STEP, LANES), F32)
    if plus is None and minus is None:
        return None
    return jnp.where(where, zero if plus is None else plus, zero if minus is None else minus)


def columns_kernel(coef, bulk_weight, columns, rows):
    rows[...] = jnp.zeros_like(rows)
    rows[3 : 3 + BULK, : bulk_weight.shape[1]] = bulk_weight[...]
    for at in range(0, rows.shape[1], LANES):
        count = min(LANES, columns.shape[0] - at)
        turned = rows[:, at : at + LANES].T
        columns[at : at + count, :] = coef[at : at + count, :] + turned[:count, :]


def columns_of(plan, bulk_weight):
    comps = plan.comps
    coef = np.zeros((comps, 3 + BULK), np.float32)
    coef[:, :3] = plan.coef
    return pl.pallas_call(
        columns_kernel,
        out_shape=jax.ShapeDtypeStruct(coef.shape, F32),
        in_specs=[VMEM] * 2,
        out_specs=VMEM,
        scratch_shapes=[pltpu.VMEM((3 + BULK, -(-comps // LANES) * LANES), F32)],
        compiler_params=PARAMS,
        cost_estimate=CHEAP,
        name="columns",
    )(jnp.asarray(coef), bulk_weight)


def pack_lon_kernel(plan, spec, mask, odd, even, maskv, both, sem):
    last_col = spec.shape[1] - 1
    west, east = sides_of(both, "lon")
    copies = [pltpu.make_async_copy(mask, maskv, sem.at[0])]
    for out, sign, col in ((east, True, last_col), (west, False, 0)):
        at = 0
        for a, b in plan.seg["x", sign]:
            copies.append(
                pltpu.make_async_copy(
                    spec.at[pl.ds(a, b - a), col, 0, :], out.at[pl.ds(at, b - a), :], sem.at[len(copies)]
                )
            )
            at += b - a
    for c in copies:
        c.start()
    for c in copies:
        c.wait()
    masks = [maskv[col : col + 1, :].astype(F32) for col in (last_col, 0)]
    lower = jnp.full((1, LANES), parity("lon"), jnp.int32) == 0
    odd[...] = both[0] * jnp.where(lower, masks[0], masks[1])
    even[...] = both[1] * jnp.where(lower, masks[1], masks[0])


def pack_lon(plan, spec4, mask):
    segments = sum(len(plan.seg["x", s]) for s in (True, False))
    shape = (plan.rows("x", True), LANES)
    assert plan.rows("x", True) == plan.rows("x", False)
    return pl.pallas_call(
        functools.partial(pack_lon_kernel, plan),
        out_shape=[jax.ShapeDtypeStruct(shape, F32)] * 2,
        in_specs=[HBM] * 2,
        out_specs=[VMEM, VMEM],
        scratch_shapes=[
            pltpu.VMEM(mask.shape, mask.dtype),
            pltpu.VMEM((2, *shape), F32),
            pltpu.SemaphoreType.DMA((segments + 1,)),
        ],
        compiler_params=PARAMS,
        cost_estimate=CHEAP,
        name="pack_lon",
    )(*pinned(spec4, mask))


def to_lane(acc, column, source, lane, lanes):
    return jnp.where(lanes == lane, pltpu.roll(column, (lane - source) % LANES, 1), acc)


def pack_lat_kernel(plan, spec_hbm, mask, u_hbm, v_hbm, after, odd, even, spec, u, v, maskv, both, sem):
    del after
    south, north = sides_of(both, "lat")
    width_x = mask.shape[0]
    levels, ocean_x, ocean_y = u.shape
    last = ocean_y - LANES
    first = pltpu.make_async_copy(mask, maskv, sem.at[0])
    first.start()
    cuts = [a for a, _ in split(0, plan.comps)] + [plan.comps]
    parts = []
    for n in range(len(cuts) - 1):
        rows = pl.ds(cuts[n] * width_x, (cuts[n + 1] - cuts[n]) * width_x)
        parts.append(pltpu.make_async_copy(spec_hbm.at[rows, :], spec.at[rows, :], sem.at[3 + n]))
        parts[-1].start()
    fields = [pltpu.make_async_copy(x, y, sem.at[1 + n]) for n, (x, y) in enumerate(((u_hbm, u), (v_hbm, v)))]
    for c in fields:
        c.start()
    first.wait()
    maskf = maskv[...].astype(F32)
    here = 0
    for out, source, sign in ((north, LANES - 1, True), (south, 0, False)):
        for a, b in plan.lat_blocks(sign):
            while cuts[here] < b:
                parts[here].wait()
                here += 1
            rows, lane = plan.lat_place(sign, a, b, width_x)
            acc = out[rows, :] if lane else jnp.zeros((b - a, LANES), F32)
            for i in range(width_x):
                x = spec[pl.ds(a * width_x + i, b - a, stride=width_x), :] * maskf[i : i + 1, :]
                acc = to_lane(acc, x, source, lane + i, lanes_of(b - a))
            out[rows, :] = acc
    assert here == len(parts)
    for c in fields:
        c.wait()
    for out, source, sign, m in ((north, LANES - 1, True, last), (south, 0, False, 0)):
        at = plan.lat_rows(sign)
        acc = jnp.zeros((ocean_x, LANES), F32)
        for f in range(2 * levels):
            field = (u, v)[f // levels]
            acc = to_lane(acc, field[f % levels, :, m : m + LANES], source, f, lanes_of(ocean_x))
        out[at : at + ocean_x, :] = acc
    odd[...] = both[0]
    even[...] = both[1]


def pack_lat(plan, spec2, mask, u, v, after):
    assert plan.lat_rows(True) == plan.lat_rows(False)
    shape = (plan.lat_rows(True) + u.shape[1], LANES)
    return pl.pallas_call(
        functools.partial(pack_lat_kernel, plan),
        out_shape=[jax.ShapeDtypeStruct(shape, F32)] * 2 + [pltpu.VMEM(spec2.shape, F32)],
        in_specs=[HBM] * 4 + [ANY],
        out_specs=[VMEM] * 3,
        cost_estimate=CHEAP,
        scratch_shapes=[pltpu.VMEM(x.shape, F32) for x in (u, v)]
        + [
            pltpu.VMEM(mask.shape, mask.dtype),
            pltpu.VMEM((2, *shape), F32),
            pltpu.SemaphoreType.DMA((3 + len(split(0, plan.comps)),)),
        ],
        compiler_params=PARAMS,
        name="pack_lat",
    )(*pinned(spec2, mask, u, v), after)


def advect_kernel(plan, step, state, coefs, more, part):
    width = part.shape[0]
    if step == 0:
        maskf = more[...].astype(F32)

    def column(i, first, last):
        if step == 0:
            return state[pl.ds(first * width + i, last - first, stride=width), :] * maskf[i : i + 1, :]
        if i in (0, width - 1):
            return more[min(i, 1), first:last, :]
        return state[i - 1, first:last, :]

    for first, last, xs, ys, _ in plan.blocks():
        count = last - first
        keep, east, up = (jnp.broadcast_to(coefs[first:last, q : q + 1], (count, LANES)) for q in range(3))
        lanes = lanes_of(count)
        x = [column(i, first, last) for i in range(width)]
        for i in range(width):
            lat = upwind(
                plan, "y", ys, first,
                lambda: jnp.where(lanes == 0, 0.0, pltpu.roll(x[i], 1, 1)),
                lambda: jnp.where(lanes == LANES - 1, 0.0, pltpu.roll(x[i], LANES - 1, 1)),
            )
            lon = upwind(
                plan, "x", xs, first,
                lambda: x[i - 1] if i else None,
                lambda: x[i + 1] if i + 1 < width else None,
            )
            a = keep * x[i] + up * lat
            if lon is not None:
                a = a + east * lon
            part[i, first:last, :] = a


def advect(plan, step, state, coefs, more):
    comps, width = (plan.comps, state.shape[0] // plan.comps if step == 0 else state.shape[0] + 2)
    return pl.pallas_call(
        functools.partial(advect_kernel, plan, step),
        out_shape=jax.ShapeDtypeStruct((width, comps, LANES), F32),
        in_specs=[VMEM] * 3,
        out_specs=VMEM,
        compiler_params=PARAMS,
        cost_estimate=CHEAP,
        name="advect",
    )(kept(state), coefs, more)


def block_rows(comps):
    return max(b for b in range(STEP, 449, STEP) if comps % b == 0)


def source_blocks(transfer, moved, comps, body):
    block = block_rows(comps)

    for n in range(comps // block):
        rows = slice(n * block, (n + 1) * block)
        body(n, rows, jnp.dot(transfer[rows, :], moved[...], preferred_element_type=F32))


def add_bulk(coefs, weights, rows, state, total):
    count = rows.stop - rows.start
    for q in range(BULK):
        if coefs is None:
            w = weights[q, rows, :]
        else:
            w = jnp.broadcast_to(coefs[rows, 3 + q : 4 + q], (count, LANES))
            weights[q, rows, :] = w
        for i in range(state.shape[0]):
            part = (w * state[i, rows, :]).reshape(count // 8, 8, LANES).sum(0)
            total[q, i] = total[q, i] + part


def interior_kernel(plan, step, *refs):
    part, from_odd, from_even, transfer, coefs, mask = refs[:6]
    if step == 0:
        inner, edge, up, down = refs[6:10]
        full, moved, both = refs[10:]
    else:
        out, edge, bulk, weights = refs[6:10]
        inner, full, moved, both, total, sem = refs[10:]
        total[...] = jnp.zeros_like(total)
    width = part.shape[0]
    maskf = mask[...].astype(F32)
    both[0] = from_odd[: both.shape[1], :]
    both[1] = from_even[: both.shape[1], :]
    south, north = sides_of(both, "lat")
    for first, last, _, ys, shifts in plan.blocks():
        rows, count = (slice(first, last), last - first)
        lanes = lanes_of(count)
        speed = jnp.broadcast_to(coefs[rows, 2:3], (count, LANES))
        halos = []
        for sign, buffer, lane in ((True, south, 0), (False, north, LANES - 1)):
            if shifts["y", sign] is not None:
                at, base = plan.lat_place(sign, first, last, width)
                here = lanes == lane
                if ys == 0:
                    here = here & picked(plan.flag["y"] == sign, first)
                halos.append((buffer[at, :] * speed, here, lane, base))
        for i in range(width):
            a = part[i, rows, :]
            for halo, here, lane, base in halos:
                a = a + jnp.where(here, pltpu.roll(halo, (lane - base - i) % LANES, 1), 0.0)
            if i in (0, width - 1):
                edge[min(i, 1), rows, :] = a
            else:
                full[i - 1, rows, :] = a
                moved[rows, (i - 1) * LANES : i * LANES] = a.astype(jnp.bfloat16)
    copies = []

    def done(n, rows, added):
        span = pl.ds(rows.start, rows.stop - rows.start)
        for i in range(1, width - 1):
            s = maskf[i : i + 1, :] * (full[i - 1, rows, :] + 0.5 * added[:, (i - 1) * LANES : i * LANES])
            inner[i - 1, rows, :] = s
            if step:
                to = out.at[span, i, 0, :]
                copies.append(pltpu.make_async_copy(inner.at[i - 1, span, :], to, sem.at[len(copies)]))
                copies[-1].start()
        if step:
            add_bulk(coefs, weights, rows, inner, total)
            return
        for packed, source, sign in ((up, LANES - 1, True), (down, 0, False)):
            for a, b in plan.lat_blocks(sign, rows.start, rows.stop):
                at, base = plan.lat_place(sign, a, b, width)
                acc = packed[at, :] if base else jnp.zeros((b - a, LANES), F32)
                for i in range(1, width - 1):
                    acc = to_lane(acc, inner[i - 1, a:b, :], source, base + i, lanes_of(b - a))
                packed[at, :] = acc

    source_blocks(transfer, moved, plan.comps, done)
    if step:
        for q in range(BULK):
            for i in range(1, width - 1):
                bulk[q, i : i + 1, :] = total[q, i - 1].sum(0, keepdims=True)
            bulk[q, 0:1, :] = jnp.zeros((1, LANES), F32)
            bulk[q, width - 1 : width, :] = jnp.zeros((1, LANES), F32)
    for c in copies:
        c.wait()


def interior(plan, step, part, from_odd, from_even, transfer, coefs, mask):
    comps, width = (plan.comps, mask.shape[0])
    middle = (width - 2, comps, LANES)
    edge = jax.ShapeDtypeStruct((2, comps, LANES), F32)
    scratch = [
        pltpu.VMEM(middle, F32),
        pltpu.VMEM((comps, (width - 2) * LANES), jnp.bfloat16),
        pltpu.VMEM((2, plan.lat_rows(True), LANES), F32),
    ]
    if step == 0:
        outs = [pltpu.VMEM(middle, F32), edge]
        outs += [jax.ShapeDtypeStruct((plan.lat_rows(s), LANES), F32) for s in (True, False)]
    else:
        outs = [pltpu.HBM((comps, width, 1, LANES), F32), edge, jax.ShapeDtypeStruct((BULK, width, LANES), F32)]
        outs += [jax.ShapeDtypeStruct((BULK, comps, LANES), F32)]
        scratch = [pltpu.VMEM(middle, F32)] + scratch + [pltpu.VMEM((BULK, width - 2, 8, LANES), F32)]
        scratch += [pltpu.SemaphoreType.DMA(((width - 2) * comps // block_rows(comps),))]
    return pl.pallas_call(
        functools.partial(interior_kernel, plan, step),
        out_shape=outs,
        in_specs=[VMEM] * 6,
        out_specs=[HBM if step else VMEM] + [VMEM] * (len(outs) - 1),
        scratch_shapes=scratch,
        compiler_params=PARAMS,
        cost_estimate=CHEAP,
        name="interior",
    )(part, from_odd, from_even, transfer, coefs, mask)


def edges_kernel(plan, step, *refs):
    part, from_odd, from_even, transfer, coefs, mask = refs[:6]
    if step == 0:
        state, odd, even = refs[6:9]
        full, moved, both = refs[9:]
    else:
        bulk_in, weights = refs[6:8]
        state, bulk, full, moved, both, total = refs[-6:]
    width = mask.shape[0]
    maskf = jnp.concatenate([mask[0:1, :], mask[width - 1 : width, :]], axis=0).astype(F32)
    both[0] = from_odd[...]
    both[1] = from_even[...]
    from_west, from_east = sides_of(both, "lon")
    for first, last, xs, ys, shifts in plan.blocks():
        rows, count = (slice(first, last), last - first)
        speed = jnp.broadcast_to(coefs[rows, 1:2], (count, LANES))
        for side, sign, buffer in ((0, True, from_west), (1, False, from_east)):
            a = part[side, rows, :]
            shift = shifts["x", sign]
            if shift is not None:
                halo = buffer[first + shift : last + shift, :]
                if xs == 0:
                    halo = jnp.where(picked(plan.flag["x"] == sign, first), halo, 0.0)
                a = a + speed * halo
            full[side, rows, :] = a
            moved[rows, side * LANES : (side + 1) * LANES] = a.astype(jnp.bfloat16)
    if step:
        total[...] = jnp.zeros_like(total)

    def done(n, rows, added):
        for side in range(2):
            s = maskf[side : side + 1, :] * (full[side, rows, :] + 0.5 * added[:, side * LANES : (side + 1) * LANES])
            state[side, rows, :] = s
        if step:
            add_bulk(None, weights, rows, state, total)

    source_blocks(transfer, moved, plan.comps, done)
    if step:
        for q in range(BULK):
            bulk[q] = bulk_in[q]
            bulk[q, 0:1, :] = total[q, 0].sum(0, keepdims=True)
            bulk[q, width - 1 : width, :] = total[q, 1].sum(0, keepdims=True)
        return
    for out, side, sign in ((from_east, 1, True), (from_west, 0, False)):
        at = 0
        for a, b in plan.seg["x", sign]:
            out[at : at + b - a, :] = state[side, a:b, :]
            at += b - a
    odd[...] = both[0]
    even[...] = both[1]


def merge_lat_kernel(plan, width, state, up_in, down_in, odd, even, both):
    down, up = sides_of(both, "lat")
    for out, given, source, sign in ((up, up_in, LANES - 1, True), (down, down_in, 0, False)):
        for a, b in plan.lat_blocks(sign):
            at, base = plan.lat_place(sign, a, b, width)
            acc = out[at, :] if base else given[at, :]
            for side, lane in ((0, base), (1, base + width - 1)):
                acc = to_lane(acc, state[side, a:b, :], source, lane, lanes_of(b - a))
            out[at, :] = acc
    odd[...] = both[0]
    even[...] = both[1]


def merge_lat(plan, width, state, up, down):
    return pl.pallas_call(
        functools.partial(merge_lat_kernel, plan, width),
        out_shape=[jax.ShapeDtypeStruct(x.shape, F32) for x in (up, down)],
        in_specs=[VMEM] * 3,
        out_specs=[VMEM] * 2,
        scratch_shapes=[pltpu.VMEM((2, *up.shape), F32)],
        compiler_params=PARAMS,
        cost_estimate=CHEAP,
        name="merge_lat",
    )(state, up, down)


def edges(plan, step, part, from_odd, from_even, transfer, coefs, mask, *more):
    comps, width = (plan.comps, mask.shape[0])
    outs = [jax.ShapeDtypeStruct((2, comps, LANES), F32)]
    scratch = [pltpu.VMEM((2, comps, LANES), F32), pltpu.VMEM((comps, 2 * LANES), jnp.bfloat16)]
    scratch += [pltpu.VMEM((2, plan.rows("x", True), LANES), F32)]
    if step == 0:
        outs += [jax.ShapeDtypeStruct((plan.rows("x", s), LANES), F32) for s in (True, False)]
    else:
        outs += [jax.ShapeDtypeStruct((BULK, width, LANES), F32)]
        scratch += [pltpu.VMEM((BULK, 2, 8, LANES), F32)]
    return pl.pallas_call(
        functools.partial(edges_kernel, plan, step),
        out_shape=outs,
        in_specs=[VMEM] * min(8, 6 + len(more)) + [ANY] * max(0, len(more) - 2),
        out_specs=[VMEM] * len(outs),
        scratch_shapes=scratch,
        compiler_params=PARAMS,
        cost_estimate=CHEAP,
        name="edges",
    )(part, from_odd, from_even, transfer, coefs, mask, *more)


def ocean_shifts(q, west, east, south, north):
    rows, lanes = q.shape
    row = lax.broadcasted_iota(jnp.int32, q.shape, 0)
    lane = lax.broadcasted_iota(jnp.int32, q.shape, 1)
    before = jnp.where(row == 0, west, pltpu.roll(q, 1, 0))
    after = jnp.where(row == rows - 1, east, pltpu.roll(q, rows - 1, 0))
    below = jnp.where(lane == 0, south, pltpu.roll(q, 1, 1))
    above = jnp.where(lane == lanes - 1, north, pltpu.roll(q, lanes - 1, 1))
    return before, after, below, above


def ocean_base_kernel(plan, u, v, from_odd, from_even, mask, coriolis, base_u, base_v, both):
    levels, ocean_x, ocean_y = u.shape
    start = plan.lat_rows(True)
    both[0] = from_odd[start : start + ocean_x, :]
    both[1] = from_even[start : start + ocean_x, :]
    from_south, from_north = sides_of(both, "lat")
    maskf = mask[...].astype(F32)
    half = 0.5 * coriolis[...]
    for f, (field, other, out, sign) in enumerate(((u, v, base_u, 1.0), (v, u, base_v, -1.0))):
        for level in range(levels):
            q = field[level]

            lane = f * levels + level
            before, after, below, above = ocean_shifts(
                q,
                0.0,
                0.0,
                from_south[:, lane : lane + 1],
                from_north[:, lane : lane + 1],
            )
            lap = before + after + below + above - 4.0 * q
            out[level] = maskf * (q + sign * half * other[level] + 0.1 * lap)


def ocean_base(plan, u, v, from_odd, from_even, mask, coriolis):
    return pl.pallas_call(
        functools.partial(ocean_base_kernel, plan),
        out_shape=[jax.ShapeDtypeStruct(u.shape, F32)] * 2,
        in_specs=[VMEM] * 6,
        out_specs=[VMEM] * 2,
        scratch_shapes=[pltpu.VMEM((2, u.shape[1], LANES), F32)],
        cost_estimate=CHEAP,
        compiler_params=PARAMS,
        name="ocean_base",
    )(u, v, from_odd, from_even, mask, coriolis)


def gathered(slabs, at, off, weight, count, acc=None, offsets=range(OFFSETS)):
    acc = [0.0] * count if acc is None else acc
    for o in offsets:
        rows = [slabs(o, q) for q in range(count)]
        for p in range(len(at)):
            w = jnp.where(off[p] == o, weight[p], 0.0)
            for q in range(count):
                acc[q] = acc[q] + w * jnp.take_along_axis(rows[q], at[p], axis=1, mode="promise_in_bounds")
    return acc


def fill_table(table, left, own, right, ratio, fields):
    width = table.shape[1] // (3 * ratio)
    for q in fields:
        for b, ref in enumerate((left, own, right)):
            for r in range(ratio):
                rows = pl.ds(b * width * ratio + r, width, stride=ratio)
                table[q, rows, :] = jnp.zeros((width, LANES), F32) if ref is None else ref[q]


def bands(from_odd, from_even, near):
    near[0] = from_odd[...]
    near[1] = from_even[...]
    return sides_of(near, "lon")


def line_rows(tiles):
    return 8 * pl.cdiv(2 * tiles, 8)


def remap_lon_kernel(own, from_odd, from_even, cell, offset, weight, u, v, *refs):
    odd, even, rows, near, both = refs[-5:]
    taps, ocean_x, ocean_y = cell.shape
    width, levels = (own.shape[1], u.shape[0])
    tiles = ocean_y // LANES
    last_row = ocean_x - 8
    left, right = bands(from_odd, from_even, near)
    west, east = sides_of(both, "lon")
    for b, ref in enumerate((left, own, right)):
        rows[:, b * width : (b + 1) * width, :] = ref[0:2]
    first_half = lax.broadcasted_iota(jnp.int32, (8, LANES), 0) < 4
    for m in range(tiles):
        lanes = slice(m * LANES, (m + 1) * LANES)
        at, off, w = (
            [jnp.where(first_half, x[p, 0:8, lanes], x[p, last_row : last_row + 8, lanes]) for p in range(taps)]
            for x in (cell, offset, weight)
        )
        acc = gathered(lambda o, q: rows[q, o : o + 8, :], at, off, w, 2)
        for q in range(2):
            n = q * tiles + m
            east[n : n + 1, :] = acc[q][7:8, :]
            west[n : n + 1, :] = acc[q][0:1, :]
    for out, row in ((east, ocean_x - 1), (west, 0)):
        at = line_rows(tiles)
        for field in (u, v):
            for m in range(tiles):
                out[at : at + levels, :] = field[:, row, m * LANES : (m + 1) * LANES]
                at += levels
    odd[...] = both[0]
    even[...] = both[1]


def remap_lat_kernel(own, from_odd, from_even, cell, offset, weight, after, odd, even, table, near, both):
    del after
    left, right = bands(from_odd, from_even, near)
    south, north = sides_of(both, "lat")
    taps, ocean_x, ocean_y = cell.shape
    ratio = ocean_x // own.shape[1]
    last_lane = ocean_y - LANES
    fill_table(table, left, own, right, ratio, range(1, 3))
    lanes = lanes_of(8)
    for t in range(ocean_x // 8):
        here = slice(8 * t, 8 * t + 8)
        at, off, w = (
            [jnp.where(lanes < LANES // 2, x[p, here, 0:LANES], x[p, here, last_lane:]) for p in range(taps)]
            for x in (cell, offset, weight)
        )
        acc = gathered(lambda o, q: table[1 + q, 8 * t + ratio * o : 8 * t + ratio * o + 8, :], at, off, w, 2)
        for out, source in ((north, LANES - 1), (south, 0)):
            packed = jnp.zeros((8, LANES), F32)
            for q in range(2):
                packed = to_lane(packed, acc[q], source, q, lanes)
            out[here, :] = packed
    odd[...] = both[0]
    even[...] = both[1]


def remap_lon(own, from_odd, from_even, cell, offset, weight, u, v, *after):
    _, ocean_x, ocean_y = cell.shape
    width, tiles = (own.shape[1], ocean_y // LANES)
    assert width == 8 and ocean_x % width == 0
    shape = (line_rows(tiles) + 2 * u.shape[0] * tiles, LANES)
    return pl.pallas_call(
        remap_lon_kernel,
        out_shape=[jax.ShapeDtypeStruct(shape, F32)] * 2,
        in_specs=[VMEM] * 8 + [ANY] * len(after),
        out_specs=[VMEM] * 2,
        scratch_shapes=[
            pltpu.VMEM((2, 3 * width, LANES), F32),
            pltpu.VMEM((2, *own.shape), F32),
            pltpu.VMEM((2, *shape), F32),
        ],
        compiler_params=PARAMS,
        cost_estimate=CHEAP,
        name="remap_lon",
    )(own, from_odd, from_even, cell, offset, weight, u, v, *after)


def remap_lat(own, from_odd, from_even, cell, offset, weight, after):
    ocean_x = cell.shape[1]
    end = jax.ShapeDtypeStruct((ocean_x, LANES), F32)
    return pl.pallas_call(
        remap_lat_kernel,
        out_shape=[end, end],
        in_specs=[VMEM] * 6 + [ANY],
        out_specs=[VMEM] * 2,
        scratch_shapes=[
            pltpu.VMEM((BULK, 3 * ocean_x, LANES), F32),
            pltpu.VMEM((2, *own.shape), F32),
            pltpu.VMEM((2, ocean_x, LANES), F32),
        ],
        compiler_params=PARAMS,
        cost_estimate=CHEAP,
        name="remap_lat",
    )(own, from_odd, from_even, cell, offset, weight, after)


def remap_kernel(mine, *refs):
    if mine:
        own, cell, offset, weight, state, given, forcing, out, table, sem = refs
        left = right = None
        last_col = out.shape[1] - 1
        copies = [
            pltpu.make_async_copy(state.at[side], out.at[:, col, 0, :], sem.at[side])
            for side, col in ((0, 0), (1, last_col))
        ]
        for c in copies:
            c.start()
    else:
        from_odd, from_even, cell, offset, weight, begun, forcing, table, near = refs
        left, right = bands(from_odd, from_even, near)
        own = None
    taps, ocean_x, ocean_y = cell.shape
    ratio = table.shape[1] // ocean_x
    width = ocean_x // ratio
    fill_table(table, left, own, right, ratio, range(BULK))
    for t in range(ocean_x // 8):
        used = []
        for o in range(OFFSETS):
            inside = [0 <= i // ratio + o - width < width for i in range(8 * t, 8 * t + 8)]
            if any(inside) if mine else not all(inside):
                used.append(o)
        for m in range(ocean_y // LANES):
            rows, lanes = (slice(8 * t, 8 * t + 8), slice(m * LANES, (m + 1) * LANES))
            at, off, w = ([x[p, rows, lanes] for p in range(taps)] for x in (cell, offset, weight))
            acc = gathered(
                lambda o, q: table[q, 8 * t + ratio * o : 8 * t + ratio * o + 8, :],
                at, off, w, BULK,
                None if mine else [begun[q, rows, lanes] for q in range(BULK)],
                used,
            )
            for q in range(BULK):
                forcing[q, rows, lanes] = acc[q]
    if mine:
        for c in copies:
            c.wait()


def remap_own(own, cell, offset, weight, state, out4):
    _, ocean_x, ocean_y = cell.shape
    return pl.pallas_call(
        functools.partial(remap_kernel, True),
        out_shape=[jax.ShapeDtypeStruct((BULK, ocean_x, ocean_y), F32), jax.ShapeDtypeStruct(out4.shape, F32)],
        in_specs=[VMEM] * 4 + [ANY] + [HBM],
        out_specs=[VMEM, HBM],
        scratch_shapes=[pltpu.VMEM((BULK, 3 * ocean_x, LANES), F32), pltpu.SemaphoreType.DMA((2,))],
        input_output_aliases={5: 1},
        compiler_params=PARAMS,
        cost_estimate=CHEAP,
        name="remap_own",
    )(own, cell, offset, weight, state, *pinned(out4))


def remap_rest(from_odd, from_even, cell, offset, weight, begun):
    ocean_x = cell.shape[1]
    return pl.pallas_call(
        functools.partial(remap_kernel, False),
        out_shape=jax.ShapeDtypeStruct(begun.shape, F32),
        in_specs=[VMEM] * 6,
        out_specs=VMEM,
        scratch_shapes=[pltpu.VMEM((BULK, 3 * ocean_x, LANES), F32), pltpu.VMEM((2, *from_odd.shape), F32)],
        compiler_params=PARAMS,
        cost_estimate=CHEAP,
        name="remap_rest",
    )(from_odd, from_even, cell, offset, weight, begun)


def ocean_final_kernel(
    forcing, lon_odd, lon_even, lat_odd, lat_even, base_u, base_v, mask, coriolis, new_u, new_v, lines, both
):
    levels, ocean_x, ocean_y = base_u.shape
    lines[0] = lon_odd[...]
    lines[1] = lon_even[...]
    from_west, from_east = sides_of(lines, "lon")
    both[0] = lat_odd[...]
    both[1] = lat_even[...]
    from_south, from_north = sides_of(both, "lat")
    tiles = ocean_y // LANES

    def line(buffer, q):
        return jnp.concatenate([buffer[q * tiles + m : q * tiles + m + 1, :] for m in range(tiles)], axis=1)

    zero_line = jnp.zeros((1, ocean_y), F32)
    zero_end = jnp.zeros((ocean_x, 1), F32)
    grad = []
    for q in range(3):
        lon = q < 2
        lat = q > 0
        before, after, below, above = ocean_shifts(
            forcing[q],
            line(from_west, q) if lon else zero_line,
            line(from_east, q) if lon else zero_line,
            from_south[:, q - 1 : q] if lat else zero_end,
            from_north[:, q - 1 : q] if lat else zero_end,
        )
        grad.append((0.5 * (after - before), 0.5 * (above - below)))
    force_x = -(grad[0][0] + grad[1][1])
    force_y = -(grad[1][0] + grad[2][1])
    maskf = mask[...].astype(F32)
    half = 0.5 * coriolis[...]
    add_u = maskf * (half * forcing[4] + 0.5 * force_x)
    add_v = maskf * (0.5 * force_y - half * forcing[3])
    for level in range(levels):
        decay = np.float32(np.exp(np.float32(-level / 3.0)))
        new_u[level] = base_u[level] + decay * add_u
        new_v[level] = base_v[level] + decay * add_v
    row = lax.broadcasted_iota(jnp.int32, (8, LANES), 0)
    for buffer, first, at in ((from_west, 0, 0), (from_east, ocean_x - 8, 7)):
        rows = slice(first, first + 8)
        for m in range(tiles):
            lanes = slice(m * LANES, (m + 1) * LANES)
            share = jnp.where(row == at, 0.1 * maskf[rows, lanes], 0.0)
            for f, out in enumerate((new_u, new_v)):
                start = line_rows(tiles) + (f * tiles + m) * levels
                for level in range(levels):
                    line_part = buffer[start + level : start + level + 1, :]
                    out[level, rows, lanes] = out[level, rows, lanes] + share * line_part


def ocean_final(forcing, halos, base_u, base_v, mask, coriolis):
    return pl.pallas_call(
        ocean_final_kernel,
        out_shape=[jax.ShapeDtypeStruct(base_u.shape, F32)] * 2,
        in_specs=[VMEM] * 9,
        out_specs=[VMEM] * 2,
        scratch_shapes=[pltpu.VMEM((2, *halos[0].shape), F32), pltpu.VMEM((2, base_u.shape[1], LANES), F32)],
        compiler_params=PARAMS,
        cost_estimate=CHEAP,
        name="ocean_final",
    )(forcing, *halos, base_u, base_v, mask, coriolis)


def swap(odd, even, axis, wrap):
    count = lax.axis_size(axis)
    got = []
    for first, value in ((0, odd), (1, even)):
        pairs = [(i, (i + 1) % count) for i in range(first, count, 2) if wrap or i + 1 < count]
        got.append(lax.ppermute(value, axis, pairs + [(j, i) for i, j in pairs]))
    return got


def exchange(lon, lat):
    from_lat = swap(*lat, "lat", False)
    return swap(*lon, "lon", True) + from_lat


def local(
    spectrum,
    sea_mask,
    transfer,
    bulk_weight,
    remap_cell,
    remap_weight,
    ocean_u,
    ocean_v,
    ocean_mask,
    coriolis,
):
    comps, width_x, width_y = spectrum.shape
    plan = Plan(comps)
    spec2 = spectrum.reshape(comps * width_x, width_y)
    lon = pack_lon(plan, spectrum.reshape(comps, width_x, 1, width_y), sea_mask)
    *lat, spec2 = pack_lat(plan, spec2, sea_mask, ocean_u, ocean_v, lon[0])
    begun = exchange(lon, lat)

    coefs = columns_of(plan, bulk_weight)
    total_y = width_y * lax.axis_size("lat")
    taps_first = remap_cell.transpose(2, 0, 1)
    offset = taps_first // total_y
    cell = taps_first % width_y
    weight = remap_weight.transpose(2, 0, 1)
    line = coriolis[None, :]

    part = advect(plan, 0, spec2, coefs, sea_mask)
    middle, edge, up, down = interior(plan, 0, part, *begun[2:], transfer, coefs, sea_mask)
    sides, *lon = edges(plan, 0, edge, *begun[:2], transfer, coefs, sea_mask)
    halos = exchange(lon, merge_lat(plan, width_x, sides, up, down))

    base_u, base_v = ocean_base(plan, ocean_u, ocean_v, *begun[2:], ocean_mask, line)
    part = advect(plan, 1, middle, coefs, sides)
    out4, edge, bulk, weights = interior(plan, 1, part, *halos[2:], transfer, coefs, sea_mask)
    sides, bulk = edges(plan, 1, edge, *halos[:2], transfer, coefs, sea_mask, bulk, weights, base_u)
    near = swap(bulk, bulk, "lon", True)
    forcing, out4 = remap_own(bulk, cell, offset, weight, sides, out4)

    remapped = (bulk, *near, cell, offset, weight)
    lon = remap_lon(*remapped, ocean_u, ocean_v, forcing)
    halos = exchange(lon, remap_lat(*remapped, lon[0]))
    forcing = remap_rest(*near, cell, offset, weight, forcing)
    new_u, new_v = ocean_final(forcing, halos, base_u, base_v, ocean_mask, line)
    state = out4.reshape(spectrum.shape)
    return (state, new_u, new_v)


def solution(mesh):
    placed = (
        P(None, "lon", "lat"),
        P("lon", "lat"),
        P(),
        P(),
        P("lon", "lat", None),
        P("lon", "lat", None),
        P(None, "lon", "lat"),
        P(None, "lon", "lat"),
        P("lon", "lat"),
        P("lat"),
    )
    return jax.shard_map(
        local,
        mesh=mesh,
        in_specs=placed,
        out_specs=(P(None, "lon", "lat"), P(None, "lon", "lat"), P(None, "lon", "lat")),
        check_vma=False,
    )
```

```python
import functools

import jax
import jax.numpy as jnp
import numpy as np
from jax import lax
from jax.experimental import pallas as pl
from jax.experimental.pallas import tpu as pltpu
from jax.sharding import PartitionSpec as P

NFREQ = 36
STEP = 16
LANES = 128
BULK = 5
GROUPS = 4
OFFSETS = 17
BLOCK = 176
F32 = jnp.float32
VMEM = pl.BlockSpec(memory_space=pltpu.VMEM)
ANY = pl.BlockSpec(memory_space=pl.ANY)
HBM = pl.BlockSpec(memory_space=pltpu.HBM)
PARAMS = pltpu.CompilerParams(vmem_limit_bytes=24 << 20)
CHEAP = pl.CostEstimate(flops=1, bytes_accessed=1, transcendentals=0)


def pinned(*arrays):
    return [pltpu.with_memory_space_constraint(x, pltpu.HBM) for x in arrays]


def kept(array):
    return pltpu.with_memory_space_constraint(array, pltpu.VMEM)


def parity(axis):
    return lax.rem(lax.axis_index(axis), 2)


def sides_of(both, axis):
    return both.at[1 - parity(axis)], both.at[parity(axis)]


class Plan:
    def __init__(self, comps):
        dirs = comps // NFREQ
        k = np.arange(comps)
        theta = 2.0 * np.pi * ((k // NFREQ) + 0.5) / dirs
        speed = 1.1 ** (-(k % NFREQ).astype(np.float64))
        cx = 0.45 * speed * np.cos(theta)
        cy = 0.45 * speed * np.sin(theta)
        self.comps = comps
        self.coef = np.stack([1.0 - np.abs(cx) - np.abs(cy), np.abs(cx), np.abs(cy)], 1).astype(np.float32)
        self.flag = {"x": cx > 0, "y": cy > 0}
        self.seg = {}
        for axis, step in (("x", 8), ("y", STEP)):
            for sign in (True, False):
                self.seg[axis, sign] = self.runs(self.flag[axis] == sign, step)

    def runs(self, flag, step):
        out = []
        for n in np.flatnonzero(flag.reshape(-1, step).any(1)):
            if out and out[-1][1] == n * step:
                out[-1][1] = int(n + 1) * step
            else:
                out.append([int(n) * step, int(n + 1) * step])
        return [(a, b) for a, b in out]

    def rows(self, axis, sign):
        return sum(b - a for a, b in self.seg[axis, sign])

    def lat_rows(self, sign):
        ((a, b),) = self.seg["y", sign]
        return -(-(b - a) // (GROUPS * STEP)) * STEP

    def lat_cuts(self):
        cuts = set()
        for sign in (True, False):
            ((a, b),) = self.seg["y", sign]
            cuts |= set(range(a, b, self.lat_rows(sign))) | {b}
        return cuts

    def lat_place(self, sign, first, last, width):
        ((a, _),) = self.seg["y", sign]
        group, row = divmod(first - a, self.lat_rows(sign))
        assert row + last - first <= self.lat_rows(sign) and (group + 1) * width <= LANES
        return slice(row, row + last - first), group * width

    def lat_blocks(self, sign, first=0, last=None):
        ((a, b),) = self.seg["y", sign]
        a, b = (max(a, first), b if last is None else min(b, last))
        return split(a, b, self.lat_cuts()) if a < b else []

    def shift(self, axis, sign, first):
        used = np.flatnonzero(self.flag[axis][first : first + STEP] == sign) + first
        if not len(used):
            return None
        base = 0
        for a, b in self.seg[axis, sign]:
            if a <= used[0] < b:
                at = base + first - a
                assert used[-1] < b and 0 <= at <= self.rows(axis, sign) - STEP
                return base - a
            base += b - a
        raise ValueError("no segment")

    def blocks(self):
        cuts = self.lat_cuts()
        return [(a, b, *rest) for first, last, *rest in self.regions() for a, b in split(first, last, cuts)]

    def regions(self):
        out = []
        for r in range(0, self.comps, STEP):
            sign = {}
            for axis in "xy":
                part = self.flag[axis][r : r + STEP]
                sign[axis] = 1 if part.all() else (0 if part.any() else -1)
            shifts = {(axis, s): self.shift(axis, s, r) for axis in "xy" for s in (True, False)}
            if out and sign["x"] and sign["y"] and out[-1][2:] == [sign["x"], sign["y"], shifts]:
                out[-1][1] = r + STEP
            else:
                out.append([r, r + STEP, sign["x"], sign["y"], shifts])
        return out


def split(first, last, cuts=(), most=BLOCK):
    out = []
    edges = [first] + sorted(c for c in cuts if first < c < last) + [last]
    for start, stop in zip(edges[:-1], edges[1:]):
        chunks = (stop - start) // STEP
        count = -(-chunks * STEP // most)
        at = [start + chunks * n // count * STEP for n in range(count + 1)]
        out += list(zip(at[:-1], at[1:]))
    return out


def lanes_of(rows):
    return lax.broadcasted_iota(jnp.int32, (rows, LANES), 1)


def picked(flag, first):
    row = lax.broadcasted_iota(jnp.int32, (STEP, LANES), 0)
    part = flag[first : first + STEP]
    out, n = (None, 0)
    while n < STEP:
        if not part[n]:
            n += 1
            continue
        m = n
        while m < STEP and part[m]:
            m += 1
        here = (row >= n) & (row < m)
        out = here if out is None else out | here
        n = m
    return out


def upwind(plan, axis, sign, first, from_plus, from_minus):
    if sign > 0:
        return from_plus()
    if sign < 0:
        return from_minus()
    plus, minus = (from_plus(), from_minus())
    where = picked(plan.flag[axis], first)
    zero = jnp.zeros((STEP, LANES), F32)
    if plus is None and minus is None:
        return None
    return jnp.where(where, zero if plus is None else plus, zero if minus is None else minus)


def columns_kernel(coef, bulk_weight, columns, rows):
    rows[...] = jnp.zeros_like(rows)
    rows[3 : 3 + BULK, : bulk_weight.shape[1]] = bulk_weight[...]
    for at in range(0, rows.shape[1], LANES):
        count = min(LANES, columns.shape[0] - at)
        turned = rows[:, at : at + LANES].T
        columns[at : at + count, :] = coef[at : at + count, :] + turned[:count, :]


def columns_of(plan, bulk_weight):
    comps = plan.comps
    coef = np.zeros((comps, 3 + BULK), np.float32)
    coef[:, :3] = plan.coef
    return pl.pallas_call(
        columns_kernel,
        out_shape=jax.ShapeDtypeStruct(coef.shape, F32),
        in_specs=[VMEM] * 2,
        out_specs=VMEM,
        scratch_shapes=[pltpu.VMEM((3 + BULK, -(-comps // LANES) * LANES), F32)],
        compiler_params=PARAMS,
        cost_estimate=CHEAP,
        name="columns",
    )(jnp.asarray(coef), bulk_weight)


def pack_lon_kernel(plan, spec, mask, odd, even, maskv, both, sem):
    last_col = spec.shape[1] - 1
    west, east = sides_of(both, "lon")
    copies = [pltpu.make_async_copy(mask, maskv, sem.at[0])]
    for out, sign, col in ((east, True, last_col), (west, False, 0)):
        at = 0
        for a, b in plan.seg["x", sign]:
            copies.append(
                pltpu.make_async_copy(
                    spec.at[pl.ds(a, b - a), col, 0, :], out.at[pl.ds(at, b - a), :], sem.at[len(copies)]
                )
            )
            at += b - a
    for c in copies:
        c.start()
    for c in copies:
        c.wait()
    masks = [maskv[col : col + 1, :].astype(F32) for col in (last_col, 0)]
    lower = jnp.full((1, LANES), parity("lon"), jnp.int32) == 0
    odd[...] = both[0] * jnp.where(lower, masks[0], masks[1])
    even[...] = both[1] * jnp.where(lower, masks[1], masks[0])


def pack_lon(plan, spec4, mask):
    segments = sum(len(plan.seg["x", s]) for s in (True, False))
    shape = (plan.rows("x", True), LANES)
    assert plan.rows("x", True) == plan.rows("x", False)
    return pl.pallas_call(
        functools.partial(pack_lon_kernel, plan),
        out_shape=[jax.ShapeDtypeStruct(shape, F32)] * 2,
        in_specs=[HBM] * 2,
        out_specs=[VMEM, VMEM],
        scratch_shapes=[
            pltpu.VMEM(mask.shape, mask.dtype),
            pltpu.VMEM((2, *shape), F32),
            pltpu.SemaphoreType.DMA((segments + 1,)),
        ],
        compiler_params=PARAMS,
        cost_estimate=CHEAP,
        name="pack_lon",
    )(*pinned(spec4, mask))


def to_lane(acc, column, source, lane, lanes):
    return jnp.where(lanes == lane, pltpu.roll(column, (lane - source) % LANES, 1), acc)


def pack_lat_kernel(plan, spec, mask, u_hbm, v_hbm, after, odd, even, both, u, v, sem):
    del after
    fields = [pltpu.make_async_copy(x, y, sem.at[n]) for n, (x, y) in enumerate(((u_hbm, u), (v_hbm, v)))]
    for c in fields:
        c.start()
    south, north = sides_of(both, "lat")
    width_x = mask.shape[0]
    levels, ocean_x, ocean_y = u.shape
    last = ocean_y - LANES
    maskf = mask[...].astype(F32)
    for out, source, sign in ((north, LANES - 1, True), (south, 0, False)):
        for a, b in plan.lat_blocks(sign):
            rows, lane = plan.lat_place(sign, a, b, width_x)
            acc = out[rows, :] if lane else jnp.zeros((b - a, LANES), F32)
            for i in range(width_x):
                x = spec[pl.ds(a * width_x + i, b - a, stride=width_x), :] * maskf[i : i + 1, :]
                acc = to_lane(acc, x, source, lane + i, lanes_of(b - a))
            out[rows, :] = acc
    for c in fields:
        c.wait()
    for out, source, sign, m in ((north, LANES - 1, True, last), (south, 0, False, 0)):
        at = plan.lat_rows(sign)
        acc = jnp.zeros((ocean_x, LANES), F32)
        for f in range(2 * levels):
            field = (u, v)[f // levels]
            acc = to_lane(acc, field[f % levels, :, m : m + LANES], source, f, lanes_of(ocean_x))
        out[at : at + ocean_x, :] = acc
    odd[...] = both[0]
    even[...] = both[1]


def pack_lat(plan, spec2, mask, u, v, after):
    assert plan.lat_rows(True) == plan.lat_rows(False)
    shape = (plan.lat_rows(True) + u.shape[1], LANES)
    return pl.pallas_call(
        functools.partial(pack_lat_kernel, plan),
        out_shape=[jax.ShapeDtypeStruct(shape, F32)] * 2,
        in_specs=[VMEM] * 2 + [HBM] * 2 + [ANY],
        out_specs=[VMEM] * 2,
        cost_estimate=CHEAP,
        scratch_shapes=[pltpu.VMEM((2, *shape), F32)]
        + [pltpu.VMEM(x.shape, F32) for x in (u, v)]
        + [pltpu.SemaphoreType.DMA((2,))],
        compiler_params=PARAMS,
        name="pack_lat",
    )(kept(spec2), mask, *pinned(u, v), after)


def advect_kernel(plan, step, state, coefs, more, part):
    width = part.shape[0]
    if step == 0:
        maskf = more[...].astype(F32)

    def column(i, first, last):
        if step == 0:
            return state[pl.ds(first * width + i, last - first, stride=width), :] * maskf[i : i + 1, :]
        if i in (0, width - 1):
            return more[min(i, 1), first:last, :]
        return state[i - 1, first:last, :]

    for first, last, xs, ys, _ in plan.blocks():
        count = last - first
        keep, east, up = (jnp.broadcast_to(coefs[first:last, q : q + 1], (count, LANES)) for q in range(3))
        lanes = lanes_of(count)
        x = [column(i, first, last) for i in range(width)]
        for i in range(width):
            lat = upwind(
                plan, "y", ys, first,
                lambda: jnp.where(lanes == 0, 0.0, pltpu.roll(x[i], 1, 1)),
                lambda: jnp.where(lanes == LANES - 1, 0.0, pltpu.roll(x[i], LANES - 1, 1)),
            )
            lon = upwind(
                plan, "x", xs, first,
                lambda: x[i - 1] if i else None,
                lambda: x[i + 1] if i + 1 < width else None,
            )
            a = keep * x[i] + up * lat
            if lon is not None:
                a = a + east * lon
            part[i, first:last, :] = a


def advect(plan, step, state, coefs, more):
    comps, width = (plan.comps, state.shape[0] // plan.comps if step == 0 else state.shape[0] + 2)
    return pl.pallas_call(
        functools.partial(advect_kernel, plan, step),
        out_shape=jax.ShapeDtypeStruct((width, comps, LANES), F32),
        in_specs=[VMEM] * 3,
        out_specs=VMEM,
        compiler_params=PARAMS,
        cost_estimate=CHEAP,
        name="advect",
    )(kept(state), coefs, more)


def block_rows(comps):
    return max(b for b in range(STEP, 449, STEP) if comps % b == 0)


def source_blocks(transfer, moved, comps, body):
    block = block_rows(comps)

    for n in range(comps // block):
        rows = slice(n * block, (n + 1) * block)
        body(n, rows, jnp.dot(transfer[rows, :], moved[...], preferred_element_type=F32))


def add_bulk(coefs, weights, rows, state, total):
    count, columns = (rows.stop - rows.start, state.shape[0])
    if coefs is not None:
        for q in range(BULK):
            weights[q, rows, :] = jnp.broadcast_to(coefs[rows, 3 + q : 4 + q], (count, LANES))
    acc = [[total[q, i] for i in range(columns)] for q in range(BULK)]
    for first in range(rows.start, rows.stop, 8):
        here = slice(first, first + 8)
        s = [state[i, here, :] for i in range(columns)]
        for q in range(BULK):
            w = weights[q, here, :]
            for i in range(columns):
                acc[q][i] = acc[q][i] + w * s[i]
    for q in range(BULK):
        for i in range(columns):
            total[q, i] = acc[q][i]


def interior_kernel(plan, step, *refs):
    part, from_odd, from_even, transfer, coefs, mask = refs[:6]
    if step == 0:
        inner, edge, up, down = refs[6:10]
        full, moved, both = refs[10:]
    else:
        out, edge, bulk, weights = refs[6:10]
        inner, full, moved, both, total, sem = refs[10:]
        total[...] = jnp.zeros_like(total)
    width = part.shape[0]
    maskf = mask[...].astype(F32)
    both[0] = from_odd[: both.shape[1], :]
    both[1] = from_even[: both.shape[1], :]
    south, north = sides_of(both, "lat")
    for first, last, _, ys, shifts in plan.blocks():
        rows, count = (slice(first, last), last - first)
        lanes = lanes_of(count)
        speed = jnp.broadcast_to(coefs[rows, 2:3], (count, LANES))
        halos = []
        for sign, buffer, lane in ((True, south, 0), (False, north, LANES - 1)):
            if shifts["y", sign] is not None:
                at, base = plan.lat_place(sign, first, last, width)
                here = lanes == lane
                if ys == 0:
                    here = here & picked(plan.flag["y"] == sign, first)
                halos.append((buffer[at, :] * speed, here, lane, base))
        for i in range(width):
            a = part[i, rows, :]
            for halo, here, lane, base in halos:
                a = a + jnp.where(here, pltpu.roll(halo, (lane - base - i) % LANES, 1), 0.0)
            if i in (0, width - 1):
                edge[min(i, 1), rows, :] = a
            else:
                full[i - 1, rows, :] = a
                moved[rows, (i - 1) * LANES : i * LANES] = a.astype(jnp.bfloat16)
    copies = []

    def done(n, rows, added):
        span = pl.ds(rows.start, rows.stop - rows.start)
        for i in range(1, width - 1):
            s = maskf[i : i + 1, :] * (full[i - 1, rows, :] + 0.5 * added[:, (i - 1) * LANES : i * LANES])
            inner[i - 1, rows, :] = s
            if step:
                to = out.at[span, i, 0, :]
                copies.append(pltpu.make_async_copy(inner.at[i - 1, span, :], to, sem.at[len(copies)]))
                copies[-1].start()
        if step:
            add_bulk(coefs, weights, rows, inner, total)
            return
        for packed, source, sign in ((up, LANES - 1, True), (down, 0, False)):
            for a, b in plan.lat_blocks(sign, rows.start, rows.stop):
                at, base = plan.lat_place(sign, a, b, width)
                acc = packed[at, :] if base else jnp.zeros((b - a, LANES), F32)
                for i in range(1, width - 1):
                    acc = to_lane(acc, inner[i - 1, a:b, :], source, base + i, lanes_of(b - a))
                packed[at, :] = acc

    source_blocks(transfer, moved, plan.comps, done)
    if step:
        for q in range(BULK):
            for i in range(1, width - 1):
                bulk[q, i : i + 1, :] = total[q, i - 1].sum(0, keepdims=True)
            bulk[q, 0:1, :] = jnp.zeros((1, LANES), F32)
            bulk[q, width - 1 : width, :] = jnp.zeros((1, LANES), F32)
    for c in copies:
        c.wait()


def interior(plan, step, part, from_odd, from_even, transfer, coefs, mask):
    comps, width = (plan.comps, mask.shape[0])
    middle = (width - 2, comps, LANES)
    edge = jax.ShapeDtypeStruct((2, comps, LANES), F32)
    scratch = [
        pltpu.VMEM(middle, F32),
        pltpu.VMEM((comps, (width - 2) * LANES), jnp.bfloat16),
        pltpu.VMEM((2, plan.lat_rows(True), LANES), F32),
    ]
    if step == 0:
        outs = [pltpu.VMEM(middle, F32), edge]
        outs += [jax.ShapeDtypeStruct((plan.lat_rows(s), LANES), F32) for s in (True, False)]
    else:
        outs = [pltpu.HBM((comps, width, 1, LANES), F32), edge, jax.ShapeDtypeStruct((BULK, width, LANES), F32)]
        outs += [jax.ShapeDtypeStruct((BULK, comps, LANES), F32)]
        scratch = [pltpu.VMEM(middle, F32)] + scratch + [pltpu.VMEM((BULK, width - 2, 8, LANES), F32)]
        scratch += [pltpu.SemaphoreType.DMA(((width - 2) * comps // block_rows(comps),))]
    return pl.pallas_call(
        functools.partial(interior_kernel, plan, step),
        out_shape=outs,
        in_specs=[VMEM] * 6,
        out_specs=[HBM if step else VMEM] + [VMEM] * (len(outs) - 1),
        scratch_shapes=scratch,
        compiler_params=PARAMS,
        cost_estimate=CHEAP,
        name="interior",
    )(part, from_odd, from_even, transfer, coefs, mask)


def edges_kernel(plan, step, *refs):
    part, from_odd, from_even, transfer, coefs, mask = refs[:6]
    if step == 0:
        state, odd, even = refs[6:9]
        full, moved, both = refs[9:]
    else:
        bulk_in, weights = refs[6:8]
        state, bulk, full, moved, both, total = refs[-6:]
    width = mask.shape[0]
    maskf = jnp.concatenate([mask[0:1, :], mask[width - 1 : width, :]], axis=0).astype(F32)
    both[0] = from_odd[...]
    both[1] = from_even[...]
    from_west, from_east = sides_of(both, "lon")
    for first, last, xs, ys, shifts in plan.blocks():
        rows, count = (slice(first, last), last - first)
        speed = jnp.broadcast_to(coefs[rows, 1:2], (count, LANES))
        for side, sign, buffer in ((0, True, from_west), (1, False, from_east)):
            a = part[side, rows, :]
            shift = shifts["x", sign]
            if shift is not None:
                halo = buffer[first + shift : last + shift, :]
                if xs == 0:
                    halo = jnp.where(picked(plan.flag["x"] == sign, first), halo, 0.0)
                a = a + speed * halo
            full[side, rows, :] = a
            moved[rows, side * LANES : (side + 1) * LANES] = a.astype(jnp.bfloat16)
    if step:
        total[...] = jnp.zeros_like(total)

    def done(n, rows, added):
        for side in range(2):
            s = maskf[side : side + 1, :] * (full[side, rows, :] + 0.5 * added[:, side * LANES : (side + 1) * LANES])
            state[side, rows, :] = s
        if step:
            add_bulk(None, weights, rows, state, total)

    source_blocks(transfer, moved, plan.comps, done)
    if step:
        for q in range(BULK):
            bulk[q] = bulk_in[q]
            bulk[q, 0:1, :] = total[q, 0].sum(0, keepdims=True)
            bulk[q, width - 1 : width, :] = total[q, 1].sum(0, keepdims=True)
        return
    for out, side, sign in ((from_east, 1, True), (from_west, 0, False)):
        at = 0
        for a, b in plan.seg["x", sign]:
            out[at : at + b - a, :] = state[side, a:b, :]
            at += b - a
    odd[...] = both[0]
    even[...] = both[1]


def merge_lat_kernel(plan, width, state, up_in, down_in, odd, even, both):
    down, up = sides_of(both, "lat")
    for out, given, source, sign in ((up, up_in, LANES - 1, True), (down, down_in, 0, False)):
        for a, b in plan.lat_blocks(sign):
            at, base = plan.lat_place(sign, a, b, width)
            acc = out[at, :] if base else given[at, :]
            for side, lane in ((0, base), (1, base + width - 1)):
                acc = to_lane(acc, state[side, a:b, :], source, lane, lanes_of(b - a))
            out[at, :] = acc
    odd[...] = both[0]
    even[...] = both[1]


def merge_lat(plan, width, state, up, down):
    return pl.pallas_call(
        functools.partial(merge_lat_kernel, plan, width),
        out_shape=[jax.ShapeDtypeStruct(x.shape, F32) for x in (up, down)],
        in_specs=[VMEM] * 3,
        out_specs=[VMEM] * 2,
        scratch_shapes=[pltpu.VMEM((2, *up.shape), F32)],
        compiler_params=PARAMS,
        cost_estimate=CHEAP,
        name="merge_lat",
    )(state, up, down)


def edges(plan, step, part, from_odd, from_even, transfer, coefs, mask, *more):
    comps, width = (plan.comps, mask.shape[0])
    outs = [jax.ShapeDtypeStruct((2, comps, LANES), F32)]
    scratch = [pltpu.VMEM((2, comps, LANES), F32), pltpu.VMEM((comps, 2 * LANES), jnp.bfloat16)]
    scratch += [pltpu.VMEM((2, plan.rows("x", True), LANES), F32)]
    if step == 0:
        outs += [jax.ShapeDtypeStruct((plan.rows("x", s), LANES), F32) for s in (True, False)]
    else:
        outs += [jax.ShapeDtypeStruct((BULK, width, LANES), F32)]
        scratch += [pltpu.VMEM((BULK, 2, 8, LANES), F32)]
    return pl.pallas_call(
        functools.partial(edges_kernel, plan, step),
        out_shape=outs,
        in_specs=[VMEM] * min(8, 6 + len(more)) + [ANY] * max(0, len(more) - 2),
        out_specs=[VMEM] * len(outs),
        scratch_shapes=scratch,
        compiler_params=PARAMS,
        cost_estimate=CHEAP,
        name="edges",
    )(part, from_odd, from_even, transfer, coefs, mask, *more)


def ocean_shifts(q, west, east, south, north):
    rows, lanes = q.shape
    row = lax.broadcasted_iota(jnp.int32, q.shape, 0)
    lane = lax.broadcasted_iota(jnp.int32, q.shape, 1)
    before = jnp.where(row == 0, west, pltpu.roll(q, 1, 0))
    after = jnp.where(row == rows - 1, east, pltpu.roll(q, rows - 1, 0))
    below = jnp.where(lane == 0, south, pltpu.roll(q, 1, 1))
    above = jnp.where(lane == lanes - 1, north, pltpu.roll(q, lanes - 1, 1))
    return before, after, below, above


def ocean_base_kernel(plan, u, v, from_odd, from_even, mask, coriolis, base_u, base_v, both):
    levels, ocean_x, ocean_y = u.shape
    start = plan.lat_rows(True)
    both[0] = from_odd[start : start + ocean_x, :]
    both[1] = from_even[start : start + ocean_x, :]
    from_south, from_north = sides_of(both, "lat")
    maskf = mask[...].astype(F32)
    half = 0.5 * coriolis[...]
    for f, (field, other, out, sign) in enumerate(((u, v, base_u, 1.0), (v, u, base_v, -1.0))):
        for level in range(levels):
            q = field[level]

            lane = f * levels + level
            before, after, below, above = ocean_shifts(
                q,
                0.0,
                0.0,
                from_south[:, lane : lane + 1],
                from_north[:, lane : lane + 1],
            )
            lap = before + after + below + above - 4.0 * q
            out[level] = maskf * (q + sign * half * other[level] + 0.1 * lap)


def ocean_base(plan, u, v, from_odd, from_even, mask, coriolis):
    return pl.pallas_call(
        functools.partial(ocean_base_kernel, plan),
        out_shape=[jax.ShapeDtypeStruct(u.shape, F32)] * 2,
        in_specs=[VMEM] * 6,
        out_specs=[VMEM] * 2,
        scratch_shapes=[pltpu.VMEM((2, u.shape[1], LANES), F32)],
        cost_estimate=CHEAP,
        compiler_params=PARAMS,
        name="ocean_base",
    )(u, v, from_odd, from_even, mask, coriolis)


def gathered(slabs, at, off, weight, count, acc=None, offsets=range(OFFSETS)):
    acc = [0.0] * count if acc is None else acc
    for p in range(len(at)):
        for q in range(count):
            got = 0.0
            for o in offsets:
                new = jnp.take_along_axis(slabs(o, q), at[p], axis=1, mode="promise_in_bounds")
                got = jnp.where(off[p] == o, new, got)
            acc[q] = acc[q] + weight[p] * got
    return acc


def fill_table(table, left, own, right, ratio, fields):
    width = table.shape[1] // (3 * ratio)
    for q in fields:
        for b, ref in enumerate((left, own, right)):
            for r in range(ratio):
                rows = pl.ds(b * width * ratio + r, width, stride=ratio)
                table[q, rows, :] = jnp.zeros((width, LANES), F32) if ref is None else ref[q]


def bands(from_odd, from_even, near):
    near[0] = from_odd[...]
    near[1] = from_even[...]
    return sides_of(near, "lon")


def line_rows(tiles):
    return 8 * pl.cdiv(2 * tiles, 8)


def remap_lon_kernel(own, from_odd, from_even, cell, offset, weight, u, v, *refs):
    odd, even, rows, near, both = refs[-5:]
    taps, ocean_x, ocean_y = cell.shape
    width, levels = (own.shape[1], u.shape[0])
    tiles = ocean_y // LANES
    last_row = ocean_x - 8
    left, right = bands(from_odd, from_even, near)
    west, east = sides_of(both, "lon")
    for b, ref in enumerate((left, own, right)):
        rows[:, b * width : (b + 1) * width, :] = ref[0:2]
    first_half = lax.broadcasted_iota(jnp.int32, (8, LANES), 0) < 4
    for m in range(tiles):
        lanes = slice(m * LANES, (m + 1) * LANES)
        at, off, w = (
            [jnp.where(first_half, x[p, 0:8, lanes], x[p, last_row : last_row + 8, lanes]) for p in range(taps)]
            for x in (cell, offset, weight)
        )
        acc = gathered(lambda o, q: rows[q, o : o + 8, :], at, off, w, 2)
        for q in range(2):
            n = q * tiles + m
            east[n : n + 1, :] = acc[q][7:8, :]
            west[n : n + 1, :] = acc[q][0:1, :]
    for out, row in ((east, ocean_x - 1), (west, 0)):
        at = line_rows(tiles)
        for field in (u, v):
            for m in range(tiles):
                out[at : at + levels, :] = field[:, row, m * LANES : (m + 1) * LANES]
                at += levels
    odd[...] = both[0]
    even[...] = both[1]


def remap_lat_kernel(own, from_odd, from_even, cell, offset, weight, after, odd, even, table, near, both):
    del after
    left, right = bands(from_odd, from_even, near)
    south, north = sides_of(both, "lat")
    taps, ocean_x, ocean_y = cell.shape
    ratio = ocean_x // own.shape[1]
    last_lane = ocean_y - LANES
    fill_table(table, left, own, right, ratio, range(1, 3))
    lanes = lanes_of(8)
    for t in range(ocean_x // 8):
        here = slice(8 * t, 8 * t + 8)
        at, off, w = (
            [jnp.where(lanes < LANES // 2, x[p, here, 0:LANES], x[p, here, last_lane:]) for p in range(taps)]
            for x in (cell, offset, weight)
        )
        acc = gathered(lambda o, q: table[1 + q, 8 * t + ratio * o : 8 * t + ratio * o + 8, :], at, off, w, 2)
        for out, source in ((north, LANES - 1), (south, 0)):
            packed = jnp.zeros((8, LANES), F32)
            for q in range(2):
                packed = to_lane(packed, acc[q], source, q, lanes)
            out[here, :] = packed
    odd[...] = both[0]
    even[...] = both[1]


def remap_lon(own, from_odd, from_even, cell, offset, weight, u, v, *after):
    _, ocean_x, ocean_y = cell.shape
    width, tiles = (own.shape[1], ocean_y // LANES)
    assert width == 8 and ocean_x % width == 0
    shape = (line_rows(tiles) + 2 * u.shape[0] * tiles, LANES)
    return pl.pallas_call(
        remap_lon_kernel,
        out_shape=[jax.ShapeDtypeStruct(shape, F32)] * 2,
        in_specs=[VMEM] * 8 + [ANY] * len(after),
        out_specs=[VMEM] * 2,
        scratch_shapes=[
            pltpu.VMEM((2, 3 * width, LANES), F32),
            pltpu.VMEM((2, *own.shape), F32),
            pltpu.VMEM((2, *shape), F32),
        ],
        compiler_params=PARAMS,
        cost_estimate=CHEAP,
        name="remap_lon",
    )(own, from_odd, from_even, cell, offset, weight, u, v, *after)


def remap_lat(own, from_odd, from_even, cell, offset, weight, after):
    ocean_x = cell.shape[1]
    end = jax.ShapeDtypeStruct((ocean_x, LANES), F32)
    return pl.pallas_call(
        remap_lat_kernel,
        out_shape=[end, end],
        in_specs=[VMEM] * 6 + [ANY],
        out_specs=[VMEM] * 2,
        scratch_shapes=[
            pltpu.VMEM((BULK, 3 * ocean_x, LANES), F32),
            pltpu.VMEM((2, *own.shape), F32),
            pltpu.VMEM((2, ocean_x, LANES), F32),
        ],
        compiler_params=PARAMS,
        cost_estimate=CHEAP,
        name="remap_lat",
    )(own, from_odd, from_even, cell, offset, weight, after)


def remap_kernel(mine, *refs):
    if mine:
        own, cell, offset, weight, state, given, forcing, out, table, sem = refs
        left = right = None
        last_col = out.shape[1] - 1
        copies = [
            pltpu.make_async_copy(state.at[side], out.at[:, col, 0, :], sem.at[side])
            for side, col in ((0, 0), (1, last_col))
        ]
        for c in copies:
            c.start()
    else:
        from_odd, from_even, cell, offset, weight, begun, forcing, table, near = refs
        left, right = bands(from_odd, from_even, near)
        own = None
    taps, ocean_x, ocean_y = cell.shape
    ratio = table.shape[1] // ocean_x
    width = ocean_x // ratio
    fill_table(table, left, own, right, ratio, range(BULK))
    for t in range(ocean_x // 8):
        used = []
        for o in range(OFFSETS):
            inside = [0 <= i // ratio + o - width < width for i in range(8 * t, 8 * t + 8)]
            if any(inside) if mine else not all(inside):
                used.append(o)
        for m in range(ocean_y // LANES):
            rows, lanes = (slice(8 * t, 8 * t + 8), slice(m * LANES, (m + 1) * LANES))
            at, off, w = ([x[p, rows, lanes] for p in range(taps)] for x in (cell, offset, weight))
            acc = gathered(
                lambda o, q: table[q, 8 * t + ratio * o : 8 * t + ratio * o + 8, :],
                at, off, w, BULK,
                None if mine else [begun[q, rows, lanes] for q in range(BULK)],
                used,
            )
            for q in range(BULK):
                forcing[q, rows, lanes] = acc[q]
    if mine:
        for c in copies:
            c.wait()


def remap_own(own, cell, offset, weight, state, out4):
    _, ocean_x, ocean_y = cell.shape
    return pl.pallas_call(
        functools.partial(remap_kernel, True),
        out_shape=[jax.ShapeDtypeStruct((BULK, ocean_x, ocean_y), F32), jax.ShapeDtypeStruct(out4.shape, F32)],
        in_specs=[VMEM] * 4 + [ANY] + [HBM],
        out_specs=[VMEM, HBM],
        scratch_shapes=[pltpu.VMEM((BULK, 3 * ocean_x, LANES), F32), pltpu.SemaphoreType.DMA((2,))],
        input_output_aliases={5: 1},
        compiler_params=PARAMS,
        cost_estimate=CHEAP,
        name="remap_own",
    )(own, cell, offset, weight, state, *pinned(out4))


def remap_rest(from_odd, from_even, cell, offset, weight, begun):
    ocean_x = cell.shape[1]
    return pl.pallas_call(
        functools.partial(remap_kernel, False),
        out_shape=jax.ShapeDtypeStruct(begun.shape, F32),
        in_specs=[VMEM] * 6,
        out_specs=VMEM,
        scratch_shapes=[pltpu.VMEM((BULK, 3 * ocean_x, LANES), F32), pltpu.VMEM((2, *from_odd.shape), F32)],
        compiler_params=PARAMS,
        cost_estimate=CHEAP,
        name="remap_rest",
    )(from_odd, from_even, cell, offset, weight, begun)


def ocean_final_kernel(
    forcing, lon_odd, lon_even, lat_odd, lat_even, base_u, base_v, mask, coriolis, new_u, new_v, lines, both
):
    levels, ocean_x, ocean_y = base_u.shape
    lines[0] = lon_odd[...]
    lines[1] = lon_even[...]
    from_west, from_east = sides_of(lines, "lon")
    both[0] = lat_odd[...]
    both[1] = lat_even[...]
    from_south, from_north = sides_of(both, "lat")
    tiles = ocean_y // LANES

    def line(buffer, q):
        return jnp.concatenate([buffer[q * tiles + m : q * tiles + m + 1, :] for m in range(tiles)], axis=1)

    zero_line = jnp.zeros((1, ocean_y), F32)
    zero_end = jnp.zeros((ocean_x, 1), F32)
    grad = []
    for q in range(3):
        lon = q < 2
        lat = q > 0
        before, after, below, above = ocean_shifts(
            forcing[q],
            line(from_west, q) if lon else zero_line,
            line(from_east, q) if lon else zero_line,
            from_south[:, q - 1 : q] if lat else zero_end,
            from_north[:, q - 1 : q] if lat else zero_end,
        )
        grad.append((0.5 * (after - before), 0.5 * (above - below)))
    force_x = -(grad[0][0] + grad[1][1])
    force_y = -(grad[1][0] + grad[2][1])
    maskf = mask[...].astype(F32)
    half = 0.5 * coriolis[...]
    add_u = maskf * (half * forcing[4] + 0.5 * force_x)
    add_v = maskf * (0.5 * force_y - half * forcing[3])
    for level in range(levels):
        decay = np.float32(np.exp(np.float32(-level / 3.0)))
        new_u[level] = base_u[level] + decay * add_u
        new_v[level] = base_v[level] + decay * add_v
    row = lax.broadcasted_iota(jnp.int32, (8, LANES), 0)
    for buffer, first, at in ((from_west, 0, 0), (from_east, ocean_x - 8, 7)):
        rows = slice(first, first + 8)
        for m in range(tiles):
            lanes = slice(m * LANES, (m + 1) * LANES)
            share = jnp.where(row == at, 0.1 * maskf[rows, lanes], 0.0)
            for f, out in enumerate((new_u, new_v)):
                start = line_rows(tiles) + (f * tiles + m) * levels
                for level in range(levels):
                    line_part = buffer[start + level : start + level + 1, :]
                    out[level, rows, lanes] = out[level, rows, lanes] + share * line_part


def ocean_final(forcing, halos, base_u, base_v, mask, coriolis):
    return pl.pallas_call(
        ocean_final_kernel,
        out_shape=[jax.ShapeDtypeStruct(base_u.shape, F32)] * 2,
        in_specs=[VMEM] * 9,
        out_specs=[VMEM] * 2,
        scratch_shapes=[pltpu.VMEM((2, *halos[0].shape), F32), pltpu.VMEM((2, base_u.shape[1], LANES), F32)],
        compiler_params=PARAMS,
        cost_estimate=CHEAP,
        name="ocean_final",
    )(forcing, *halos, base_u, base_v, mask, coriolis)


def swap(odd, even, axis, wrap):
    count = lax.axis_size(axis)
    got = []
    for first, value in ((0, odd), (1, even)):
        pairs = [(i, (i + 1) % count) for i in range(first, count, 2) if wrap or i + 1 < count]
        got.append(lax.ppermute(value, axis, pairs + [(j, i) for i, j in pairs]))
    return got


def exchange(lon, lat):
    from_lat = swap(*lat, "lat", False)
    return swap(*lon, "lon", True) + from_lat


def local(
    spectrum,
    sea_mask,
    transfer,
    bulk_weight,
    remap_cell,
    remap_weight,
    ocean_u,
    ocean_v,
    ocean_mask,
    coriolis,
):
    comps, width_x, width_y = spectrum.shape
    plan = Plan(comps)
    spec2 = spectrum.reshape(comps * width_x, width_y)
    lon = pack_lon(plan, spectrum.reshape(comps, width_x, 1, width_y), sea_mask)
    lat = pack_lat(plan, spec2, sea_mask, ocean_u, ocean_v, lon[0])
    begun = exchange(lon, lat)

    coefs = columns_of(plan, bulk_weight)
    total_y = width_y * lax.axis_size("lat")
    taps_first = remap_cell.transpose(2, 0, 1)
    offset = taps_first // total_y
    cell = taps_first % width_y
    weight = remap_weight.transpose(2, 0, 1)
    line = coriolis[None, :]

    part = advect(plan, 0, spec2, coefs, sea_mask)
    middle, edge, up, down = interior(plan, 0, part, *begun[2:], transfer, coefs, sea_mask)
    sides, *lon = edges(plan, 0, edge, *begun[:2], transfer, coefs, sea_mask)
    halos = exchange(lon, merge_lat(plan, width_x, sides, up, down))

    base_u, base_v = ocean_base(plan, ocean_u, ocean_v, *begun[2:], ocean_mask, line)
    part = advect(plan, 1, middle, coefs, sides)
    out4, edge, bulk, weights = interior(plan, 1, part, *halos[2:], transfer, coefs, sea_mask)
    sides, bulk = edges(plan, 1, edge, *halos[:2], transfer, coefs, sea_mask, bulk, weights, base_u)
    near = swap(bulk, bulk, "lon", True)
    forcing, out4 = remap_own(bulk, cell, offset, weight, sides, out4)

    remapped = (bulk, *near, cell, offset, weight)
    lon = remap_lon(*remapped, ocean_u, ocean_v, forcing)
    halos = exchange(lon, remap_lat(*remapped, lon[0]))
    forcing = remap_rest(*near, cell, offset, weight, forcing)
    new_u, new_v = ocean_final(forcing, halos, base_u, base_v, ocean_mask, line)
    state = out4.reshape(spectrum.shape)
    return (state, new_u, new_v)


def solution(mesh):
    placed = (
        P(None, "lon", "lat"),
        P("lon", "lat"),
        P(),
        P(),
        P("lon", "lat", None),
        P("lon", "lat", None),
        P(None, "lon", "lat"),
        P(None, "lon", "lat"),
        P("lon", "lat"),
        P("lat"),
    )
    return jax.shard_map(
        local,
        mesh=mesh,
        in_specs=placed,
        out_specs=(P(None, "lon", "lat"), P(None, "lon", "lat"), P(None, "lon", "lat")),
        check_vma=False,
    )
```

```python
import functools

import jax
import jax.numpy as jnp
import numpy as np
from jax import lax
from jax.experimental import pallas as pl
from jax.experimental.pallas import tpu as pltpu
from jax.sharding import PartitionSpec as P

NFREQ = 36
STEP = 16
LANES = 128
BULK = 5
GROUPS = 4
OFFSETS = 17
BLOCK = 176
F32 = jnp.float32
VMEM = pl.BlockSpec(memory_space=pltpu.VMEM)
ANY = pl.BlockSpec(memory_space=pl.ANY)
HBM = pl.BlockSpec(memory_space=pltpu.HBM)
PARAMS = pltpu.CompilerParams(vmem_limit_bytes=24 << 20)
CHEAP = pl.CostEstimate(flops=1, bytes_accessed=1, transcendentals=0)


def pinned(*arrays):
    return [pltpu.with_memory_space_constraint(x, pltpu.HBM) for x in arrays]


def kept(array):
    return pltpu.with_memory_space_constraint(array, pltpu.VMEM)


def parity(axis):
    return lax.rem(lax.axis_index(axis), 2)


def sides_of(both, axis):
    return both.at[1 - parity(axis)], both.at[parity(axis)]


class Plan:
    def __init__(self, comps):
        dirs = comps // NFREQ
        k = np.arange(comps)
        theta = 2.0 * np.pi * ((k // NFREQ) + 0.5) / dirs
        speed = 1.1 ** (-(k % NFREQ).astype(np.float64))
        cx = 0.45 * speed * np.cos(theta)
        cy = 0.45 * speed * np.sin(theta)
        self.comps = comps
        self.coef = np.stack([1.0 - np.abs(cx) - np.abs(cy), np.abs(cx), np.abs(cy)], 1).astype(np.float32)
        self.flag = {"x": cx > 0, "y": cy > 0}
        self.seg = {}
        for axis, step in (("x", 8), ("y", STEP)):
            for sign in (True, False):
                self.seg[axis, sign] = self.runs(self.flag[axis] == sign, step)

    def runs(self, flag, step):
        out = []
        for n in np.flatnonzero(flag.reshape(-1, step).any(1)):
            if out and out[-1][1] == n * step:
                out[-1][1] = int(n + 1) * step
            else:
                out.append([int(n) * step, int(n + 1) * step])
        return [(a, b) for a, b in out]

    def rows(self, axis, sign):
        return sum(b - a for a, b in self.seg[axis, sign])

    def lat_rows(self, sign):
        ((a, b),) = self.seg["y", sign]
        return -(-(b - a) // (GROUPS * STEP)) * STEP

    def lat_cuts(self):
        cuts = set()
        for sign in (True, False):
            ((a, b),) = self.seg["y", sign]
            cuts |= set(range(a, b, self.lat_rows(sign))) | {b}
        return cuts

    def lat_place(self, sign, first, last, width):
        ((a, _),) = self.seg["y", sign]
        group, row = divmod(first - a, self.lat_rows(sign))
        assert row + last - first <= self.lat_rows(sign) and (group + 1) * width <= LANES
        return slice(row, row + last - first), group * width

    def lat_blocks(self, sign, first=0, last=None):
        ((a, b),) = self.seg["y", sign]
        a, b = (max(a, first), b if last is None else min(b, last))
        return split(a, b, self.lat_cuts()) if a < b else []

    def shift(self, axis, sign, first):
        used = np.flatnonzero(self.flag[axis][first : first + STEP] == sign) + first
        if not len(used):
            return None
        base = 0
        for a, b in self.seg[axis, sign]:
            if a <= used[0] < b:
                at = base + first - a
                assert used[-1] < b and 0 <= at <= self.rows(axis, sign) - STEP
                return base - a
            base += b - a
        raise ValueError("no segment")

    def blocks(self):
        cuts = self.lat_cuts()
        return [(a, b, *rest) for first, last, *rest in self.regions() for a, b in split(first, last, cuts)]

    def regions(self):
        out = []
        for r in range(0, self.comps, STEP):
            sign = {}
            for axis in "xy":
                part = self.flag[axis][r : r + STEP]
                sign[axis] = 1 if part.all() else (0 if part.any() else -1)
            shifts = {(axis, s): self.shift(axis, s, r) for axis in "xy" for s in (True, False)}
            if out and sign["x"] and sign["y"] and out[-1][2:] == [sign["x"], sign["y"], shifts]:
                out[-1][1] = r + STEP
            else:
                out.append([r, r + STEP, sign["x"], sign["y"], shifts])
        return out


def split(first, last, cuts=(), most=BLOCK):
    out = []
    edges = [first] + sorted(c for c in cuts if first < c < last) + [last]
    for start, stop in zip(edges[:-1], edges[1:]):
        chunks = (stop - start) // STEP
        count = -(-chunks * STEP // most)
        at = [start + chunks * n // count * STEP for n in range(count + 1)]
        out += list(zip(at[:-1], at[1:]))
    return out


def lanes_of(rows):
    return lax.broadcasted_iota(jnp.int32, (rows, LANES), 1)


def picked(flag, first):
    row = lax.broadcasted_iota(jnp.int32, (STEP, LANES), 0)
    part = flag[first : first + STEP]
    out, n = (None, 0)
    while n < STEP:
        if not part[n]:
            n += 1
            continue
        m = n
        while m < STEP and part[m]:
            m += 1
        here = (row >= n) & (row < m)
        out = here if out is None else out | here
        n = m
    return out


def upwind(plan, axis, sign, first, from_plus, from_minus):
    if sign > 0:
        return from_plus()
    if sign < 0:
        return from_minus()
    plus, minus = (from_plus(), from_minus())
    where = picked(plan.flag[axis], first)
    zero = jnp.zeros((STEP, LANES), F32)
    if plus is None and minus is None:
        return None
    return jnp.where(where, zero if plus is None else plus, zero if minus is None else minus)


def columns_kernel(coef, bulk_weight, columns, rows):
    rows[...] = jnp.zeros_like(rows)
    rows[3 : 3 + BULK, : bulk_weight.shape[1]] = bulk_weight[...]
    for at in range(0, rows.shape[1], LANES):
        count = min(LANES, columns.shape[0] - at)
        turned = rows[:, at : at + LANES].T
        columns[at : at + count, :] = coef[at : at + count, :] + turned[:count, :]


def columns_of(plan, bulk_weight):
    comps = plan.comps
    coef = np.zeros((comps, 3 + BULK), np.float32)
    coef[:, :3] = plan.coef
    return pl.pallas_call(
        columns_kernel,
        out_shape=jax.ShapeDtypeStruct(coef.shape, F32),
        in_specs=[VMEM] * 2,
        out_specs=VMEM,
        scratch_shapes=[pltpu.VMEM((3 + BULK, -(-comps // LANES) * LANES), F32)],
        compiler_params=PARAMS,
        cost_estimate=CHEAP,
        name="columns",
    )(jnp.asarray(coef), bulk_weight)


def pack_lon_kernel(plan, spec, mask, odd, even, maskv, both, sem):
    last_col = spec.shape[1] - 1
    west, east = sides_of(both, "lon")
    copies = [pltpu.make_async_copy(mask, maskv, sem.at[0])]
    for out, sign, col in ((east, True, last_col), (west, False, 0)):
        at = 0
        for a, b in plan.seg["x", sign]:
            copies.append(
                pltpu.make_async_copy(
                    spec.at[pl.ds(a, b - a), col, 0, :], out.at[pl.ds(at, b - a), :], sem.at[len(copies)]
                )
            )
            at += b - a
    for c in copies:
        c.start()
    for c in copies:
        c.wait()
    masks = [maskv[col : col + 1, :].astype(F32) for col in (last_col, 0)]
    lower = jnp.full((1, LANES), parity("lon"), jnp.int32) == 0
    odd[...] = both[0] * jnp.where(lower, masks[0], masks[1])
    even[...] = both[1] * jnp.where(lower, masks[1], masks[0])


def pack_lon(plan, spec4, mask):
    segments = sum(len(plan.seg["x", s]) for s in (True, False))
    shape = (plan.rows("x", True), LANES)
    assert plan.rows("x", True) == plan.rows("x", False)
    return pl.pallas_call(
        functools.partial(pack_lon_kernel, plan),
        out_shape=[jax.ShapeDtypeStruct(shape, F32)] * 2,
        in_specs=[HBM] * 2,
        out_specs=[VMEM, VMEM],
        scratch_shapes=[
            pltpu.VMEM(mask.shape, mask.dtype),
            pltpu.VMEM((2, *shape), F32),
            pltpu.SemaphoreType.DMA((segments + 1,)),
        ],
        compiler_params=PARAMS,
        cost_estimate=CHEAP,
        name="pack_lon",
    )(*pinned(spec4, mask))


def to_lane(acc, column, source, lane, lanes):
    return jnp.where(lanes == lane, pltpu.roll(column, (lane - source) % LANES, 1), acc)


def pack_lat_kernel(plan, spec, mask, u_hbm, v_hbm, after, odd, even, both, u, v, sem):
    del after
    fields = [pltpu.make_async_copy(x, y, sem.at[n]) for n, (x, y) in enumerate(((u_hbm, u), (v_hbm, v)))]
    for c in fields:
        c.start()
    south, north = sides_of(both, "lat")
    width_x = mask.shape[0]
    levels, ocean_x, ocean_y = u.shape
    last = ocean_y - LANES
    maskf = mask[...].astype(F32)
    for out, source, sign in ((north, LANES - 1, True), (south, 0, False)):
        for a, b in plan.lat_blocks(sign):
            rows, lane = plan.lat_place(sign, a, b, width_x)
            acc = out[rows, :] if lane else jnp.zeros((b - a, LANES), F32)
            for i in range(width_x):
                x = spec[pl.ds(a * width_x + i, b - a, stride=width_x), :] * maskf[i : i + 1, :]
                acc = to_lane(acc, x, source, lane + i, lanes_of(b - a))
            out[rows, :] = acc
    for c in fields:
        c.wait()
    for out, source, sign, m in ((north, LANES - 1, True, last), (south, 0, False, 0)):
        at = plan.lat_rows(sign)
        acc = jnp.zeros((ocean_x, LANES), F32)
        for f in range(2 * levels):
            field = (u, v)[f // levels]
            acc = to_lane(acc, field[f % levels, :, m : m + LANES], source, f, lanes_of(ocean_x))
        out[at : at + ocean_x, :] = acc
    odd[...] = both[0]
    even[...] = both[1]


def pack_lat(plan, spec2, mask, u, v, after):
    assert plan.lat_rows(True) == plan.lat_rows(False)
    shape = (plan.lat_rows(True) + u.shape[1], LANES)
    return pl.pallas_call(
        functools.partial(pack_lat_kernel, plan),
        out_shape=[jax.ShapeDtypeStruct(shape, F32)] * 2,
        in_specs=[VMEM] * 2 + [HBM] * 2 + [ANY],
        out_specs=[VMEM] * 2,
        cost_estimate=CHEAP,
        scratch_shapes=[pltpu.VMEM((2, *shape), F32)]
        + [pltpu.VMEM(x.shape, F32) for x in (u, v)]
        + [pltpu.SemaphoreType.DMA((2,))],
        compiler_params=PARAMS,
        name="pack_lat",
    )(kept(spec2), mask, *pinned(u, v), after)


def advect_kernel(plan, step, state, coefs, more, part):
    width = part.shape[0]
    if step == 0:
        maskf = more[...].astype(F32)

    def column(i, first, last):
        if step == 0:
            return state[pl.ds(first * width + i, last - first, stride=width), :] * maskf[i : i + 1, :]
        if i in (0, width - 1):
            return more[min(i, 1), first:last, :]
        return state[i - 1, first:last, :]

    for first, last, xs, ys, _ in plan.blocks():
        count = last - first
        keep, east, up = (jnp.broadcast_to(coefs[first:last, q : q + 1], (count, LANES)) for q in range(3))
        lanes = lanes_of(count)
        x = [column(i, first, last) for i in range(width)]
        for i in range(width):
            lat = upwind(
                plan, "y", ys, first,
                lambda: jnp.where(lanes == 0, 0.0, pltpu.roll(x[i], 1, 1)),
                lambda: jnp.where(lanes == LANES - 1, 0.0, pltpu.roll(x[i], LANES - 1, 1)),
            )
            lon = upwind(
                plan, "x", xs, first,
                lambda: x[i - 1] if i else None,
                lambda: x[i + 1] if i + 1 < width else None,
            )
            a = keep * x[i] + up * lat
            if lon is not None:
                a = a + east * lon
            part[i, first:last, :] = a


def advect(plan, step, state, coefs, more):
    comps, width = (plan.comps, state.shape[0] // plan.comps if step == 0 else state.shape[0] + 2)
    return pl.pallas_call(
        functools.partial(advect_kernel, plan, step),
        out_shape=jax.ShapeDtypeStruct((width, comps, LANES), F32),
        in_specs=[VMEM] * 3,
        out_specs=VMEM,
        compiler_params=PARAMS,
        cost_estimate=CHEAP,
        name="advect",
    )(kept(state), coefs, more)


def block_rows(comps):
    return max(b for b in range(STEP, 449, STEP) if comps % b == 0)


def source_blocks(transfer, moved, comps, body):
    block = block_rows(comps)

    for n in range(comps // block):
        rows = slice(n * block, (n + 1) * block)
        body(n, rows, jnp.dot(transfer[rows, :], moved[...], preferred_element_type=F32))


def add_bulk(coefs, weights, rows, state, total):
    count, columns = (rows.stop - rows.start, state.shape[0])
    if coefs is not None:
        for q in range(BULK):
            weights[q, rows, :] = jnp.broadcast_to(coefs[rows, 3 + q : 4 + q], (count, LANES))
    acc = [[total[q, i] for i in range(columns)] for q in range(BULK)]
    for first in range(rows.start, rows.stop, 8):
        here = slice(first, first + 8)
        s = [state[i, here, :] for i in range(columns)]
        for q in range(BULK):
            w = weights[q, here, :]
            for i in range(columns):
                acc[q][i] = acc[q][i] + w * s[i]
    for q in range(BULK):
        for i in range(columns):
            total[q, i] = acc[q][i]


def interior_kernel(plan, step, *refs):
    part, from_odd, from_even, transfer, coefs, mask = refs[:6]
    if step == 0:
        inner, edge, up, down = refs[6:10]
        full, moved, both = refs[10:]
    else:
        out, edge, bulk, weights = refs[6:10]
        inner, full, moved, both, total, sem = refs[10:]
        total[...] = jnp.zeros_like(total)
    width = part.shape[0]
    maskf = mask[...].astype(F32)
    both[0] = from_odd[: both.shape[1], :]
    both[1] = from_even[: both.shape[1], :]
    south, north = sides_of(both, "lat")
    for first, last, _, ys, shifts in plan.blocks():
        rows, count = (slice(first, last), last - first)
        lanes = lanes_of(count)
        speed = jnp.broadcast_to(coefs[rows, 2:3], (count, LANES))
        halos = []
        for sign, buffer, lane in ((True, south, 0), (False, north, LANES - 1)):
            if shifts["y", sign] is not None:
                at, base = plan.lat_place(sign, first, last, width)
                here = lanes == lane
                if ys == 0:
                    here = here & picked(plan.flag["y"] == sign, first)
                halos.append((buffer[at, :] * speed, here, lane, base))
        for i in range(width):
            a = part[i, rows, :]
            for halo, here, lane, base in halos:
                a = a + jnp.where(here, pltpu.roll(halo, (lane - base - i) % LANES, 1), 0.0)
            if i in (0, width - 1):
                edge[min(i, 1), rows, :] = a
            else:
                full[i - 1, rows, :] = a
                moved[rows, (i - 1) * LANES : i * LANES] = a.astype(jnp.bfloat16)
    copies = []

    def done(n, rows, added):
        span = pl.ds(rows.start, rows.stop - rows.start)
        for i in range(1, width - 1):
            s = maskf[i : i + 1, :] * (full[i - 1, rows, :] + 0.5 * added[:, (i - 1) * LANES : i * LANES])
            inner[i - 1, rows, :] = s
            if step:
                to = out.at[span, i, 0, :]
                copies.append(pltpu.make_async_copy(inner.at[i - 1, span, :], to, sem.at[len(copies)]))
                copies[-1].start()
        if step:
            add_bulk(coefs, weights, rows, inner, total)
            return
        for packed, source, sign in ((up, LANES - 1, True), (down, 0, False)):
            for a, b in plan.lat_blocks(sign, rows.start, rows.stop):
                at, base = plan.lat_place(sign, a, b, width)
                acc = packed[at, :] if base else jnp.zeros((b - a, LANES), F32)
                for i in range(1, width - 1):
                    acc = to_lane(acc, inner[i - 1, a:b, :], source, base + i, lanes_of(b - a))
                packed[at, :] = acc

    source_blocks(transfer, moved, plan.comps, done)
    if step:
        for q in range(BULK):
            for i in range(1, width - 1):
                bulk[q, i : i + 1, :] = total[q, i - 1].sum(0, keepdims=True)
            bulk[q, 0:1, :] = jnp.zeros((1, LANES), F32)
            bulk[q, width - 1 : width, :] = jnp.zeros((1, LANES), F32)
    for c in copies:
        c.wait()


def interior(plan, step, part, from_odd, from_even, transfer, coefs, mask):
    comps, width = (plan.comps, mask.shape[0])
    middle = (width - 2, comps, LANES)
    edge = jax.ShapeDtypeStruct((2, comps, LANES), F32)
    scratch = [
        pltpu.VMEM(middle, F32),
        pltpu.VMEM((comps, (width - 2) * LANES), jnp.bfloat16),
        pltpu.VMEM((2, plan.lat_rows(True), LANES), F32),
    ]
    if step == 0:
        outs = [pltpu.VMEM(middle, F32), edge]
        outs += [jax.ShapeDtypeStruct((plan.lat_rows(s), LANES), F32) for s in (True, False)]
    else:
        outs = [pltpu.HBM((comps, width, 1, LANES), F32), edge, jax.ShapeDtypeStruct((BULK, width, LANES), F32)]
        outs += [jax.ShapeDtypeStruct((BULK, comps, LANES), F32)]
        scratch = [pltpu.VMEM(middle, F32)] + scratch + [pltpu.VMEM((BULK, width - 2, 8, LANES), F32)]
        scratch += [pltpu.SemaphoreType.DMA(((width - 2) * comps // block_rows(comps),))]
    return pl.pallas_call(
        functools.partial(interior_kernel, plan, step),
        out_shape=outs,
        in_specs=[VMEM] * 6,
        out_specs=[HBM if step else VMEM] + [VMEM] * (len(outs) - 1),
        scratch_shapes=scratch,
        compiler_params=PARAMS,
        cost_estimate=CHEAP,
        name="interior",
    )(part, from_odd, from_even, transfer, coefs, mask)


def edges_kernel(plan, step, *refs):
    part, from_odd, from_even, transfer, coefs, mask = refs[:6]
    if step == 0:
        state, odd, even = refs[6:9]
        full, moved, both = refs[9:]
    else:
        bulk_in, weights = refs[6:8]
        state, bulk, longer, full, moved, both, total = refs[-7:]
    width = mask.shape[0]
    maskf = jnp.concatenate([mask[0:1, :], mask[width - 1 : width, :]], axis=0).astype(F32)
    both[0] = from_odd[...]
    both[1] = from_even[...]
    from_west, from_east = sides_of(both, "lon")
    for first, last, xs, ys, shifts in plan.blocks():
        rows, count = (slice(first, last), last - first)
        speed = jnp.broadcast_to(coefs[rows, 1:2], (count, LANES))
        for side, sign, buffer in ((0, True, from_west), (1, False, from_east)):
            a = part[side, rows, :]
            shift = shifts["x", sign]
            if shift is not None:
                halo = buffer[first + shift : last + shift, :]
                if xs == 0:
                    halo = jnp.where(picked(plan.flag["x"] == sign, first), halo, 0.0)
                a = a + speed * halo
            full[side, rows, :] = a
            moved[rows, side * LANES : (side + 1) * LANES] = a.astype(jnp.bfloat16)
    if step:
        total[...] = jnp.zeros_like(total)

    def done(n, rows, added):
        for side in range(2):
            s = maskf[side : side + 1, :] * (full[side, rows, :] + 0.5 * added[:, side * LANES : (side + 1) * LANES])
            state[side, rows, :] = s
        if step:
            add_bulk(None, weights, rows, state, total)

    source_blocks(transfer, moved, plan.comps, done)
    if step:
        for q in range(BULK):
            bulk[q] = bulk_in[q]
            bulk[q, 0:1, :] = total[q, 0].sum(0, keepdims=True)
            bulk[q, width - 1 : width, :] = total[q, 1].sum(0, keepdims=True)
        longer[:BULK] = bulk[...]
        longer[BULK:] = jnp.zeros((longer.shape[0] - BULK, width, LANES), F32)
        return
    for out, side, sign in ((from_east, 1, True), (from_west, 0, False)):
        at = 0
        for a, b in plan.seg["x", sign]:
            out[at : at + b - a, :] = state[side, a:b, :]
            at += b - a
    odd[...] = both[0]
    even[...] = both[1]


def merge_lat_kernel(plan, width, state, up_in, down_in, odd, even, both):
    down, up = sides_of(both, "lat")
    for out, given, source, sign in ((up, up_in, LANES - 1, True), (down, down_in, 0, False)):
        for a, b in plan.lat_blocks(sign):
            at, base = plan.lat_place(sign, a, b, width)
            acc = out[at, :] if base else given[at, :]
            for side, lane in ((0, base), (1, base + width - 1)):
                acc = to_lane(acc, state[side, a:b, :], source, lane, lanes_of(b - a))
            out[at, :] = acc
    odd[...] = both[0]
    even[...] = both[1]


def merge_lat(plan, width, state, up, down):
    return pl.pallas_call(
        functools.partial(merge_lat_kernel, plan, width),
        out_shape=[jax.ShapeDtypeStruct(x.shape, F32) for x in (up, down)],
        in_specs=[VMEM] * 3,
        out_specs=[VMEM] * 2,
        scratch_shapes=[pltpu.VMEM((2, *up.shape), F32)],
        compiler_params=PARAMS,
        cost_estimate=CHEAP,
        name="merge_lat",
    )(state, up, down)


def edges(plan, step, part, from_odd, from_even, transfer, coefs, mask, *more):
    comps, width = (plan.comps, mask.shape[0])
    outs = [jax.ShapeDtypeStruct((2, comps, LANES), F32)]
    scratch = [pltpu.VMEM((2, comps, LANES), F32), pltpu.VMEM((comps, 2 * LANES), jnp.bfloat16)]
    scratch += [pltpu.VMEM((2, plan.rows("x", True), LANES), F32)]
    if step == 0:
        outs += [jax.ShapeDtypeStruct((plan.rows("x", s), LANES), F32) for s in (True, False)]
    else:
        outs += [jax.ShapeDtypeStruct((BULK + extra, width, LANES), F32) for extra in (0, 1)]
        scratch += [pltpu.VMEM((BULK, 2, 8, LANES), F32)]
    return pl.pallas_call(
        functools.partial(edges_kernel, plan, step),
        out_shape=outs,
        in_specs=[VMEM] * min(8, 6 + len(more)) + [ANY] * max(0, len(more) - 2),
        out_specs=[VMEM] * len(outs),
        scratch_shapes=scratch,
        compiler_params=PARAMS,
        cost_estimate=CHEAP,
        name="edges",
    )(part, from_odd, from_even, transfer, coefs, mask, *more)


def ocean_shifts(q, west, east, south, north):
    rows, lanes = q.shape
    row = lax.broadcasted_iota(jnp.int32, q.shape, 0)
    lane = lax.broadcasted_iota(jnp.int32, q.shape, 1)
    before = jnp.where(row == 0, west, pltpu.roll(q, 1, 0))
    after = jnp.where(row == rows - 1, east, pltpu.roll(q, rows - 1, 0))
    below = jnp.where(lane == 0, south, pltpu.roll(q, 1, 1))
    above = jnp.where(lane == lanes - 1, north, pltpu.roll(q, lanes - 1, 1))
    return before, after, below, above


def ocean_base_kernel(plan, u, v, from_odd, from_even, mask, coriolis, after, base_u, base_v, both):
    del after
    levels, ocean_x, ocean_y = u.shape
    start = plan.lat_rows(True)
    both[0] = from_odd[start : start + ocean_x, :]
    both[1] = from_even[start : start + ocean_x, :]
    from_south, from_north = sides_of(both, "lat")
    maskf = mask[...].astype(F32)
    half = 0.5 * coriolis[...]
    for f, (field, other, out, sign) in enumerate(((u, v, base_u, 1.0), (v, u, base_v, -1.0))):
        for level in range(levels):
            q = field[level]

            lane = f * levels + level
            before, after, below, above = ocean_shifts(
                q,
                0.0,
                0.0,
                from_south[:, lane : lane + 1],
                from_north[:, lane : lane + 1],
            )
            lap = before + after + below + above - 4.0 * q
            out[level] = maskf * (q + sign * half * other[level] + 0.1 * lap)


def ocean_base(plan, u, v, from_odd, from_even, mask, coriolis, after):
    return pl.pallas_call(
        functools.partial(ocean_base_kernel, plan),
        out_shape=[jax.ShapeDtypeStruct(u.shape, F32)] * 2,
        in_specs=[VMEM] * 6 + [ANY],
        out_specs=[VMEM] * 2,
        scratch_shapes=[pltpu.VMEM((2, u.shape[1], LANES), F32)],
        cost_estimate=CHEAP,
        compiler_params=PARAMS,
        name="ocean_base",
    )(u, v, from_odd, from_even, mask, coriolis, after)


def gathered(slabs, at, off, weight, count, acc=None, offsets=range(OFFSETS)):
    acc = [0.0] * count if acc is None else acc
    for p in range(len(at)):
        for q in range(count):
            got = 0.0
            for o in offsets:
                new = jnp.take_along_axis(slabs(o, q), at[p], axis=1, mode="promise_in_bounds")
                got = jnp.where(off[p] == o, new, got)
            acc[q] = acc[q] + weight[p] * got
    return acc


def fill_table(table, left, own, right, ratio, fields):
    width = table.shape[1] // (3 * ratio)
    for q in fields:
        for b, ref in enumerate((left, own, right)):
            for r in range(ratio):
                rows = pl.ds(b * width * ratio + r, width, stride=ratio)
                table[q, rows, :] = jnp.zeros((width, LANES), F32) if ref is None else ref[q]


def bands(from_odd, from_even, near):
    near[0] = from_odd[...]
    near[1] = from_even[: near.shape[1]]
    return sides_of(near, "lon")


def line_rows(tiles):
    return 8 * pl.cdiv(2 * tiles, 8)


def remap_lon_kernel(own, from_odd, from_even, cell, offset, weight, u, v, *refs):
    odd, even, rows, near, both = refs[-5:]
    taps, ocean_x, ocean_y = cell.shape
    width, levels = (own.shape[1], u.shape[0])
    tiles = ocean_y // LANES
    last_row = ocean_x - 8
    left, right = bands(from_odd, from_even, near)
    west, east = sides_of(both, "lon")
    for b, ref in enumerate((left, own, right)):
        rows[:, b * width : (b + 1) * width, :] = ref[0:2]
    first_half = lax.broadcasted_iota(jnp.int32, (8, LANES), 0) < 4
    for m in range(tiles):
        lanes = slice(m * LANES, (m + 1) * LANES)
        at, off, w = (
            [jnp.where(first_half, x[p, 0:8, lanes], x[p, last_row : last_row + 8, lanes]) for p in range(taps)]
            for x in (cell, offset, weight)
        )
        acc = gathered(lambda o, q: rows[q, o : o + 8, :], at, off, w, 2)
        for q in range(2):
            n = q * tiles + m
            east[n : n + 1, :] = acc[q][7:8, :]
            west[n : n + 1, :] = acc[q][0:1, :]
    for out, row in ((east, ocean_x - 1), (west, 0)):
        at = line_rows(tiles)
        for field in (u, v):
            for m in range(tiles):
                out[at : at + levels, :] = field[:, row, m * LANES : (m + 1) * LANES]
                at += levels
    odd[...] = both[0]
    even[: both.shape[1], :] = both[1]
    even[both.shape[1] :, :] = jnp.zeros((even.shape[0] - both.shape[1], LANES), F32)


def remap_lat_kernel(own, from_odd, from_even, cell, offset, weight, after, odd, even, table, near, both):
    del after
    left, right = bands(from_odd, from_even, near)
    south, north = sides_of(both, "lat")
    taps, ocean_x, ocean_y = cell.shape
    ratio = ocean_x // own.shape[1]
    last_lane = ocean_y - LANES
    fill_table(table, left, own, right, ratio, range(1, 3))
    lanes = lanes_of(8)
    for t in range(ocean_x // 8):
        here = slice(8 * t, 8 * t + 8)
        at, off, w = (
            [jnp.where(lanes < LANES // 2, x[p, here, 0:LANES], x[p, here, last_lane:]) for p in range(taps)]
            for x in (cell, offset, weight)
        )
        acc = gathered(lambda o, q: table[1 + q, 8 * t + ratio * o : 8 * t + ratio * o + 8, :], at, off, w, 2)
        for out, source in ((north, LANES - 1), (south, 0)):
            packed = jnp.zeros((8, LANES), F32)
            for q in range(2):
                packed = to_lane(packed, acc[q], source, q, lanes)
            out[here, :] = packed
    odd[...] = both[0]
    even[...] = both[1]


def remap_lon(own, from_odd, from_even, cell, offset, weight, u, v, *after):
    _, ocean_x, ocean_y = cell.shape
    width, tiles = (own.shape[1], ocean_y // LANES)
    assert width == 8 and ocean_x % width == 0
    shape = (line_rows(tiles) + 2 * u.shape[0] * tiles, LANES)
    return pl.pallas_call(
        remap_lon_kernel,
        out_shape=[jax.ShapeDtypeStruct((shape[0] + extra, LANES), F32) for extra in (0, 8)],
        in_specs=[VMEM] * 8 + [ANY] * len(after),
        out_specs=[VMEM] * 2,
        scratch_shapes=[
            pltpu.VMEM((2, 3 * width, LANES), F32),
            pltpu.VMEM((2, *own.shape), F32),
            pltpu.VMEM((2, *shape), F32),
        ],
        compiler_params=PARAMS,
        cost_estimate=CHEAP,
        name="remap_lon",
    )(own, from_odd, from_even, cell, offset, weight, u, v, *after)


def remap_lat(own, from_odd, from_even, cell, offset, weight, after):
    ocean_x = cell.shape[1]
    end = jax.ShapeDtypeStruct((ocean_x, LANES), F32)
    return pl.pallas_call(
        remap_lat_kernel,
        out_shape=[end, end],
        in_specs=[VMEM] * 6 + [ANY],
        out_specs=[VMEM] * 2,
        scratch_shapes=[
            pltpu.VMEM((BULK, 3 * ocean_x, LANES), F32),
            pltpu.VMEM((2, *own.shape), F32),
            pltpu.VMEM((2, ocean_x, LANES), F32),
        ],
        compiler_params=PARAMS,
        cost_estimate=CHEAP,
        name="remap_lat",
    )(own, from_odd, from_even, cell, offset, weight, after)


def remap_kernel(mine, *refs):
    if mine:
        own, cell, offset, weight, state, given, forcing, out, table, sem = refs
        left = right = None
        last_col = out.shape[1] - 1
        copies = [
            pltpu.make_async_copy(state.at[side], out.at[:, col, 0, :], sem.at[side])
            for side, col in ((0, 0), (1, last_col))
        ]
        for c in copies:
            c.start()
    else:
        from_odd, from_even, cell, offset, weight, begun, forcing, table, near = refs
        left, right = bands(from_odd, from_even, near)
        own = None
    taps, ocean_x, ocean_y = cell.shape
    ratio = table.shape[1] // ocean_x
    width = ocean_x // ratio
    fill_table(table, left, own, right, ratio, range(BULK))
    for t in range(ocean_x // 8):
        used = []
        for o in range(OFFSETS):
            inside = [0 <= i // ratio + o - width < width for i in range(8 * t, 8 * t + 8)]
            if any(inside) if mine else not all(inside):
                used.append(o)
        for m in range(ocean_y // LANES):
            rows, lanes = (slice(8 * t, 8 * t + 8), slice(m * LANES, (m + 1) * LANES))
            at, off, w = ([x[p, rows, lanes] for p in range(taps)] for x in (cell, offset, weight))
            acc = gathered(
                lambda o, q: table[q, 8 * t + ratio * o : 8 * t + ratio * o + 8, :],
                at, off, w, BULK,
                None if mine else [begun[q, rows, lanes] for q in range(BULK)],
                used,
            )
            for q in range(BULK):
                forcing[q, rows, lanes] = acc[q]
    if mine:
        for c in copies:
            c.wait()


def remap_own(own, cell, offset, weight, state, out4):
    _, ocean_x, ocean_y = cell.shape
    return pl.pallas_call(
        functools.partial(remap_kernel, True),
        out_shape=[jax.ShapeDtypeStruct((BULK, ocean_x, ocean_y), F32), jax.ShapeDtypeStruct(out4.shape, F32)],
        in_specs=[VMEM] * 4 + [ANY] + [HBM],
        out_specs=[VMEM, HBM],
        scratch_shapes=[pltpu.VMEM((BULK, 3 * ocean_x, LANES), F32), pltpu.SemaphoreType.DMA((2,))],
        input_output_aliases={5: 1},
        compiler_params=PARAMS,
        cost_estimate=CHEAP,
        name="remap_own",
    )(own, cell, offset, weight, state, *pinned(out4))


def remap_rest(from_odd, from_even, cell, offset, weight, begun):
    ocean_x = cell.shape[1]
    return pl.pallas_call(
        functools.partial(remap_kernel, False),
        out_shape=jax.ShapeDtypeStruct(begun.shape, F32),
        in_specs=[VMEM] * 6,
        out_specs=VMEM,
        scratch_shapes=[pltpu.VMEM((BULK, 3 * ocean_x, LANES), F32), pltpu.VMEM((2, *from_odd.shape), F32)],
        compiler_params=PARAMS,
        cost_estimate=CHEAP,
        name="remap_rest",
    )(from_odd, from_even, cell, offset, weight, begun)


def ocean_final_kernel(
    forcing, lon_odd, lon_even, lat_odd, lat_even, base_u, base_v, mask, coriolis, new_u, new_v, lines, both
):
    levels, ocean_x, ocean_y = base_u.shape
    lines[0] = lon_odd[...]
    lines[1] = lon_even[: lines.shape[1], :]
    from_west, from_east = sides_of(lines, "lon")
    both[0] = lat_odd[...]
    both[1] = lat_even[...]
    from_south, from_north = sides_of(both, "lat")
    tiles = ocean_y // LANES

    def line(buffer, q):
        return jnp.concatenate([buffer[q * tiles + m : q * tiles + m + 1, :] for m in range(tiles)], axis=1)

    zero_line = jnp.zeros((1, ocean_y), F32)
    zero_end = jnp.zeros((ocean_x, 1), F32)
    grad = []
    for q in range(3):
        lon = q < 2
        lat = q > 0
        before, after, below, above = ocean_shifts(
            forcing[q],
            line(from_west, q) if lon else zero_line,
            line(from_east, q) if lon else zero_line,
            from_south[:, q - 1 : q] if lat else zero_end,
            from_north[:, q - 1 : q] if lat else zero_end,
        )
        grad.append((0.5 * (after - before), 0.5 * (above - below)))
    force_x = -(grad[0][0] + grad[1][1])
    force_y = -(grad[1][0] + grad[2][1])
    maskf = mask[...].astype(F32)
    half = 0.5 * coriolis[...]
    add_u = maskf * (half * forcing[4] + 0.5 * force_x)
    add_v = maskf * (0.5 * force_y - half * forcing[3])
    for level in range(levels):
        decay = np.float32(np.exp(np.float32(-level / 3.0)))
        new_u[level] = base_u[level] + decay * add_u
        new_v[level] = base_v[level] + decay * add_v
    row = lax.broadcasted_iota(jnp.int32, (8, LANES), 0)
    for buffer, first, at in ((from_west, 0, 0), (from_east, ocean_x - 8, 7)):
        rows = slice(first, first + 8)
        for m in range(tiles):
            lanes = slice(m * LANES, (m + 1) * LANES)
            share = jnp.where(row == at, 0.1 * maskf[rows, lanes], 0.0)
            for f, out in enumerate((new_u, new_v)):
                start = line_rows(tiles) + (f * tiles + m) * levels
                for level in range(levels):
                    line_part = buffer[start + level : start + level + 1, :]
                    out[level, rows, lanes] = out[level, rows, lanes] + share * line_part


def ocean_final(forcing, halos, base_u, base_v, mask, coriolis):
    return pl.pallas_call(
        ocean_final_kernel,
        out_shape=[jax.ShapeDtypeStruct(base_u.shape, F32)] * 2,
        in_specs=[VMEM] * 9,
        out_specs=[VMEM] * 2,
        scratch_shapes=[pltpu.VMEM((2, *halos[0].shape), F32), pltpu.VMEM((2, base_u.shape[1], LANES), F32)],
        compiler_params=PARAMS,
        cost_estimate=CHEAP,
        name="ocean_final",
    )(forcing, *halos, base_u, base_v, mask, coriolis)


def swap(odd, even, axis, wrap):
    count = lax.axis_size(axis)
    got = []
    for first, value in ((0, odd), (1, even)):
        pairs = [(i, (i + 1) % count) for i in range(first, count, 2) if wrap or i + 1 < count]
        got.append(lax.ppermute(value, axis, pairs + [(j, i) for i, j in pairs]))
    return got


def exchange(lon, lat):
    from_lat = swap(*lat, "lat", False)
    return swap(*lon, "lon", True) + from_lat


def local(
    spectrum,
    sea_mask,
    transfer,
    bulk_weight,
    remap_cell,
    remap_weight,
    ocean_u,
    ocean_v,
    ocean_mask,
    coriolis,
):
    comps, width_x, width_y = spectrum.shape
    plan = Plan(comps)
    spec2 = spectrum.reshape(comps * width_x, width_y)
    lon = pack_lon(plan, spectrum.reshape(comps, width_x, 1, width_y), sea_mask)
    lat = pack_lat(plan, spec2, sea_mask, ocean_u, ocean_v, lon[0])
    begun = exchange(lon, lat)

    coefs = columns_of(plan, bulk_weight)
    total_y = width_y * lax.axis_size("lat")
    taps_first = remap_cell.transpose(2, 0, 1)
    offset = taps_first // total_y
    cell = taps_first % width_y
    weight = remap_weight.transpose(2, 0, 1)
    line = coriolis[None, :]

    part = advect(plan, 0, spec2, coefs, sea_mask)
    middle, edge, up, down = interior(plan, 0, part, *begun[2:], transfer, coefs, sea_mask)
    sides, *lon = edges(plan, 0, edge, *begun[:2], transfer, coefs, sea_mask)
    halos = exchange(lon, merge_lat(plan, width_x, sides, up, down))

    part = advect(plan, 1, middle, coefs, sides)
    out4, edge, bulk, weights = interior(plan, 1, part, *halos[2:], transfer, coefs, sea_mask)
    sides, bulk, longer = edges(plan, 1, edge, *halos[:2], transfer, coefs, sea_mask, bulk, weights)
    near = swap(bulk, longer, "lon", True)
    forcing, out4 = remap_own(bulk, cell, offset, weight, sides, out4)
    base_u, base_v = ocean_base(plan, ocean_u, ocean_v, *begun[2:], ocean_mask, line, bulk)

    remapped = (bulk, *near, cell, offset, weight)
    lon = remap_lon(*remapped, ocean_u, ocean_v, forcing, base_u)
    halos = exchange(lon, remap_lat(*remapped, lon[0]))
    forcing = remap_rest(*near, cell, offset, weight, forcing)
    new_u, new_v = ocean_final(forcing, halos, base_u, base_v, ocean_mask, line)
    state = out4.reshape(spectrum.shape)
    return (state, new_u, new_v)


def solution(mesh):
    placed = (
        P(None, "lon", "lat"),
        P("lon", "lat"),
        P(),
        P(),
        P("lon", "lat", None),
        P("lon", "lat", None),
        P(None, "lon", "lat"),
        P(None, "lon", "lat"),
        P("lon", "lat"),
        P("lat"),
    )
    return jax.shard_map(
        local,
        mesh=mesh,
        in_specs=placed,
        out_specs=(P(None, "lon", "lat"), P(None, "lon", "lat"), P(None, "lon", "lat")),
        check_vma=False,
    )
```

```python
import functools

import jax
import jax.numpy as jnp
import numpy as np
from jax import lax
from jax.experimental import pallas as pl
from jax.experimental.pallas import tpu as pltpu
from jax.sharding import PartitionSpec as P

NFREQ = 36
STEP = 16
LANES = 128
BULK = 5
GROUPS = 4
OFFSETS = 17
BLOCK = 176
F32 = jnp.float32
VMEM = pl.BlockSpec(memory_space=pltpu.VMEM)
ANY = pl.BlockSpec(memory_space=pl.ANY)
HBM = pl.BlockSpec(memory_space=pltpu.HBM)
PARAMS = pltpu.CompilerParams(vmem_limit_bytes=24 << 20)
CHEAP = pl.CostEstimate(flops=1, bytes_accessed=1, transcendentals=0)


def pinned(*arrays):
    return [pltpu.with_memory_space_constraint(x, pltpu.HBM) for x in arrays]


def kept(array):
    return pltpu.with_memory_space_constraint(array, pltpu.VMEM)


def parity(axis):
    return lax.rem(lax.axis_index(axis), 2)


def sides_of(both, axis):
    return both.at[1 - parity(axis)], both.at[parity(axis)]


class Plan:
    def __init__(self, comps):
        dirs = comps // NFREQ
        k = np.arange(comps)
        theta = 2.0 * np.pi * ((k // NFREQ) + 0.5) / dirs
        speed = 1.1 ** (-(k % NFREQ).astype(np.float64))
        cx = 0.45 * speed * np.cos(theta)
        cy = 0.45 * speed * np.sin(theta)
        self.comps = comps
        self.coef = np.stack([1.0 - np.abs(cx) - np.abs(cy), np.abs(cx), np.abs(cy)], 1).astype(np.float32)
        self.flag = {"x": cx > 0, "y": cy > 0}
        self.seg = {}
        for axis, step in (("x", 8), ("y", STEP)):
            for sign in (True, False):
                self.seg[axis, sign] = self.runs(self.flag[axis] == sign, step)

    def runs(self, flag, step):
        out = []
        for n in np.flatnonzero(flag.reshape(-1, step).any(1)):
            if out and out[-1][1] == n * step:
                out[-1][1] = int(n + 1) * step
            else:
                out.append([int(n) * step, int(n + 1) * step])
        return [(a, b) for a, b in out]

    def rows(self, axis, sign):
        return sum(b - a for a, b in self.seg[axis, sign])

    def lat_rows(self, sign):
        ((a, b),) = self.seg["y", sign]
        return -(-(b - a) // (GROUPS * STEP)) * STEP

    def lat_cuts(self):
        cuts = set()
        for sign in (True, False):
            ((a, b),) = self.seg["y", sign]
            cuts |= set(range(a, b, self.lat_rows(sign))) | {b}
        return cuts

    def lat_place(self, sign, first, last, width):
        ((a, _),) = self.seg["y", sign]
        group, row = divmod(first - a, self.lat_rows(sign))
        assert row + last - first <= self.lat_rows(sign) and (group + 1) * width <= LANES
        return slice(row, row + last - first), group * width

    def lat_blocks(self, sign, first=0, last=None):
        ((a, b),) = self.seg["y", sign]
        a, b = (max(a, first), b if last is None else min(b, last))
        return split(a, b, self.lat_cuts()) if a < b else []

    def shift(self, axis, sign, first):
        used = np.flatnonzero(self.flag[axis][first : first + STEP] == sign) + first
        if not len(used):
            return None
        base = 0
        for a, b in self.seg[axis, sign]:
            if a <= used[0] < b:
                at = base + first - a
                assert used[-1] < b and 0 <= at <= self.rows(axis, sign) - STEP
                return base - a
            base += b - a
        raise ValueError("no segment")

    def blocks(self):
        cuts = self.lat_cuts()
        return [(a, b, *rest) for first, last, *rest in self.regions() for a, b in split(first, last, cuts)]

    def regions(self):
        out = []
        for r in range(0, self.comps, STEP):
            sign = {}
            for axis in "xy":
                part = self.flag[axis][r : r + STEP]
                sign[axis] = 1 if part.all() else (0 if part.any() else -1)
            shifts = {(axis, s): self.shift(axis, s, r) for axis in "xy" for s in (True, False)}
            if out and sign["x"] and sign["y"] and out[-1][2:] == [sign["x"], sign["y"], shifts]:
                out[-1][1] = r + STEP
            else:
                out.append([r, r + STEP, sign["x"], sign["y"], shifts])
        return out


def split(first, last, cuts=(), most=BLOCK):
    out = []
    edges = [first] + sorted(c for c in cuts if first < c < last) + [last]
    for start, stop in zip(edges[:-1], edges[1:]):
        chunks = (stop - start) // STEP
        count = -(-chunks * STEP // most)
        at = [start + chunks * n // count * STEP for n in range(count + 1)]
        out += list(zip(at[:-1], at[1:]))
    return out


def lanes_of(rows):
    return lax.broadcasted_iota(jnp.int32, (rows, LANES), 1)


def picked(flag, first):
    row = lax.broadcasted_iota(jnp.int32, (STEP, LANES), 0)
    part = flag[first : first + STEP]
    out, n = (None, 0)
    while n < STEP:
        if not part[n]:
            n += 1
            continue
        m = n
        while m < STEP and part[m]:
            m += 1
        here = (row >= n) & (row < m)
        out = here if out is None else out | here
        n = m
    return out


def upwind(plan, axis, sign, first, from_plus, from_minus):
    if sign > 0:
        return from_plus()
    if sign < 0:
        return from_minus()
    plus, minus = (from_plus(), from_minus())
    where = picked(plan.flag[axis], first)
    zero = jnp.zeros((STEP, LANES), F32)
    if plus is None and minus is None:
        return None
    return jnp.where(where, zero if plus is None else plus, zero if minus is None else minus)


def columns_kernel(coef, bulk_weight, columns, rows):
    rows[...] = jnp.zeros_like(rows)
    rows[3 : 3 + BULK, : bulk_weight.shape[1]] = bulk_weight[...]
    for at in range(0, rows.shape[1], LANES):
        count = min(LANES, columns.shape[0] - at)
        turned = rows[:, at : at + LANES].T
        columns[at : at + count, :] = coef[at : at + count, :] + turned[:count, :]


def columns_of(plan, bulk_weight):
    comps = plan.comps
    coef = np.zeros((comps, 3 + BULK), np.float32)
    coef[:, :3] = plan.coef
    return pl.pallas_call(
        columns_kernel,
        out_shape=jax.ShapeDtypeStruct(coef.shape, F32),
        in_specs=[VMEM] * 2,
        out_specs=VMEM,
        scratch_shapes=[pltpu.VMEM((3 + BULK, -(-comps // LANES) * LANES), F32)],
        compiler_params=PARAMS,
        cost_estimate=CHEAP,
        name="columns",
    )(jnp.asarray(coef), bulk_weight)


def by_parity(axis, body):
    for lower in (True, False):
        pl.when(parity(axis) == (0 if lower else 1))(functools.partial(body, lower))


def pack_lon_kernel(plan, spec, mask, odd, even, maskv, sem):
    last_col = spec.shape[1] - 1
    first = pltpu.make_async_copy(mask, maskv, sem.at[0])
    first.start()

    def fetch(lower):
        copies = []
        for out, sign in ((odd, lower), (even, not lower)):
            at = 0
            for a, b in plan.seg["x", sign]:
                from_ref = spec.at[pl.ds(a, b - a), last_col if sign else 0, 0, :]
                copies.append(
                    pltpu.make_async_copy(from_ref, out.at[pl.ds(at, b - a), :], sem.at[1 + len(copies)])
                )
                at += b - a
        for c in copies:
            c.start()
        for c in copies:
            c.wait()

    by_parity("lon", fetch)
    first.wait()
    masks = [maskv[col : col + 1, :].astype(F32) for col in (last_col, 0)]
    lower = jnp.full((1, LANES), parity("lon"), jnp.int32) == 0
    odd[...] = odd[...] * jnp.where(lower, masks[0], masks[1])
    even[...] = even[...] * jnp.where(lower, masks[1], masks[0])


def pack_lon(plan, spec4, mask):
    segments = sum(len(plan.seg["x", s]) for s in (True, False))
    shape = (plan.rows("x", True), LANES)
    assert plan.rows("x", True) == plan.rows("x", False)
    return pl.pallas_call(
        functools.partial(pack_lon_kernel, plan),
        out_shape=[jax.ShapeDtypeStruct(shape, F32)] * 2,
        in_specs=[HBM] * 2,
        out_specs=[VMEM, VMEM],
        scratch_shapes=[
            pltpu.VMEM(mask.shape, mask.dtype),
            pltpu.SemaphoreType.DMA((segments + 1,)),
        ],
        compiler_params=PARAMS,
        cost_estimate=CHEAP,
        name="pack_lon",
    )(*pinned(spec4, mask))


def to_lane(acc, column, source, lane, lanes):
    return jnp.where(lanes == lane, pltpu.roll(column, (lane - source) % LANES, 1), acc)


def pack_lat_kernel(plan, spec, mask, u_hbm, v_hbm, after, odd, even, both, u, v, sem):
    del after
    fields = [pltpu.make_async_copy(x, y, sem.at[n]) for n, (x, y) in enumerate(((u_hbm, u), (v_hbm, v)))]
    for c in fields:
        c.start()
    south, north = sides_of(both, "lat")
    width_x = mask.shape[0]
    levels, ocean_x, ocean_y = u.shape
    last = ocean_y - LANES
    maskf = mask[...].astype(F32)
    for out, source, sign in ((north, LANES - 1, True), (south, 0, False)):
        for a, b in plan.lat_blocks(sign):
            rows, lane = plan.lat_place(sign, a, b, width_x)
            acc = out[rows, :] if lane else jnp.zeros((b - a, LANES), F32)
            for i in range(width_x):
                x = spec[pl.ds(a * width_x + i, b - a, stride=width_x), :] * maskf[i : i + 1, :]
                acc = to_lane(acc, x, source, lane + i, lanes_of(b - a))
            out[rows, :] = acc
    for c in fields:
        c.wait()
    for out, source, sign, m in ((north, LANES - 1, True, last), (south, 0, False, 0)):
        at = plan.lat_rows(sign)
        acc = jnp.zeros((ocean_x, LANES), F32)
        for f in range(2 * levels):
            field = (u, v)[f // levels]
            acc = to_lane(acc, field[f % levels, :, m : m + LANES], source, f, lanes_of(ocean_x))
        out[at : at + ocean_x, :] = acc
    odd[...] = both[0]
    even[...] = both[1]


def pack_lat(plan, spec2, mask, u, v, after):
    assert plan.lat_rows(True) == plan.lat_rows(False)
    shape = (plan.lat_rows(True) + u.shape[1], LANES)
    return pl.pallas_call(
        functools.partial(pack_lat_kernel, plan),
        out_shape=[jax.ShapeDtypeStruct(shape, F32)] * 2,
        in_specs=[VMEM] * 2 + [HBM] * 2 + [ANY],
        out_specs=[VMEM] * 2,
        cost_estimate=CHEAP,
        scratch_shapes=[pltpu.VMEM((2, *shape), F32)]
        + [pltpu.VMEM(x.shape, F32) for x in (u, v)]
        + [pltpu.SemaphoreType.DMA((2,))],
        compiler_params=PARAMS,
        name="pack_lat",
    )(kept(spec2), mask, *pinned(u, v), after)


def advect_kernel(plan, step, state, coefs, more, part):
    width = part.shape[0]
    if step == 0:
        maskf = more[...].astype(F32)

    def column(i, first, last):
        if step == 0:
            return state[pl.ds(first * width + i, last - first, stride=width), :] * maskf[i : i + 1, :]
        if i in (0, width - 1):
            return more[min(i, 1), first:last, :]
        return state[i - 1, first:last, :]

    for first, last, xs, ys, _ in plan.blocks():
        count = last - first
        keep, east, up = (jnp.broadcast_to(coefs[first:last, q : q + 1], (count, LANES)) for q in range(3))
        lanes = lanes_of(count)
        x = [column(i, first, last) for i in range(width)]
        for i in range(width):
            lat = upwind(
                plan, "y", ys, first,
                lambda: jnp.where(lanes == 0, 0.0, pltpu.roll(x[i], 1, 1)),
                lambda: jnp.where(lanes == LANES - 1, 0.0, pltpu.roll(x[i], LANES - 1, 1)),
            )
            lon = upwind(
                plan, "x", xs, first,
                lambda: x[i - 1] if i else None,
                lambda: x[i + 1] if i + 1 < width else None,
            )
            a = keep * x[i] + up * lat
            if lon is not None:
                a = a + east * lon
            part[i, first:last, :] = a


def advect(plan, step, state, coefs, more):
    comps, width = (plan.comps, state.shape[0] // plan.comps if step == 0 else state.shape[0] + 2)
    return pl.pallas_call(
        functools.partial(advect_kernel, plan, step),
        out_shape=jax.ShapeDtypeStruct((width, comps, LANES), F32),
        in_specs=[VMEM] * 3,
        out_specs=VMEM,
        compiler_params=PARAMS,
        cost_estimate=CHEAP,
        name="advect",
    )(kept(state), coefs, more)


def block_rows(comps):
    return max(b for b in range(STEP, 449, STEP) if comps % b == 0)


def source_blocks(transfer, moved, comps, body):
    block = block_rows(comps)

    for n in range(comps // block):
        rows = slice(n * block, (n + 1) * block)
        body(n, rows, jnp.dot(transfer[rows, :], moved[...], preferred_element_type=F32))


def add_bulk(coefs, weights, rows, state, total):
    count, columns = (rows.stop - rows.start, state.shape[0])
    if coefs is not None:
        for q in range(BULK):
            weights[q, rows, :] = jnp.broadcast_to(coefs[rows, 3 + q : 4 + q], (count, LANES))
    acc = [[total[q, i] for i in range(columns)] for q in range(BULK)]
    for first in range(rows.start, rows.stop, 8):
        here = slice(first, first + 8)
        s = [state[i, here, :] for i in range(columns)]
        for q in range(BULK):
            w = weights[q, here, :]
            for i in range(columns):
                acc[q][i] = acc[q][i] + w * s[i]
    for q in range(BULK):
        for i in range(columns):
            total[q, i] = acc[q][i]


def interior_kernel(plan, step, *refs):
    part, from_odd, from_even, transfer, coefs, mask = refs[:6]
    if step == 0:
        inner, edge, up, down = refs[6:10]
        full, moved, both = refs[10:]
    else:
        out, edge, bulk, weights = refs[6:10]
        inner, full, moved, both, total, sem = refs[10:]
        total[...] = jnp.zeros_like(total)
    width = part.shape[0]
    maskf = mask[...].astype(F32)
    both[0] = from_odd[: both.shape[1], :]
    both[1] = from_even[: both.shape[1], :]
    south, north = sides_of(both, "lat")
    for first, last, _, ys, shifts in plan.blocks():
        rows, count = (slice(first, last), last - first)
        lanes = lanes_of(count)
        speed = jnp.broadcast_to(coefs[rows, 2:3], (count, LANES))
        halos = []
        for sign, buffer, lane in ((True, south, 0), (False, north, LANES - 1)):
            if shifts["y", sign] is not None:
                at, base = plan.lat_place(sign, first, last, width)
                here = lanes == lane
                if ys == 0:
                    here = here & picked(plan.flag["y"] == sign, first)
                halos.append((buffer[at, :] * speed, here, lane, base))
        for i in range(width):
            a = part[i, rows, :]
            for halo, here, lane, base in halos:
                a = a + jnp.where(here, pltpu.roll(halo, (lane - base - i) % LANES, 1), 0.0)
            if i in (0, width - 1):
                edge[min(i, 1), rows, :] = a
            else:
                full[i - 1, rows, :] = a
                moved[rows, (i - 1) * LANES : i * LANES] = a.astype(jnp.bfloat16)
    copies = []

    def done(n, rows, added):
        span = pl.ds(rows.start, rows.stop - rows.start)
        for i in range(1, width - 1):
            s = maskf[i : i + 1, :] * (full[i - 1, rows, :] + 0.5 * added[:, (i - 1) * LANES : i * LANES])
            inner[i - 1, rows, :] = s
            if step:
                to = out.at[span, i, 0, :]
                copies.append(pltpu.make_async_copy(inner.at[i - 1, span, :], to, sem.at[len(copies)]))
                copies[-1].start()
        if step:
            add_bulk(coefs, weights, rows, inner, total)
            return
        for packed, source, sign in ((up, LANES - 1, True), (down, 0, False)):
            for a, b in plan.lat_blocks(sign, rows.start, rows.stop):
                at, base = plan.lat_place(sign, a, b, width)
                acc = packed[at, :] if base else jnp.zeros((b - a, LANES), F32)
                for i in range(1, width - 1):
                    acc = to_lane(acc, inner[i - 1, a:b, :], source, base + i, lanes_of(b - a))
                packed[at, :] = acc

    source_blocks(transfer, moved, plan.comps, done)
    if step:
        for q in range(BULK):
            for i in range(1, width - 1):
                bulk[q, i : i + 1, :] = total[q, i - 1].sum(0, keepdims=True)
            bulk[q, 0:1, :] = jnp.zeros((1, LANES), F32)
            bulk[q, width - 1 : width, :] = jnp.zeros((1, LANES), F32)
    for c in copies:
        c.wait()


def interior(plan, step, part, from_odd, from_even, transfer, coefs, mask):
    comps, width = (plan.comps, mask.shape[0])
    middle = (width - 2, comps, LANES)
    edge = jax.ShapeDtypeStruct((2, comps, LANES), F32)
    scratch = [
        pltpu.VMEM(middle, F32),
        pltpu.VMEM((comps, (width - 2) * LANES), jnp.bfloat16),
        pltpu.VMEM((2, plan.lat_rows(True), LANES), F32),
    ]
    if step == 0:
        outs = [pltpu.VMEM(middle, F32), edge]
        outs += [jax.ShapeDtypeStruct((plan.lat_rows(s), LANES), F32) for s in (True, False)]
    else:
        outs = [pltpu.HBM((comps, width, 1, LANES), F32), edge, jax.ShapeDtypeStruct((BULK, width, LANES), F32)]
        outs += [jax.ShapeDtypeStruct((BULK, comps, LANES), F32)]
        scratch = [pltpu.VMEM(middle, F32)] + scratch + [pltpu.VMEM((BULK, width - 2, 8, LANES), F32)]
        scratch += [pltpu.SemaphoreType.DMA(((width - 2) * comps // block_rows(comps),))]
    return pl.pallas_call(
        functools.partial(interior_kernel, plan, step),
        out_shape=outs,
        in_specs=[VMEM] * 6,
        out_specs=[HBM if step else VMEM] + [VMEM] * (len(outs) - 1),
        scratch_shapes=scratch,
        compiler_params=PARAMS,
        cost_estimate=CHEAP,
        name="interior",
    )(part, from_odd, from_even, transfer, coefs, mask)


def edges_kernel(plan, step, *refs):
    part, from_odd, from_even, transfer, coefs, mask = refs[:6]
    if step == 0:
        state, odd, even = refs[6:9]
        full, moved, both = refs[9:]
    else:
        bulk_in, weights = refs[6:8]
        state, bulk, longer, full, moved, both, total = refs[-7:]
    width = mask.shape[0]
    maskf = jnp.concatenate([mask[0:1, :], mask[width - 1 : width, :]], axis=0).astype(F32)
    both[0] = from_odd[...]
    both[1] = from_even[...]
    from_west, from_east = sides_of(both, "lon")
    for first, last, xs, ys, shifts in plan.blocks():
        rows, count = (slice(first, last), last - first)
        speed = jnp.broadcast_to(coefs[rows, 1:2], (count, LANES))
        for side, sign, buffer in ((0, True, from_west), (1, False, from_east)):
            a = part[side, rows, :]
            shift = shifts["x", sign]
            if shift is not None:
                halo = buffer[first + shift : last + shift, :]
                if xs == 0:
                    halo = jnp.where(picked(plan.flag["x"] == sign, first), halo, 0.0)
                a = a + speed * halo
            full[side, rows, :] = a
            moved[rows, side * LANES : (side + 1) * LANES] = a.astype(jnp.bfloat16)
    if step:
        total[...] = jnp.zeros_like(total)

    def done(n, rows, added):
        for side in range(2):
            s = maskf[side : side + 1, :] * (full[side, rows, :] + 0.5 * added[:, side * LANES : (side + 1) * LANES])
            state[side, rows, :] = s
        if step:
            add_bulk(None, weights, rows, state, total)

    source_blocks(transfer, moved, plan.comps, done)
    if step:
        for q in range(BULK):
            bulk[q] = bulk_in[q]
            bulk[q, 0:1, :] = total[q, 0].sum(0, keepdims=True)
            bulk[q, width - 1 : width, :] = total[q, 1].sum(0, keepdims=True)
        longer[:BULK] = bulk[...]
        longer[BULK:] = jnp.zeros((longer.shape[0] - BULK, width, LANES), F32)
        return

    def hand_over(lower):
        for out, sign in ((odd, lower), (even, not lower)):
            at = 0
            for a, b in plan.seg["x", sign]:
                out[at : at + b - a, :] = state[1 if sign else 0, a:b, :]
                at += b - a

    by_parity("lon", hand_over)


def merge_lat_kernel(plan, width, state, up_in, down_in, odd, even, both):
    down, up = sides_of(both, "lat")
    for out, given, source, sign in ((up, up_in, LANES - 1, True), (down, down_in, 0, False)):
        for a, b in plan.lat_blocks(sign):
            at, base = plan.lat_place(sign, a, b, width)
            acc = out[at, :] if base else given[at, :]
            for side, lane in ((0, base), (1, base + width - 1)):
                acc = to_lane(acc, state[side, a:b, :], source, lane, lanes_of(b - a))
            out[at, :] = acc
    odd[...] = both[0]
    even[...] = both[1]


def merge_lat(plan, width, state, up, down):
    return pl.pallas_call(
        functools.partial(merge_lat_kernel, plan, width),
        out_shape=[jax.ShapeDtypeStruct(x.shape, F32) for x in (up, down)],
        in_specs=[VMEM] * 3,
        out_specs=[VMEM] * 2,
        scratch_shapes=[pltpu.VMEM((2, *up.shape), F32)],
        compiler_params=PARAMS,
        cost_estimate=CHEAP,
        name="merge_lat",
    )(state, up, down)


def edges(plan, step, part, from_odd, from_even, transfer, coefs, mask, *more):
    comps, width = (plan.comps, mask.shape[0])
    outs = [jax.ShapeDtypeStruct((2, comps, LANES), F32)]
    scratch = [pltpu.VMEM((2, comps, LANES), F32), pltpu.VMEM((comps, 2 * LANES), jnp.bfloat16)]
    scratch += [pltpu.VMEM((2, plan.rows("x", True), LANES), F32)]
    if step == 0:
        outs += [jax.ShapeDtypeStruct((plan.rows("x", s), LANES), F32) for s in (True, False)]
    else:
        outs += [jax.ShapeDtypeStruct((BULK + extra, width, LANES), F32) for extra in (0, 1)]
        scratch += [pltpu.VMEM((BULK, 2, 8, LANES), F32)]
    return pl.pallas_call(
        functools.partial(edges_kernel, plan, step),
        out_shape=outs,
        in_specs=[VMEM] * min(8, 6 + len(more)) + [ANY] * max(0, len(more) - 2),
        out_specs=[VMEM] * len(outs),
        scratch_shapes=scratch,
        compiler_params=PARAMS,
        cost_estimate=CHEAP,
        name="edges",
    )(part, from_odd, from_even, transfer, coefs, mask, *more)


def ocean_shifts(q, west, east, south, north):
    rows, lanes = q.shape
    row = lax.broadcasted_iota(jnp.int32, q.shape, 0)
    lane = lax.broadcasted_iota(jnp.int32, q.shape, 1)
    before = jnp.where(row == 0, west, pltpu.roll(q, 1, 0))
    after = jnp.where(row == rows - 1, east, pltpu.roll(q, rows - 1, 0))
    below = jnp.where(lane == 0, south, pltpu.roll(q, 1, 1))
    above = jnp.where(lane == lanes - 1, north, pltpu.roll(q, lanes - 1, 1))
    return before, after, below, above


def ocean_base_kernel(plan, u, v, from_odd, from_even, mask, coriolis, after, base_u, base_v, both):
    del after
    levels, ocean_x, ocean_y = u.shape
    start = plan.lat_rows(True)
    both[0] = from_odd[start : start + ocean_x, :]
    both[1] = from_even[start : start + ocean_x, :]
    from_south, from_north = sides_of(both, "lat")
    maskf = mask[...].astype(F32)
    half = 0.5 * coriolis[...]
    for f, (field, other, out, sign) in enumerate(((u, v, base_u, 1.0), (v, u, base_v, -1.0))):
        for level in range(levels):
            q = field[level]

            lane = f * levels + level
            before, after, below, above = ocean_shifts(
                q,
                0.0,
                0.0,
                from_south[:, lane : lane + 1],
                from_north[:, lane : lane + 1],
            )
            lap = before + after + below + above - 4.0 * q
            out[level] = maskf * (q + sign * half * other[level] + 0.1 * lap)


def ocean_base(plan, u, v, from_odd, from_even, mask, coriolis, after):
    return pl.pallas_call(
        functools.partial(ocean_base_kernel, plan),
        out_shape=[jax.ShapeDtypeStruct(u.shape, F32)] * 2,
        in_specs=[VMEM] * 6 + [ANY],
        out_specs=[VMEM] * 2,
        scratch_shapes=[pltpu.VMEM((2, u.shape[1], LANES), F32)],
        cost_estimate=CHEAP,
        compiler_params=PARAMS,
        name="ocean_base",
    )(u, v, from_odd, from_even, mask, coriolis, after)


def gathered(slabs, at, off, weight, count, acc=None, offsets=range(OFFSETS)):
    acc = [0.0] * count if acc is None else acc
    for p in range(len(at)):
        for q in range(count):
            got = 0.0
            for o in offsets:
                new = jnp.take_along_axis(slabs(o, q), at[p], axis=1, mode="promise_in_bounds")
                got = jnp.where(off[p] == o, new, got)
            acc[q] = acc[q] + weight[p] * got
    return acc


def fill_table(table, left, own, right, ratio, fields):
    width = table.shape[1] // (3 * ratio)
    for q in fields:
        for b, ref in enumerate((left, own, right)):
            for r in range(ratio):
                rows = pl.ds(b * width * ratio + r, width, stride=ratio)
                table[q, rows, :] = jnp.zeros((width, LANES), F32) if ref is None else ref[q]


def bands(from_odd, from_even, near):
    near[0] = from_odd[...]
    near[1] = from_even[: near.shape[1]]
    return sides_of(near, "lon")


def line_rows(tiles):
    return 8 * pl.cdiv(2 * tiles, 8)


def remap_lon_kernel(own, from_odd, from_even, cell, offset, weight, u, v, *refs):
    odd, even, rows, near, both = refs[-5:]
    taps, ocean_x, ocean_y = cell.shape
    width, levels = (own.shape[1], u.shape[0])
    tiles = ocean_y // LANES
    last_row = ocean_x - 8
    left, right = bands(from_odd, from_even, near)
    west, east = sides_of(both, "lon")
    for b, ref in enumerate((left, own, right)):
        rows[:, b * width : (b + 1) * width, :] = ref[0:2]
    first_half = lax.broadcasted_iota(jnp.int32, (8, LANES), 0) < 4
    for m in range(tiles):
        lanes = slice(m * LANES, (m + 1) * LANES)
        at, off, w = (
            [jnp.where(first_half, x[p, 0:8, lanes], x[p, last_row : last_row + 8, lanes]) for p in range(taps)]
            for x in (cell, offset, weight)
        )
        acc = gathered(lambda o, q: rows[q, o : o + 8, :], at, off, w, 2)
        for q in range(2):
            n = q * tiles + m
            east[n : n + 1, :] = acc[q][7:8, :]
            west[n : n + 1, :] = acc[q][0:1, :]
    for out, row in ((east, ocean_x - 1), (west, 0)):
        at = line_rows(tiles)
        for field in (u, v):
            for m in range(tiles):
                out[at : at + levels, :] = field[:, row, m * LANES : (m + 1) * LANES]
                at += levels
    odd[...] = both[0]
    even[: both.shape[1], :] = both[1]
    even[both.shape[1] :, :] = jnp.zeros((even.shape[0] - both.shape[1], LANES), F32)


def remap_lat_kernel(own, from_odd, from_even, cell, offset, weight, after, odd, even, table, near, both):
    del after
    left, right = bands(from_odd, from_even, near)
    south, north = sides_of(both, "lat")
    taps, ocean_x, ocean_y = cell.shape
    ratio = ocean_x // own.shape[1]
    last_lane = ocean_y - LANES
    fill_table(table, left, own, right, ratio, range(1, 3))
    lanes = lanes_of(8)
    for t in range(ocean_x // 8):
        here = slice(8 * t, 8 * t + 8)
        at, off, w = (
            [jnp.where(lanes < LANES // 2, x[p, here, 0:LANES], x[p, here, last_lane:]) for p in range(taps)]
            for x in (cell, offset, weight)
        )
        acc = gathered(lambda o, q: table[1 + q, 8 * t + ratio * o : 8 * t + ratio * o + 8, :], at, off, w, 2)
        for out, source in ((north, LANES - 1), (south, 0)):
            packed = jnp.zeros((8, LANES), F32)
            for q in range(2):
                packed = to_lane(packed, acc[q], source, q, lanes)
            out[here, :] = packed
    odd[...] = both[0]
    even[...] = both[1]


def remap_lon(own, from_odd, from_even, cell, offset, weight, u, v, *after):
    _, ocean_x, ocean_y = cell.shape
    width, tiles = (own.shape[1], ocean_y // LANES)
    assert width == 8 and ocean_x % width == 0
    shape = (line_rows(tiles) + 2 * u.shape[0] * tiles, LANES)
    return pl.pallas_call(
        remap_lon_kernel,
        out_shape=[jax.ShapeDtypeStruct((shape[0] + extra, LANES), F32) for extra in (0, 8)],
        in_specs=[VMEM] * 8 + [ANY] * len(after),
        out_specs=[VMEM] * 2,
        scratch_shapes=[
            pltpu.VMEM((2, 3 * width, LANES), F32),
            pltpu.VMEM((2, *own.shape), F32),
            pltpu.VMEM((2, *shape), F32),
        ],
        compiler_params=PARAMS,
        cost_estimate=CHEAP,
        name="remap_lon",
    )(own, from_odd, from_even, cell, offset, weight, u, v, *after)


def remap_lat(own, from_odd, from_even, cell, offset, weight, after):
    ocean_x = cell.shape[1]
    end = jax.ShapeDtypeStruct((ocean_x, LANES), F32)
    return pl.pallas_call(
        remap_lat_kernel,
        out_shape=[end, end],
        in_specs=[VMEM] * 6 + [ANY],
        out_specs=[VMEM] * 2,
        scratch_shapes=[
            pltpu.VMEM((BULK, 3 * ocean_x, LANES), F32),
            pltpu.VMEM((2, *own.shape), F32),
            pltpu.VMEM((2, ocean_x, LANES), F32),
        ],
        compiler_params=PARAMS,
        cost_estimate=CHEAP,
        name="remap_lat",
    )(own, from_odd, from_even, cell, offset, weight, after)


def remap_kernel(mine, *refs):
    if mine:
        own, cell, offset, weight, state, given, forcing, out, table, sem = refs
        left = right = None
        last_col = out.shape[1] - 1
        copies = [
            pltpu.make_async_copy(state.at[side], out.at[:, col, 0, :], sem.at[side])
            for side, col in ((0, 0), (1, last_col))
        ]
        for c in copies:
            c.start()
    else:
        from_odd, from_even, cell, offset, weight, begun, forcing, table, near = refs
        left, right = bands(from_odd, from_even, near)
        own = None
    taps, ocean_x, ocean_y = cell.shape
    ratio = table.shape[1] // ocean_x
    width = ocean_x // ratio
    fill_table(table, left, own, right, ratio, range(BULK))
    for t in range(ocean_x // 8):
        used = []
        for o in range(OFFSETS):
            inside = [0 <= i // ratio + o - width < width for i in range(8 * t, 8 * t + 8)]
            if any(inside) if mine else not all(inside):
                used.append(o)
        for m in range(ocean_y // LANES):
            rows, lanes = (slice(8 * t, 8 * t + 8), slice(m * LANES, (m + 1) * LANES))
            at, off, w = ([x[p, rows, lanes] for p in range(taps)] for x in (cell, offset, weight))
            acc = gathered(
                lambda o, q: table[q, 8 * t + ratio * o : 8 * t + ratio * o + 8, :],
                at, off, w, BULK,
                None if mine else [begun[q, rows, lanes] for q in range(BULK)],
                used,
            )
            for q in range(BULK):
                forcing[q, rows, lanes] = acc[q]
    if mine:
        for c in copies:
            c.wait()


def remap_own(own, cell, offset, weight, state, out4):
    _, ocean_x, ocean_y = cell.shape
    return pl.pallas_call(
        functools.partial(remap_kernel, True),
        out_shape=[jax.ShapeDtypeStruct((BULK, ocean_x, ocean_y), F32), jax.ShapeDtypeStruct(out4.shape, F32)],
        in_specs=[VMEM] * 4 + [ANY] + [HBM],
        out_specs=[VMEM, HBM],
        scratch_shapes=[pltpu.VMEM((BULK, 3 * ocean_x, LANES), F32), pltpu.SemaphoreType.DMA((2,))],
        input_output_aliases={5: 1},
        compiler_params=PARAMS,
        cost_estimate=CHEAP,
        name="remap_own",
    )(own, cell, offset, weight, state, *pinned(out4))


def remap_rest(from_odd, from_even, cell, offset, weight, begun):
    ocean_x = cell.shape[1]
    return pl.pallas_call(
        functools.partial(remap_kernel, False),
        out_shape=jax.ShapeDtypeStruct(begun.shape, F32),
        in_specs=[VMEM] * 6,
        out_specs=VMEM,
        scratch_shapes=[pltpu.VMEM((BULK, 3 * ocean_x, LANES), F32), pltpu.VMEM((2, *from_odd.shape), F32)],
        compiler_params=PARAMS,
        cost_estimate=CHEAP,
        name="remap_rest",
    )(from_odd, from_even, cell, offset, weight, begun)


def ocean_final_kernel(
    forcing, lon_odd, lon_even, lat_odd, lat_even, base_u, base_v, mask, coriolis, new_u, new_v, lines, both
):
    levels, ocean_x, ocean_y = base_u.shape
    lines[0] = lon_odd[...]
    lines[1] = lon_even[: lines.shape[1], :]
    from_west, from_east = sides_of(lines, "lon")
    both[0] = lat_odd[...]
    both[1] = lat_even[...]
    from_south, from_north = sides_of(both, "lat")
    tiles = ocean_y // LANES

    def line(buffer, q):
        return jnp.concatenate([buffer[q * tiles + m : q * tiles + m + 1, :] for m in range(tiles)], axis=1)

    zero_line = jnp.zeros((1, ocean_y), F32)
    zero_end = jnp.zeros((ocean_x, 1), F32)
    grad = []
    for q in range(3):
        lon = q < 2
        lat = q > 0
        before, after, below, above = ocean_shifts(
            forcing[q],
            line(from_west, q) if lon else zero_line,
            line(from_east, q) if lon else zero_line,
            from_south[:, q - 1 : q] if lat else zero_end,
            from_north[:, q - 1 : q] if lat else zero_end,
        )
        grad.append((0.5 * (after - before), 0.5 * (above - below)))
    force_x = -(grad[0][0] + grad[1][1])
    force_y = -(grad[1][0] + grad[2][1])
    maskf = mask[...].astype(F32)
    half = 0.5 * coriolis[...]
    add_u = maskf * (half * forcing[4] + 0.5 * force_x)
    add_v = maskf * (0.5 * force_y - half * forcing[3])
    for level in range(levels):
        decay = np.float32(np.exp(np.float32(-level / 3.0)))
        new_u[level] = base_u[level] + decay * add_u
        new_v[level] = base_v[level] + decay * add_v
    row = lax.broadcasted_iota(jnp.int32, (8, LANES), 0)
    for buffer, first, at in ((from_west, 0, 0), (from_east, ocean_x - 8, 7)):
        rows = slice(first, first + 8)
        for m in range(tiles):
            lanes = slice(m * LANES, (m + 1) * LANES)
            share = jnp.where(row == at, 0.1 * maskf[rows, lanes], 0.0)
            for f, out in enumerate((new_u, new_v)):
                start = line_rows(tiles) + (f * tiles + m) * levels
                for level in range(levels):
                    line_part = buffer[start + level : start + level + 1, :]
                    out[level, rows, lanes] = out[level, rows, lanes] + share * line_part


def ocean_final(forcing, halos, base_u, base_v, mask, coriolis):
    return pl.pallas_call(
        ocean_final_kernel,
        out_shape=[jax.ShapeDtypeStruct(base_u.shape, F32)] * 2,
        in_specs=[VMEM] * 9,
        out_specs=[VMEM] * 2,
        scratch_shapes=[pltpu.VMEM((2, *halos[0].shape), F32), pltpu.VMEM((2, base_u.shape[1], LANES), F32)],
        compiler_params=PARAMS,
        cost_estimate=CHEAP,
        name="ocean_final",
    )(forcing, *halos, base_u, base_v, mask, coriolis)


def swap(odd, even, axis, wrap):
    count = lax.axis_size(axis)
    got = []
    for first, value in ((0, odd), (1, even)):
        pairs = [(i, (i + 1) % count) for i in range(first, count, 2) if wrap or i + 1 < count]
        got.append(lax.ppermute(value, axis, pairs + [(j, i) for i, j in pairs]))
    return got


def exchange(lon, lat):
    from_lat = swap(*lat, "lat", False)
    return swap(*lon, "lon", True) + from_lat


def local(
    spectrum,
    sea_mask,
    transfer,
    bulk_weight,
    remap_cell,
    remap_weight,
    ocean_u,
    ocean_v,
    ocean_mask,
    coriolis,
):
    comps, width_x, width_y = spectrum.shape
    plan = Plan(comps)
    spec2 = spectrum.reshape(comps * width_x, width_y)
    lon = pack_lon(plan, spectrum.reshape(comps, width_x, 1, width_y), sea_mask)
    lat = pack_lat(plan, spec2, sea_mask, ocean_u, ocean_v, lon[0])
    begun = exchange(lon, lat)

    coefs = columns_of(plan, bulk_weight)
    total_y = width_y * lax.axis_size("lat")
    taps_first = remap_cell.transpose(2, 0, 1)
    offset = taps_first // total_y
    cell = taps_first % width_y
    weight = remap_weight.transpose(2, 0, 1)
    line = coriolis[None, :]

    part = advect(plan, 0, spec2, coefs, sea_mask)
    middle, edge, up, down = interior(plan, 0, part, *begun[2:], transfer, coefs, sea_mask)
    sides, *lon = edges(plan, 0, edge, *begun[:2], transfer, coefs, sea_mask)
    halos = exchange(lon, merge_lat(plan, width_x, sides, up, down))

    part = advect(plan, 1, middle, coefs, sides)
    out4, edge, bulk, weights = interior(plan, 1, part, *halos[2:], transfer, coefs, sea_mask)
    sides, bulk, longer = edges(plan, 1, edge, *halos[:2], transfer, coefs, sea_mask, bulk, weights)
    near = swap(bulk, longer, "lon", True)
    forcing, out4 = remap_own(bulk, cell, offset, weight, sides, out4)
    base_u, base_v = ocean_base(plan, ocean_u, ocean_v, *begun[2:], ocean_mask, line, bulk)

    remapped = (bulk, *near, cell, offset, weight)
    lon = remap_lon(*remapped, ocean_u, ocean_v, forcing, base_u)
    halos = exchange(lon, remap_lat(*remapped, lon[0]))
    forcing = remap_rest(*near, cell, offset, weight, forcing)
    new_u, new_v = ocean_final(forcing, halos, base_u, base_v, ocean_mask, line)
    state = out4.reshape(spectrum.shape)
    return (state, new_u, new_v)


def solution(mesh):
    placed = (
        P(None, "lon", "lat"),
        P("lon", "lat"),
        P(),
        P(),
        P("lon", "lat", None),
        P("lon", "lat", None),
        P(None, "lon", "lat"),
        P(None, "lon", "lat"),
        P("lon", "lat"),
        P("lat"),
    )
    return jax.shard_map(
        local,
        mesh=mesh,
        in_specs=placed,
        out_specs=(P(None, "lon", "lat"), P(None, "lon", "lat"), P(None, "lon", "lat")),
        check_vma=False,
    )
```

```python
import functools

import jax
import jax.numpy as jnp
import numpy as np
from jax import lax
from jax.experimental import pallas as pl
from jax.experimental.pallas import tpu as pltpu
from jax.sharding import PartitionSpec as P

NFREQ = 36
STEP = 16
LANES = 128
BULK = 5
GROUPS = 4
OFFSETS = 17
BLOCK = 176
F32 = jnp.float32
VMEM = pl.BlockSpec(memory_space=pltpu.VMEM)
ANY = pl.BlockSpec(memory_space=pl.ANY)
HBM = pl.BlockSpec(memory_space=pltpu.HBM)
PARAMS = pltpu.CompilerParams(vmem_limit_bytes=24 << 20)
CHEAP = pl.CostEstimate(flops=1, bytes_accessed=1, transcendentals=0)


def pinned(*arrays):
    return [pltpu.with_memory_space_constraint(x, pltpu.HBM) for x in arrays]


def kept(array):
    return pltpu.with_memory_space_constraint(array, pltpu.VMEM)


def parity(axis):
    return lax.rem(lax.axis_index(axis), 2)


def sides_of(both, axis):
    return both.at[1 - parity(axis)], both.at[parity(axis)]


class Plan:
    def __init__(self, comps):
        dirs = comps // NFREQ
        k = np.arange(comps)
        theta = 2.0 * np.pi * ((k // NFREQ) + 0.5) / dirs
        speed = 1.1 ** (-(k % NFREQ).astype(np.float64))
        cx = 0.45 * speed * np.cos(theta)
        cy = 0.45 * speed * np.sin(theta)
        self.comps = comps
        self.coef = np.stack([1.0 - np.abs(cx) - np.abs(cy), np.abs(cx), np.abs(cy)], 1).astype(np.float32)
        self.flag = {"x": cx > 0, "y": cy > 0}
        self.seg = {}
        for axis, step in (("x", 8), ("y", STEP)):
            for sign in (True, False):
                self.seg[axis, sign] = self.runs(self.flag[axis] == sign, step)

    def runs(self, flag, step):
        out = []
        for n in np.flatnonzero(flag.reshape(-1, step).any(1)):
            if out and out[-1][1] == n * step:
                out[-1][1] = int(n + 1) * step
            else:
                out.append([int(n) * step, int(n + 1) * step])
        return [(a, b) for a, b in out]

    def rows(self, axis, sign):
        return sum(b - a for a, b in self.seg[axis, sign])

    def lat_rows(self, sign):
        ((a, b),) = self.seg["y", sign]
        return -(-(b - a) // (GROUPS * STEP)) * STEP

    def lat_cuts(self):
        cuts = set()
        for sign in (True, False):
            ((a, b),) = self.seg["y", sign]
            cuts |= set(range(a, b, self.lat_rows(sign))) | {b}
        return cuts

    def lat_place(self, sign, first, last, width):
        ((a, _),) = self.seg["y", sign]
        group, row = divmod(first - a, self.lat_rows(sign))
        assert row + last - first <= self.lat_rows(sign) and (group + 1) * width <= LANES
        return slice(row, row + last - first), group * width

    def lat_blocks(self, sign, first=0, last=None):
        ((a, b),) = self.seg["y", sign]
        a, b = (max(a, first), b if last is None else min(b, last))
        return split(a, b, self.lat_cuts()) if a < b else []

    def shift(self, axis, sign, first):
        used = np.flatnonzero(self.flag[axis][first : first + STEP] == sign) + first
        if not len(used):
            return None
        base = 0
        for a, b in self.seg[axis, sign]:
            if a <= used[0] < b:
                at = base + first - a
                assert used[-1] < b and 0 <= at <= self.rows(axis, sign) - STEP
                return base - a
            base += b - a
        raise ValueError("no segment")

    def blocks(self):
        cuts = self.lat_cuts()
        return [(a, b, *rest) for first, last, *rest in self.regions() for a, b in split(first, last, cuts)]

    def regions(self):
        out = []
        for r in range(0, self.comps, STEP):
            sign = {}
            for axis in "xy":
                part = self.flag[axis][r : r + STEP]
                sign[axis] = 1 if part.all() else (0 if part.any() else -1)
            shifts = {(axis, s): self.shift(axis, s, r) for axis in "xy" for s in (True, False)}
            if out and sign["x"] and sign["y"] and out[-1][2:] == [sign["x"], sign["y"], shifts]:
                out[-1][1] = r + STEP
            else:
                out.append([r, r + STEP, sign["x"], sign["y"], shifts])
        return out


def split(first, last, cuts=(), most=BLOCK):
    out = []
    edges = [first] + sorted(c for c in cuts if first < c < last) + [last]
    for start, stop in zip(edges[:-1], edges[1:]):
        chunks = (stop - start) // STEP
        count = -(-chunks * STEP // most)
        at = [start + chunks * n // count * STEP for n in range(count + 1)]
        out += list(zip(at[:-1], at[1:]))
    return out


def lanes_of(rows):
    return lax.broadcasted_iota(jnp.int32, (rows, LANES), 1)


def picked(flag, first):
    row = lax.broadcasted_iota(jnp.int32, (STEP, LANES), 0)
    part = flag[first : first + STEP]
    out, n = (None, 0)
    while n < STEP:
        if not part[n]:
            n += 1
            continue
        m = n
        while m < STEP and part[m]:
            m += 1
        here = (row >= n) & (row < m)
        out = here if out is None else out | here
        n = m
    return out


def upwind(plan, axis, sign, first, from_plus, from_minus):
    if sign > 0:
        return from_plus()
    if sign < 0:
        return from_minus()
    plus, minus = (from_plus(), from_minus())
    where = picked(plan.flag[axis], first)
    zero = jnp.zeros((STEP, LANES), F32)
    if plus is None and minus is None:
        return None
    return jnp.where(where, zero if plus is None else plus, zero if minus is None else minus)


def columns_kernel(coef, bulk_weight, columns, rows):
    rows[...] = jnp.zeros_like(rows)
    rows[3 : 3 + BULK, : bulk_weight.shape[1]] = bulk_weight[...]
    for at in range(0, rows.shape[1], LANES):
        count = min(LANES, columns.shape[0] - at)
        turned = rows[:, at : at + LANES].T
        columns[at : at + count, :] = coef[at : at + count, :] + turned[:count, :]


def columns_of(plan, bulk_weight):
    comps = plan.comps
    coef = np.zeros((comps, 3 + BULK), np.float32)
    coef[:, :3] = plan.coef
    return pl.pallas_call(
        columns_kernel,
        out_shape=jax.ShapeDtypeStruct(coef.shape, F32),
        in_specs=[VMEM] * 2,
        out_specs=VMEM,
        scratch_shapes=[pltpu.VMEM((3 + BULK, -(-comps // LANES) * LANES), F32)],
        compiler_params=PARAMS,
        cost_estimate=CHEAP,
        name="columns",
    )(jnp.asarray(coef), bulk_weight)


def by_parity(axis, body):
    for lower in (True, False):
        pl.when(parity(axis) == (0 if lower else 1))(functools.partial(body, lower))


def pack_lon_kernel(plan, spec, mask, odd, even, maskv, sem):
    last_col = spec.shape[1] - 1
    first = pltpu.make_async_copy(mask, maskv, sem.at[0])
    first.start()

    def fetch(lower):
        copies = []
        for out, sign in ((odd, lower), (even, not lower)):
            at = 0
            for a, b in plan.seg["x", sign]:
                from_ref = spec.at[pl.ds(a, b - a), last_col if sign else 0, 0, :]
                copies.append(
                    pltpu.make_async_copy(from_ref, out.at[pl.ds(at, b - a), :], sem.at[1 + len(copies)])
                )
                at += b - a
        for c in copies:
            c.start()
        for c in copies:
            c.wait()

    by_parity("lon", fetch)
    first.wait()
    masks = [maskv[col : col + 1, :].astype(F32) for col in (last_col, 0)]
    lower = jnp.full((1, LANES), parity("lon"), jnp.int32) == 0
    odd[...] = odd[...] * jnp.where(lower, masks[0], masks[1])
    even[...] = even[...] * jnp.where(lower, masks[1], masks[0])


def pack_lon(plan, spec4, mask):
    segments = sum(len(plan.seg["x", s]) for s in (True, False))
    shape = (plan.rows("x", True), LANES)
    assert plan.rows("x", True) == plan.rows("x", False)
    return pl.pallas_call(
        functools.partial(pack_lon_kernel, plan),
        out_shape=[jax.ShapeDtypeStruct(shape, F32)] * 2,
        in_specs=[HBM] * 2,
        out_specs=[VMEM, VMEM],
        scratch_shapes=[
            pltpu.VMEM(mask.shape, mask.dtype),
            pltpu.SemaphoreType.DMA((segments + 1,)),
        ],
        compiler_params=PARAMS,
        cost_estimate=CHEAP,
        name="pack_lon",
    )(*pinned(spec4, mask))


def to_lane(acc, column, source, lane, lanes):
    return jnp.where(lanes == lane, pltpu.roll(column, (lane - source) % LANES, 1), acc)


def pack_lat_kernel(plan, spec, mask, u_hbm, v_hbm, after, odd, even, both, u, v, sem):
    del after
    fields = [pltpu.make_async_copy(x, y, sem.at[n]) for n, (x, y) in enumerate(((u_hbm, u), (v_hbm, v)))]
    for c in fields:
        c.start()
    south, north = sides_of(both, "lat")
    width_x = mask.shape[0]
    levels, ocean_x, ocean_y = u.shape
    last = ocean_y - LANES
    maskf = mask[...].astype(F32)
    for out, source, sign in ((north, LANES - 1, True), (south, 0, False)):
        for a, b in plan.lat_blocks(sign):
            rows, lane = plan.lat_place(sign, a, b, width_x)
            acc = out[rows, :] if lane else jnp.zeros((b - a, LANES), F32)
            for i in range(width_x):
                x = spec[pl.ds(a * width_x + i, b - a, stride=width_x), :] * maskf[i : i + 1, :]
                acc = to_lane(acc, x, source, lane + i, lanes_of(b - a))
            out[rows, :] = acc
    for c in fields:
        c.wait()
    for out, source, sign, m in ((north, LANES - 1, True, last), (south, 0, False, 0)):
        at = plan.lat_rows(sign)
        acc = jnp.zeros((ocean_x, LANES), F32)
        for f in range(2 * levels):
            field = (u, v)[f // levels]
            acc = to_lane(acc, field[f % levels, :, m : m + LANES], source, f, lanes_of(ocean_x))
        out[at : at + ocean_x, :] = acc
    odd[...] = both[0]
    even[...] = both[1]


def pack_lat(plan, spec2, mask, u, v, after):
    assert plan.lat_rows(True) == plan.lat_rows(False)
    shape = (plan.lat_rows(True) + u.shape[1], LANES)
    return pl.pallas_call(
        functools.partial(pack_lat_kernel, plan),
        out_shape=[jax.ShapeDtypeStruct(shape, F32)] * 2,
        in_specs=[VMEM] * 2 + [HBM] * 2 + [ANY],
        out_specs=[VMEM] * 2,
        cost_estimate=CHEAP,
        scratch_shapes=[pltpu.VMEM((2, *shape), F32)]
        + [pltpu.VMEM(x.shape, F32) for x in (u, v)]
        + [pltpu.SemaphoreType.DMA((2,))],
        compiler_params=PARAMS,
        name="pack_lat",
    )(kept(spec2), mask, *pinned(u, v), after)


def advect_kernel(plan, step, state, coefs, more, part):
    width = part.shape[0]
    if step == 0:
        maskf = more[...].astype(F32)

    def column(i, first, last):
        if step == 0:
            return state[pl.ds(first * width + i, last - first, stride=width), :] * maskf[i : i + 1, :]
        if i in (0, width - 1):
            return more[min(i, 1), first:last, :]
        return state[i - 1, first:last, :]

    for first, last, xs, ys, _ in plan.blocks():
        count = last - first
        keep, east, up = (jnp.broadcast_to(coefs[first:last, q : q + 1], (count, LANES)) for q in range(3))
        lanes = lanes_of(count)
        x = [column(i, first, last) for i in range(width)]
        for i in range(width):
            lat = upwind(
                plan, "y", ys, first,
                lambda: jnp.where(lanes == 0, 0.0, pltpu.roll(x[i], 1, 1)),
                lambda: jnp.where(lanes == LANES - 1, 0.0, pltpu.roll(x[i], LANES - 1, 1)),
            )
            lon = upwind(
                plan, "x", xs, first,
                lambda: x[i - 1] if i else None,
                lambda: x[i + 1] if i + 1 < width else None,
            )
            a = keep * x[i] + up * lat
            if lon is not None:
                a = a + east * lon
            part[i, first:last, :] = a


def advect(plan, step, state, coefs, more):
    comps, width = (plan.comps, state.shape[0] // plan.comps if step == 0 else state.shape[0] + 2)
    return pl.pallas_call(
        functools.partial(advect_kernel, plan, step),
        out_shape=jax.ShapeDtypeStruct((width, comps, LANES), F32),
        in_specs=[VMEM] * 3,
        out_specs=VMEM,
        compiler_params=PARAMS,
        cost_estimate=CHEAP,
        name="advect",
    )(kept(state), coefs, more)


def block_rows(comps):
    return max(b for b in range(STEP, 449, STEP) if comps % b == 0)


def source_blocks(transfer, moved, comps, body):
    block = comps if moved.shape[1] <= 2 * LANES else block_rows(comps)

    for n in range(comps // block):
        rows = slice(n * block, (n + 1) * block)
        body(n, rows, jnp.dot(transfer[rows, :], moved[...], preferred_element_type=F32))


def add_bulk(coefs, weights, rows, state, total):
    count, columns = (rows.stop - rows.start, state.shape[0])
    if coefs is not None:
        for q in range(BULK):
            weights[q, rows, :] = jnp.broadcast_to(coefs[rows, 3 + q : 4 + q], (count, LANES))
    acc = [[total[q, i] for i in range(columns)] for q in range(BULK)]
    for first in range(rows.start, rows.stop, 8):
        here = slice(first, first + 8)
        s = [state[i, here, :] for i in range(columns)]
        for q in range(BULK):
            w = weights[q, here, :]
            for i in range(columns):
                acc[q][i] = acc[q][i] + w * s[i]
    for q in range(BULK):
        for i in range(columns):
            total[q, i] = acc[q][i]


def interior_kernel(plan, step, *refs):
    part, from_odd, from_even, transfer, coefs, mask = refs[:6]
    if step == 0:
        inner, edge, up, down = refs[6:10]
        full, moved, both = refs[10:]
    else:
        out, edge, bulk, weights = refs[6:10]
        inner, full, moved, both, total, sem = refs[10:]
        total[...] = jnp.zeros_like(total)
    width = part.shape[0]
    maskf = mask[...].astype(F32)
    both[0] = from_odd[: both.shape[1], :]
    both[1] = from_even[: both.shape[1], :]
    south, north = sides_of(both, "lat")
    for first, last, _, ys, shifts in plan.blocks():
        rows, count = (slice(first, last), last - first)
        lanes = lanes_of(count)
        speed = jnp.broadcast_to(coefs[rows, 2:3], (count, LANES))
        halos = []
        for sign, buffer, lane in ((True, south, 0), (False, north, LANES - 1)):
            if shifts["y", sign] is not None:
                at, base = plan.lat_place(sign, first, last, width)
                here = lanes == lane
                if ys == 0:
                    here = here & picked(plan.flag["y"] == sign, first)
                halos.append((buffer[at, :] * speed, here, lane, base))
        for i in range(width):
            a = part[i, rows, :]
            for halo, here, lane, base in halos:
                a = a + jnp.where(here, pltpu.roll(halo, (lane - base - i) % LANES, 1), 0.0)
            if i in (0, width - 1):
                edge[min(i, 1), rows, :] = a
            else:
                full[i - 1, rows, :] = a
                moved[rows, (i - 1) * LANES : i * LANES] = a.astype(jnp.bfloat16)
    copies = []

    def done(n, rows, added):
        span = pl.ds(rows.start, rows.stop - rows.start)
        for i in range(1, width - 1):
            s = maskf[i : i + 1, :] * (full[i - 1, rows, :] + 0.5 * added[:, (i - 1) * LANES : i * LANES])
            inner[i - 1, rows, :] = s
            if step:
                to = out.at[span, i, 0, :]
                copies.append(pltpu.make_async_copy(inner.at[i - 1, span, :], to, sem.at[len(copies)]))
                copies[-1].start()
        if step:
            add_bulk(coefs, weights, rows, inner, total)
            return
        for packed, source, sign in ((up, LANES - 1, True), (down, 0, False)):
            for a, b in plan.lat_blocks(sign, rows.start, rows.stop):
                at, base = plan.lat_place(sign, a, b, width)
                acc = packed[at, :] if base else jnp.zeros((b - a, LANES), F32)
                for i in range(1, width - 1):
                    acc = to_lane(acc, inner[i - 1, a:b, :], source, base + i, lanes_of(b - a))
                packed[at, :] = acc

    source_blocks(transfer, moved, plan.comps, done)
    if step:
        for q in range(BULK):
            for i in range(1, width - 1):
                bulk[q, i : i + 1, :] = total[q, i - 1].sum(0, keepdims=True)
            bulk[q, 0:1, :] = jnp.zeros((1, LANES), F32)
            bulk[q, width - 1 : width, :] = jnp.zeros((1, LANES), F32)
    for c in copies:
        c.wait()


def interior(plan, step, part, from_odd, from_even, transfer, coefs, mask):
    comps, width = (plan.comps, mask.shape[0])
    middle = (width - 2, comps, LANES)
    edge = jax.ShapeDtypeStruct((2, comps, LANES), F32)
    scratch = [
        pltpu.VMEM(middle, F32),
        pltpu.VMEM((comps, (width - 2) * LANES), jnp.bfloat16),
        pltpu.VMEM((2, plan.lat_rows(True), LANES), F32),
    ]
    if step == 0:
        outs = [pltpu.VMEM(middle, F32), edge]
        outs += [jax.ShapeDtypeStruct((plan.lat_rows(s), LANES), F32) for s in (True, False)]
    else:
        outs = [pltpu.HBM((comps, width, 1, LANES), F32), edge, jax.ShapeDtypeStruct((BULK, width, LANES), F32)]
        outs += [jax.ShapeDtypeStruct((BULK, comps, LANES), F32)]
        scratch = [pltpu.VMEM(middle, F32)] + scratch + [pltpu.VMEM((BULK, width - 2, 8, LANES), F32)]
        scratch += [pltpu.SemaphoreType.DMA(((width - 2) * comps // block_rows(comps),))]
    return pl.pallas_call(
        functools.partial(interior_kernel, plan, step),
        out_shape=outs,
        in_specs=[VMEM] * 6,
        out_specs=[HBM if step else VMEM] + [VMEM] * (len(outs) - 1),
        scratch_shapes=scratch,
        compiler_params=PARAMS,
        cost_estimate=CHEAP,
        name="interior",
    )(part, from_odd, from_even, transfer, coefs, mask)


def edges_kernel(plan, step, *refs):
    part, from_odd, from_even, transfer, coefs, mask = refs[:6]
    if step == 0:
        state, odd, even = refs[6:9]
        full, moved, both = refs[9:]
    else:
        bulk_in, weights = refs[6:8]
        state, bulk, longer, full, moved, both, total = refs[-7:]
    width = mask.shape[0]
    maskf = jnp.concatenate([mask[0:1, :], mask[width - 1 : width, :]], axis=0).astype(F32)
    both[0] = from_odd[...]
    both[1] = from_even[...]
    from_west, from_east = sides_of(both, "lon")
    for first, last, xs, ys, shifts in plan.blocks():
        rows, count = (slice(first, last), last - first)
        speed = jnp.broadcast_to(coefs[rows, 1:2], (count, LANES))
        for side, sign, buffer in ((0, True, from_west), (1, False, from_east)):
            a = part[side, rows, :]
            shift = shifts["x", sign]
            if shift is not None:
                halo = buffer[first + shift : last + shift, :]
                if xs == 0:
                    halo = jnp.where(picked(plan.flag["x"] == sign, first), halo, 0.0)
                a = a + speed * halo
            full[side, rows, :] = a
            moved[rows, side * LANES : (side + 1) * LANES] = a.astype(jnp.bfloat16)
    if step:
        total[...] = jnp.zeros_like(total)

    def done(n, rows, added):
        for side in range(2):
            s = maskf[side : side + 1, :] * (full[side, rows, :] + 0.5 * added[:, side * LANES : (side + 1) * LANES])
            state[side, rows, :] = s
        if step:
            add_bulk(None, weights, rows, state, total)

    source_blocks(transfer, moved, plan.comps, done)
    if step:
        for q in range(BULK):
            bulk[q] = bulk_in[q]
            bulk[q, 0:1, :] = total[q, 0].sum(0, keepdims=True)
            bulk[q, width - 1 : width, :] = total[q, 1].sum(0, keepdims=True)
        longer[:BULK] = bulk[...]
        longer[BULK:] = jnp.zeros((longer.shape[0] - BULK, width, LANES), F32)
        return

    def hand_over(lower):
        for out, sign in ((odd, lower), (even, not lower)):
            at = 0
            for a, b in plan.seg["x", sign]:
                out[at : at + b - a, :] = state[1 if sign else 0, a:b, :]
                at += b - a

    by_parity("lon", hand_over)


def merge_lat_kernel(plan, width, state, up_in, down_in, odd, even, both):
    down, up = sides_of(both, "lat")
    for out, given, source, sign in ((up, up_in, LANES - 1, True), (down, down_in, 0, False)):
        for a, b in plan.lat_blocks(sign):
            at, base = plan.lat_place(sign, a, b, width)
            acc = out[at, :] if base else given[at, :]
            for side, lane in ((0, base), (1, base + width - 1)):
                acc = to_lane(acc, state[side, a:b, :], source, lane, lanes_of(b - a))
            out[at, :] = acc
    odd[...] = both[0]
    even[...] = both[1]


def merge_lat(plan, width, state, up, down):
    return pl.pallas_call(
        functools.partial(merge_lat_kernel, plan, width),
        out_shape=[jax.ShapeDtypeStruct(x.shape, F32) for x in (up, down)],
        in_specs=[VMEM] * 3,
        out_specs=[VMEM] * 2,
        scratch_shapes=[pltpu.VMEM((2, *up.shape), F32)],
        compiler_params=PARAMS,
        cost_estimate=CHEAP,
        name="merge_lat",
    )(state, up, down)


def edges(plan, step, part, from_odd, from_even, transfer, coefs, mask, *more):
    comps, width = (plan.comps, mask.shape[0])
    outs = [jax.ShapeDtypeStruct((2, comps, LANES), F32)]
    scratch = [pltpu.VMEM((2, comps, LANES), F32), pltpu.VMEM((comps, 2 * LANES), jnp.bfloat16)]
    scratch += [pltpu.VMEM((2, plan.rows("x", True), LANES), F32)]
    if step == 0:
        outs += [jax.ShapeDtypeStruct((plan.rows("x", s), LANES), F32) for s in (True, False)]
    else:
        outs += [jax.ShapeDtypeStruct((BULK + extra, width, LANES), F32) for extra in (0, 1)]
        scratch += [pltpu.VMEM((BULK, 2, 8, LANES), F32)]
    return pl.pallas_call(
        functools.partial(edges_kernel, plan, step),
        out_shape=outs,
        in_specs=[VMEM] * min(8, 6 + len(more)) + [ANY] * max(0, len(more) - 2),
        out_specs=[VMEM] * len(outs),
        scratch_shapes=scratch,
        compiler_params=PARAMS,
        cost_estimate=CHEAP,
        name="edges",
    )(part, from_odd, from_even, transfer, coefs, mask, *more)


def ocean_shifts(q, west, east, south, north):
    rows, lanes = q.shape
    row = lax.broadcasted_iota(jnp.int32, q.shape, 0)
    lane = lax.broadcasted_iota(jnp.int32, q.shape, 1)
    before = jnp.where(row == 0, west, pltpu.roll(q, 1, 0))
    after = jnp.where(row == rows - 1, east, pltpu.roll(q, rows - 1, 0))
    below = jnp.where(lane == 0, south, pltpu.roll(q, 1, 1))
    above = jnp.where(lane == lanes - 1, north, pltpu.roll(q, lanes - 1, 1))
    return before, after, below, above


def ocean_base_kernel(plan, u, v, from_odd, from_even, mask, coriolis, after, base_u, base_v, both):
    del after
    levels, ocean_x, ocean_y = u.shape
    start = plan.lat_rows(True)
    both[0] = from_odd[start : start + ocean_x, :]
    both[1] = from_even[start : start + ocean_x, :]
    from_south, from_north = sides_of(both, "lat")
    maskf = mask[...].astype(F32)
    half = 0.5 * coriolis[...]
    for f, (field, other, out, sign) in enumerate(((u, v, base_u, 1.0), (v, u, base_v, -1.0))):
        for level in range(levels):
            q = field[level]

            lane = f * levels + level
            before, after, below, above = ocean_shifts(
                q,
                0.0,
                0.0,
                from_south[:, lane : lane + 1],
                from_north[:, lane : lane + 1],
            )
            lap = before + after + below + above - 4.0 * q
            out[level] = maskf * (q + sign * half * other[level] + 0.1 * lap)


def ocean_base(plan, u, v, from_odd, from_even, mask, coriolis, after):
    return pl.pallas_call(
        functools.partial(ocean_base_kernel, plan),
        out_shape=[jax.ShapeDtypeStruct(u.shape, F32)] * 2,
        in_specs=[VMEM] * 6 + [ANY],
        out_specs=[VMEM] * 2,
        scratch_shapes=[pltpu.VMEM((2, u.shape[1], LANES), F32)],
        cost_estimate=CHEAP,
        compiler_params=PARAMS,
        name="ocean_base",
    )(u, v, from_odd, from_even, mask, coriolis, after)


def gathered(slabs, at, off, weight, count, acc=None, offsets=range(OFFSETS)):
    acc = [0.0] * count if acc is None else acc
    for p in range(len(at)):
        for q in range(count):
            got = 0.0
            for o in offsets:
                new = jnp.take_along_axis(slabs(o, q), at[p], axis=1, mode="promise_in_bounds")
                got = jnp.where(off[p] == o, new, got)
            acc[q] = acc[q] + weight[p] * got
    return acc


def fill_table(table, left, own, right, ratio, fields):
    width = table.shape[1] // (3 * ratio)
    for q in fields:
        for b, ref in enumerate((left, own, right)):
            for r in range(ratio):
                rows = pl.ds(b * width * ratio + r, width, stride=ratio)
                table[q, rows, :] = jnp.zeros((width, LANES), F32) if ref is None else ref[q]


def bands(from_odd, from_even, near):
    near[0] = from_odd[...]
    near[1] = from_even[: near.shape[1]]
    return sides_of(near, "lon")


def line_rows(tiles):
    return 8 * pl.cdiv(2 * tiles, 8)


def remap_lon_kernel(own, from_odd, from_even, cell, offset, weight, u, v, *refs):
    odd, even, rows, near, both = refs[-5:]
    taps, ocean_x, ocean_y = cell.shape
    width, levels = (own.shape[1], u.shape[0])
    tiles = ocean_y // LANES
    last_row = ocean_x - 8
    left, right = bands(from_odd, from_even, near)
    west, east = sides_of(both, "lon")
    for b, ref in enumerate((left, own, right)):
        rows[:, b * width : (b + 1) * width, :] = ref[0:2]
    first_half = lax.broadcasted_iota(jnp.int32, (8, LANES), 0) < 4
    for m in range(tiles):
        lanes = slice(m * LANES, (m + 1) * LANES)
        at, off, w = (
            [jnp.where(first_half, x[p, 0:8, lanes], x[p, last_row : last_row + 8, lanes]) for p in range(taps)]
            for x in (cell, offset, weight)
        )
        acc = gathered(lambda o, q: rows[q, o : o + 8, :], at, off, w, 2)
        for q in range(2):
            n = q * tiles + m
            east[n : n + 1, :] = acc[q][7:8, :]
            west[n : n + 1, :] = acc[q][0:1, :]
    for out, row in ((east, ocean_x - 1), (west, 0)):
        at = line_rows(tiles)
        for field in (u, v):
            for m in range(tiles):
                out[at : at + levels, :] = field[:, row, m * LANES : (m + 1) * LANES]
                at += levels
    odd[...] = both[0]
    even[: both.shape[1], :] = both[1]
    even[both.shape[1] :, :] = jnp.zeros((even.shape[0] - both.shape[1], LANES), F32)


def remap_lat_kernel(own, from_odd, from_even, cell, offset, weight, after, odd, even, table, near, both):
    del after
    left, right = bands(from_odd, from_even, near)
    south, north = sides_of(both, "lat")
    taps, ocean_x, ocean_y = cell.shape
    ratio = ocean_x // own.shape[1]
    last_lane = ocean_y - LANES
    fill_table(table, left, own, right, ratio, range(1, 3))
    lanes = lanes_of(8)
    for t in range(ocean_x // 8):
        here = slice(8 * t, 8 * t + 8)
        at, off, w = (
            [jnp.where(lanes < LANES // 2, x[p, here, 0:LANES], x[p, here, last_lane:]) for p in range(taps)]
            for x in (cell, offset, weight)
        )
        acc = gathered(lambda o, q: table[1 + q, 8 * t + ratio * o : 8 * t + ratio * o + 8, :], at, off, w, 2)
        for out, source in ((north, LANES - 1), (south, 0)):
            packed = jnp.zeros((8, LANES), F32)
            for q in range(2):
                packed = to_lane(packed, acc[q], source, q, lanes)
            out[here, :] = packed
    odd[...] = both[0]
    even[...] = both[1]


def remap_lon(own, from_odd, from_even, cell, offset, weight, u, v, *after):
    _, ocean_x, ocean_y = cell.shape
    width, tiles = (own.shape[1], ocean_y // LANES)
    assert width == 8 and ocean_x % width == 0
    shape = (line_rows(tiles) + 2 * u.shape[0] * tiles, LANES)
    return pl.pallas_call(
        remap_lon_kernel,
        out_shape=[jax.ShapeDtypeStruct((shape[0] + extra, LANES), F32) for extra in (0, 8)],
        in_specs=[VMEM] * 8 + [ANY] * len(after),
        out_specs=[VMEM] * 2,
        scratch_shapes=[
            pltpu.VMEM((2, 3 * width, LANES), F32),
            pltpu.VMEM((2, *own.shape), F32),
            pltpu.VMEM((2, *shape), F32),
        ],
        compiler_params=PARAMS,
        cost_estimate=CHEAP,
        name="remap_lon",
    )(own, from_odd, from_even, cell, offset, weight, u, v, *after)


def remap_lat(own, from_odd, from_even, cell, offset, weight, after):
    ocean_x = cell.shape[1]
    end = jax.ShapeDtypeStruct((ocean_x, LANES), F32)
    return pl.pallas_call(
        remap_lat_kernel,
        out_shape=[end, end],
        in_specs=[VMEM] * 6 + [ANY],
        out_specs=[VMEM] * 2,
        scratch_shapes=[
            pltpu.VMEM((BULK, 3 * ocean_x, LANES), F32),
            pltpu.VMEM((2, *own.shape), F32),
            pltpu.VMEM((2, ocean_x, LANES), F32),
        ],
        compiler_params=PARAMS,
        cost_estimate=CHEAP,
        name="remap_lat",
    )(own, from_odd, from_even, cell, offset, weight, after)


def remap_kernel(mine, *refs):
    if mine:
        own, cell, offset, weight, state, given, forcing, out, table, sem = refs
        left = right = None
        last_col = out.shape[1] - 1
        copies = [
            pltpu.make_async_copy(state.at[side], out.at[:, col, 0, :], sem.at[side])
            for side, col in ((0, 0), (1, last_col))
        ]
        for c in copies:
            c.start()
    else:
        from_odd, from_even, cell, offset, weight, begun, forcing, table, near = refs
        left, right = bands(from_odd, from_even, near)
        own = None
    taps, ocean_x, ocean_y = cell.shape
    ratio = table.shape[1] // ocean_x
    width = ocean_x // ratio
    fill_table(table, left, own, right, ratio, range(BULK))
    for t in range(ocean_x // 8):
        used = []
        for o in range(OFFSETS):
            inside = [0 <= i // ratio + o - width < width for i in range(8 * t, 8 * t + 8)]
            if any(inside) if mine else not all(inside):
                used.append(o)
        for m in range(ocean_y // LANES):
            rows, lanes = (slice(8 * t, 8 * t + 8), slice(m * LANES, (m + 1) * LANES))
            at, off, w = ([x[p, rows, lanes] for p in range(taps)] for x in (cell, offset, weight))
            acc = gathered(
                lambda o, q: table[q, 8 * t + ratio * o : 8 * t + ratio * o + 8, :],
                at, off, w, BULK,
                None if mine else [begun[q, rows, lanes] for q in range(BULK)],
                used,
            )
            for q in range(BULK):
                forcing[q, rows, lanes] = acc[q]
    if mine:
        for c in copies:
            c.wait()


def remap_own(own, cell, offset, weight, state, out4):
    _, ocean_x, ocean_y = cell.shape
    return pl.pallas_call(
        functools.partial(remap_kernel, True),
        out_shape=[jax.ShapeDtypeStruct((BULK, ocean_x, ocean_y), F32), jax.ShapeDtypeStruct(out4.shape, F32)],
        in_specs=[VMEM] * 4 + [ANY] + [HBM],
        out_specs=[VMEM, HBM],
        scratch_shapes=[pltpu.VMEM((BULK, 3 * ocean_x, LANES), F32), pltpu.SemaphoreType.DMA((2,))],
        input_output_aliases={5: 1},
        compiler_params=PARAMS,
        cost_estimate=CHEAP,
        name="remap_own",
    )(own, cell, offset, weight, state, *pinned(out4))


def remap_rest(from_odd, from_even, cell, offset, weight, begun):
    ocean_x = cell.shape[1]
    return pl.pallas_call(
        functools.partial(remap_kernel, False),
        out_shape=jax.ShapeDtypeStruct(begun.shape, F32),
        in_specs=[VMEM] * 6,
        out_specs=VMEM,
        scratch_shapes=[pltpu.VMEM((BULK, 3 * ocean_x, LANES), F32), pltpu.VMEM((2, *from_odd.shape), F32)],
        compiler_params=PARAMS,
        cost_estimate=CHEAP,
        name="remap_rest",
    )(from_odd, from_even, cell, offset, weight, begun)


def ocean_final_kernel(
    forcing, lon_odd, lon_even, lat_odd, lat_even, base_u, base_v, mask, coriolis, new_u, new_v, lines, both
):
    levels, ocean_x, ocean_y = base_u.shape
    lines[0] = lon_odd[...]
    lines[1] = lon_even[: lines.shape[1], :]
    from_west, from_east = sides_of(lines, "lon")
    both[0] = lat_odd[...]
    both[1] = lat_even[...]
    from_south, from_north = sides_of(both, "lat")
    tiles = ocean_y // LANES

    def line(buffer, q):
        return jnp.concatenate([buffer[q * tiles + m : q * tiles + m + 1, :] for m in range(tiles)], axis=1)

    zero_line = jnp.zeros((1, ocean_y), F32)
    zero_end = jnp.zeros((ocean_x, 1), F32)
    grad = []
    for q in range(3):
        lon = q < 2
        lat = q > 0
        before, after, below, above = ocean_shifts(
            forcing[q],
            line(from_west, q) if lon else zero_line,
            line(from_east, q) if lon else zero_line,
            from_south[:, q - 1 : q] if lat else zero_end,
            from_north[:, q - 1 : q] if lat else zero_end,
        )
        grad.append((0.5 * (after - before), 0.5 * (above - below)))
    force_x = -(grad[0][0] + grad[1][1])
    force_y = -(grad[1][0] + grad[2][1])
    maskf = mask[...].astype(F32)
    half = 0.5 * coriolis[...]
    add_u = maskf * (half * forcing[4] + 0.5 * force_x)
    add_v = maskf * (0.5 * force_y - half * forcing[3])
    for level in range(levels):
        decay = np.float32(np.exp(np.float32(-level / 3.0)))
        new_u[level] = base_u[level] + decay * add_u
        new_v[level] = base_v[level] + decay * add_v
    row = lax.broadcasted_iota(jnp.int32, (8, LANES), 0)
    for buffer, first, at in ((from_west, 0, 0), (from_east, ocean_x - 8, 7)):
        rows = slice(first, first + 8)
        for m in range(tiles):
            lanes = slice(m * LANES, (m + 1) * LANES)
            share = jnp.where(row == at, 0.1 * maskf[rows, lanes], 0.0)
            for f, out in enumerate((new_u, new_v)):
                start = line_rows(tiles) + (f * tiles + m) * levels
                for level in range(levels):
                    line_part = buffer[start + level : start + level + 1, :]
                    out[level, rows, lanes] = out[level, rows, lanes] + share * line_part


def ocean_final(forcing, halos, base_u, base_v, mask, coriolis):
    return pl.pallas_call(
        ocean_final_kernel,
        out_shape=[jax.ShapeDtypeStruct(base_u.shape, F32)] * 2,
        in_specs=[VMEM] * 9,
        out_specs=[VMEM] * 2,
        scratch_shapes=[pltpu.VMEM((2, *halos[0].shape), F32), pltpu.VMEM((2, base_u.shape[1], LANES), F32)],
        compiler_params=PARAMS,
        cost_estimate=CHEAP,
        name="ocean_final",
    )(forcing, *halos, base_u, base_v, mask, coriolis)


def swap(odd, even, axis, wrap):
    count = lax.axis_size(axis)
    got = []
    for first, value in ((0, odd), (1, even)):
        pairs = [(i, (i + 1) % count) for i in range(first, count, 2) if wrap or i + 1 < count]
        got.append(lax.ppermute(value, axis, pairs + [(j, i) for i, j in pairs]))
    return got


def exchange(lon, lat):
    from_lat = swap(*lat, "lat", False)
    return swap(*lon, "lon", True) + from_lat


def local(
    spectrum,
    sea_mask,
    transfer,
    bulk_weight,
    remap_cell,
    remap_weight,
    ocean_u,
    ocean_v,
    ocean_mask,
    coriolis,
):
    comps, width_x, width_y = spectrum.shape
    plan = Plan(comps)
    spec2 = spectrum.reshape(comps * width_x, width_y)
    lon = pack_lon(plan, spectrum.reshape(comps, width_x, 1, width_y), sea_mask)
    lat = pack_lat(plan, spec2, sea_mask, ocean_u, ocean_v, lon[0])
    begun = exchange(lon, lat)

    coefs = columns_of(plan, bulk_weight)
    total_y = width_y * lax.axis_size("lat")
    taps_first = remap_cell.transpose(2, 0, 1)
    offset = taps_first // total_y
    cell = taps_first % width_y
    weight = remap_weight.transpose(2, 0, 1)
    line = coriolis[None, :]

    part = advect(plan, 0, spec2, coefs, sea_mask)
    middle, edge, up, down = interior(plan, 0, part, *begun[2:], transfer, coefs, sea_mask)
    sides, *lon = edges(plan, 0, edge, *begun[:2], transfer, coefs, sea_mask)
    halos = exchange(lon, merge_lat(plan, width_x, sides, up, down))

    part = advect(plan, 1, middle, coefs, sides)
    out4, edge, bulk, weights = interior(plan, 1, part, *halos[2:], transfer, coefs, sea_mask)
    sides, bulk, longer = edges(plan, 1, edge, *halos[:2], transfer, coefs, sea_mask, bulk, weights)
    near = swap(bulk, longer, "lon", True)
    forcing, out4 = remap_own(bulk, cell, offset, weight, sides, out4)
    base_u, base_v = ocean_base(plan, ocean_u, ocean_v, *begun[2:], ocean_mask, line, bulk)

    remapped = (bulk, *near, cell, offset, weight)
    lon = remap_lon(*remapped, ocean_u, ocean_v, forcing, base_u)
    halos = exchange(lon, remap_lat(*remapped, lon[0]))
    forcing = remap_rest(*near, cell, offset, weight, forcing)
    new_u, new_v = ocean_final(forcing, halos, base_u, base_v, ocean_mask, line)
    state = out4.reshape(spectrum.shape)
    return (state, new_u, new_v)


def solution(mesh):
    placed = (
        P(None, "lon", "lat"),
        P("lon", "lat"),
        P(),
        P(),
        P("lon", "lat", None),
        P("lon", "lat", None),
        P(None, "lon", "lat"),
        P(None, "lon", "lat"),
        P("lon", "lat"),
        P("lat"),
    )
    return jax.shard_map(
        local,
        mesh=mesh,
        in_specs=placed,
        out_specs=(P(None, "lon", "lat"), P(None, "lon", "lat"), P(None, "lon", "lat")),
        check_vma=False,
    )
```
